32 devices in a mesh: seq: 8 (over z, y), batch: 4 (over x, core).
Axes of the slice: x: 2, y: 2, z: 4, core: 2. Of those that a mesh axis runs over, the one named last changes fastest.
Arguments:
- stream_in: bfloat16 [8, 1024, 512], P('batch', 'seq'), may hold values from -6 to 6
- out_grad: bfloat16 [8, 1024, 512], P('batch', 'seq'), may hold values from -6 to 6
- doc_lengths: int32 [8, 16], P('batch'), may hold values from 0 to 897, as said below
- mats: float32 [2, 4, 2048, 512], P(None, 'batch', 'seq')
- mat_momenta: float32 [2, 4, 2048, 512], P(None, 'batch', 'seq')
- mat_averages: float32 [2, 4, 2048, 512], P(None, 'batch', 'seq')
- vectors: float32 [2, 3072], replicated
- vec_momenta: float32 [2, 3072], replicated
- vec_averages: float32 [2, 3072], replicated
Outputs:
- activations: bfloat16 [8, 1024, 512], P('batch', 'seq')
- input_grad: float32 [8, 1024, 512], P('batch', 'seq')
- mat_grads: float32 [2, 4, 2048, 512], P(None, 'batch', 'seq')
- new_momenta: float32 [2, 4, 2048, 512], P(None, 'batch')
- new_mats: float32 [2, 4, 2048, 512], P(None, 'batch', 'seq')
- new_averages: float32 [2, 4, 2048, 512], P(None, 'batch', 'seq')
- vec_grads: float32 [2, 3072], replicated
- new_vec_momenta: float32 [2, 3072], replicated
- new_vectors: float32 [2, 3072], replicated
- new_vec_averages: float32 [2, 3072], replicated
The draws below stay inside these ranges and needn't reach their ends.
Inputs may be any that keep to these rules, and one draw needn't show every extreme that they name: `doc_lengths`: each row sums to 1024; in every group of 2 consecutive streams one stream holds a document of exactly 897 tokens.
All inputs are finite; a program needn't handle non-finite values.
Results may differ from the reference program's by a relative error of at most 0.0085.
The reference program's roundings to bfloat16 on the way count: a program that leaves them out, or rounds other values in their place, can miss the bound.
Values may be sent and summed in bfloat16 or wider, within the bound.
A program may use at most 192 MiB of HBM per device.

```python
import math
import jax
import jax.numpy as jnp
from jax import lax

D = 512
H = 1024
FF = 2048
LAYERS = 2
NS_STEPS = 2
DOCS = 16
SPAN = 128
STREAMS_DEV = 2
SLEN = 1024
STREAMS = 8
TOKENS = 8192
MOST = 897
ROW_BLOCKS = 4
HID_BLOCK = 256
FFN_BLOCK = 512
BLOCK_ROWS = 2048
VEC = 3072


def kind_rows(factors):
    row_sizes = [HID_BLOCK, HID_BLOCK, HID_BLOCK, HID_BLOCK, FFN_BLOCK, FFN_BLOCK]
    return jnp.concatenate([jnp.full((row_count,), factor, jnp.float32) for row_count, factor in zip(row_sizes, factors)])


def weight_scales():
    return kind_rows([D ** (-0.5), D ** (-0.5), D ** (-0.5), (H / 4.0) ** (-0.5), D ** (-0.5), FF ** (-0.5)])


def vector_law(key):
    gain_key, forget_key, input_key = jax.random.split(key, 3)
    gains = 1.0 + 0.1 * jax.random.uniform(gain_key, (LAYERS, 2 * D), jnp.float32, -1.0, 1.0)
    bias_forget = jax.random.uniform(forget_key, (LAYERS, H), jnp.float32, -1.0, 2.0)
    bias_input = -math.log(SLEN) * jax.random.uniform(input_key, (LAYERS, H), jnp.float32, 0.3, 1.6) - 1.0
    return jnp.concatenate([gains, bias_forget, bias_input], axis=1)


def draw_mats(key, part):
    key = jax.random.fold_in(key, 1)
    array_shape = (LAYERS, ROW_BLOCKS, BLOCK_ROWS, D)
    noise_draw = jax.random.normal(key, array_shape, jnp.float32)
    return noise_draw * weight_scales()[None, None, :, None]


def draw_mat_averages(key, part):
    key = jax.random.fold_in(key, 2)
    array_shape = (LAYERS, ROW_BLOCKS, BLOCK_ROWS, D)
    noise_draw = jax.random.normal(key, array_shape, jnp.float32)
    return noise_draw * weight_scales()[None, None, :, None]


def draw_mat_momenta(key, part):
    key = jax.random.fold_in(key, 3)
    array_shape = (LAYERS, ROW_BLOCKS, BLOCK_ROWS, D)
    noise_draw = jax.random.normal(key, array_shape, jnp.float32)
    top_rise = 3.0
    row_rise = 1.0 + (top_rise - 1.0) * jnp.arange(ROW_BLOCKS, dtype=jnp.float32) / max(ROW_BLOCKS - 1, 1)
    kind_scales = kind_rows([0.05, 0.05, 0.2, 0.3, 0.15, 0.3]) * math.sqrt(TOKENS)
    return noise_draw * row_rise[None, :, None, None] * kind_scales[None, None, :, None]


def draw_vectors(key, part):
    key = jax.random.fold_in(key, 4)
    return vector_law(key)


def draw_vec_averages(key, part):
    key = jax.random.fold_in(key, 5)
    return vector_law(key)


def draw_vec_momenta(key, part):
    key = jax.random.fold_in(key, 6)
    noise_draw = jax.random.normal(key, (LAYERS, VEC), jnp.float32)
    seg_scales = jnp.concatenate([jnp.full((2 * D,), 0.3, jnp.float32), jnp.full((2 * H,), 0.05, jnp.float32)])
    return noise_draw * seg_scales[None, :] * math.sqrt(TOKENS)


def draw_doc_lengths(key, part):
    key = jax.random.fold_in(key, 7)
    cut_key, head_key, pick_key = jax.random.split(key, 3)
    cut_points = jax.random.randint(cut_key, (STREAMS, DOCS - 2), 0, SLEN + 1)
    middle_cut = jnp.full((STREAMS, 1), SLEN // 2, jnp.int32)
    sorted_cuts = jnp.sort(jnp.concatenate([cut_points, middle_cut], axis=1), axis=1)
    edge_points = jnp.concatenate([jnp.zeros((STREAMS, 1), jnp.int32), sorted_cuts, jnp.full((STREAMS, 1), SLEN, jnp.int32)], axis=1)
    regular = edge_points[:, 1:] - edge_points[:, :-1]
    head_len = jax.random.randint(head_key, (STREAMS, 1), 1, SPAN)
    long_row = jnp.concatenate([head_len, jnp.full((STREAMS, 1), MOST, jnp.int32), SPAN - 1 - head_len, jnp.zeros((STREAMS, DOCS - 3), jnp.int32)], axis=1)
    chosen = jax.random.randint(pick_key, (STREAMS // STREAMS_DEV,), 0, STREAMS_DEV)
    pick_mask = jnp.arange(STREAMS) % STREAMS_DEV == jnp.repeat(chosen, STREAMS_DEV)
    return jnp.where(pick_mask[:, None], long_row, regular).astype(jnp.int32)


def shard_levels(stream_key, extent, cuts, low, high):
    def one(position, blocks):
        steps = jax.random.uniform(jax.random.fold_in(jax.random.fold_in(stream_key, 6), position), (blocks,), jnp.float32, low / len(cuts), high / len(cuts))
        return jnp.repeat(jnp.exp(steps), extent[position] // blocks).reshape((-1,) + (1,) * (len(extent) - position - 1))

    level = one(*cuts[0])
    for cut in cuts[1:]:
        level = level * one(*cut)
    return level


def normal_values(rng, shape, spread, limit, cuts=(), held_as=jnp.bfloat16):
    array = spread * jax.random.normal(rng, shape, jnp.float32)
    if cuts:
        array = array * shard_levels(rng, shape, cuts, -0.22, 0.18)
    return jnp.clip(array, -limit, limit).astype(held_as)


def setup_inputs(seed: int = 0) -> dict:
    key_list = jax.random.split(jax.random.key(seed), 10)
    stream_in = normal_values(key_list[0], (STREAMS, SLEN, D), 1.0, 6.0, ((0, 4), (1, 8)))
    out_grad = normal_values(key_list[1], (STREAMS, SLEN, D), 1.0, 6.0, ((0, 4), (1, 8)))
    doc_lengths = draw_doc_lengths(jax.random.fold_in(key_list[9], 71), 0)
    mats = draw_mats(jax.random.fold_in(key_list[9], 71), 0)
    mat_momenta = draw_mat_momenta(jax.random.fold_in(key_list[9], 71), 0)
    mat_averages = draw_mat_averages(jax.random.fold_in(key_list[9], 71), 0)
    vectors = draw_vectors(jax.random.fold_in(key_list[9], 71), 0)
    vec_momenta = draw_vec_momenta(jax.random.fold_in(key_list[9], 71), 0)
    vec_averages = draw_vec_averages(jax.random.fold_in(key_list[9], 71), 0)
    return {"stream_in": stream_in, "out_grad": out_grad, "doc_lengths": doc_lengths, "mats": mats, "mat_momenta": mat_momenta, "mat_averages": mat_averages, "vectors": vectors, "vec_momenta": vec_momenta, "vec_averages": vec_averages}


@jax.custom_vjp
def low(v):
    return lax.optimization_barrier(v.astype(jnp.bfloat16)).astype(jnp.float32)

@jax.custom_vjp
def low_back(v):
    return v

def low_keep(v):
    return (low(v), None)

def low_pass(kept, grad):
    return (grad,)

def back_keep(v):
    return (v, None)

def back_low(kept, grad):
    return (low(grad),)
low.defvjp(low_keep, low_pass)
low_back.defvjp(back_keep, back_low)
HIGHEST = lax.Precision.HIGHEST
EPSILON = 1e-05
MOMENTUM_DECAY = 0.5
AVERAGE_DECAY = 0.9
MATRIX_RATE = 0.3
SEGMENT_RATES = (0.3, 0.3, 0.5, 2.0)
QUINTIC = (3.4445, -4.775, 2.0315)

def row_offsets():
    return [0, HID_BLOCK, 2 * HID_BLOCK, 3 * HID_BLOCK, 4 * HID_BLOCK, 4 * HID_BLOCK + FFN_BLOCK, BLOCK_ROWS]

def split_full(full):
    offsets = row_offsets()
    result = []
    for layer_idx in range(LAYERS):
        result.append([full[layer_idx, :, offsets[member]:offsets[member + 1], :].reshape(ROW_BLOCKS * (offsets[member + 1] - offsets[member]), D) for member in range(6)])
    return result

def pack_full(per_layer):
    return jnp.stack([jnp.concatenate([matrix.reshape(ROW_BLOCKS, matrix.shape[0] // ROW_BLOCKS, D) for matrix in matrices], axis=1) for matrices in per_layer])

def rms_scale(values):
    return lax.rsqrt(lax.optimization_barrier(jnp.mean(values * values, axis=-1, keepdims=True)) + EPSILON)

def linked(earlier, latter):
    return (earlier[0] * latter[0], latter[0] * earlier[1] + latter[1])

def gelu_tanh(values):
    return jax.nn.gelu(values, approximate=True)

def build_mask(lengths):
    doc_starts = jnp.cumsum(lengths) - lengths
    positions = jnp.arange(SLEN, dtype=jnp.int32)
    return 1.0 - jnp.any(positions[:, None] == doc_starts[None, :], axis=1).astype(jnp.float32)

def layer_forward(residual, matrices, vector_row, carry_mask):
    w_forget, w_input, w_cand, w_out, w_up, w_down = [low(matrix) for matrix in matrices]
    gain_one = vector_row[:D]
    gain_two = vector_row[D:2 * D]
    bias_forget = vector_row[2 * D:2 * D + H]
    bias_input = vector_row[2 * D + H:]
    gated_in = low(residual * rms_scale(residual) * gain_one)
    pre_forget = low_back(jnp.dot(gated_in, w_forget.T, precision=HIGHEST, preferred_element_type=jnp.float32) + bias_forget)
    pre_input = low_back(jnp.dot(gated_in, w_input.T, precision=HIGHEST, preferred_element_type=jnp.float32) + bias_input)
    candidate = low_back(jnp.dot(gated_in, w_cand.T, precision=HIGHEST, preferred_element_type=jnp.float32))
    forget_gate = jax.nn.sigmoid(pre_forget)
    input_gate = jax.nn.sigmoid(pre_input)
    gate_total = forget_gate + input_gate
    decay_coef = forget_gate / gate_total * carry_mask[:, None]
    input_term = input_gate / gate_total * candidate
    states = lax.associative_scan(linked, (decay_coef, input_term), axis=0)[1]
    middle = residual + low_back(jnp.dot(low(states), w_out, precision=HIGHEST, preferred_element_type=jnp.float32))
    normed = low(middle * rms_scale(middle) * gain_two)
    inner_pre = low_back(jnp.dot(normed, w_up.T, precision=HIGHEST, preferred_element_type=jnp.float32))
    active = low(gelu_tanh(inner_pre))
    return middle + low_back(jnp.dot(active, w_down, precision=HIGHEST, preferred_element_type=jnp.float32))

def network(tokens_f, full_mats, vectors_f, carry_mask):
    per_layer = split_full(full_mats)
    residual = tokens_f
    for layer_idx in range(LAYERS):
        residual = layer_forward(residual, per_layer[layer_idx], vectors_f[layer_idx], carry_mask)
    return residual

def newton_schulz(momentum):
    iterate = (momentum / (jnp.sqrt(jnp.sum(momentum * momentum)) + 1e-07)).astype(jnp.bfloat16)
    for step_idx in range(NS_STEPS):
        iterate_f = iterate.astype(jnp.float32)
        row_groups = iterate_f.reshape(ROW_BLOCKS, iterate_f.shape[0] // ROW_BLOCKS, D)
        partials = jnp.einsum('brd,bre->bde', row_groups, row_groups, precision=HIGHEST)
        gram_sums = lax.optimization_barrier(jnp.sum(lax.optimization_barrier(partials.astype(jnp.bfloat16)).astype(jnp.float32), axis=0))
        gram_low = lax.optimization_barrier(gram_sums.astype(jnp.bfloat16)).astype(jnp.float32)
        polynomial = QUINTIC[1] * gram_sums + QUINTIC[2] * jnp.dot(gram_low, gram_low, precision=HIGHEST)
        poly_low = lax.optimization_barrier(polynomial.astype(jnp.bfloat16)).astype(jnp.float32)
        iterate = (QUINTIC[0] * iterate_f + jnp.dot(iterate_f, poly_low, precision=HIGHEST)).astype(jnp.bfloat16)
    return iterate.astype(jnp.float32)

def vector_steps(moments):
    edge_list = [0, D, 2 * D, 2 * D + H, 2 * D + 2 * H]
    pieces = []
    for member in range(4):
        segment = moments[:, edge_list[member]:edge_list[member + 1]]
        pieces.append(SEGMENT_RATES[member] * segment * lax.rsqrt(lax.optimization_barrier(jnp.mean(segment * segment, axis=1, keepdims=True)) + 1e-06))
    return jnp.concatenate(pieces, axis=1)

def reference(stream_in, out_grad, doc_lengths, mats, mat_momenta, mat_averages, vectors, vec_momenta, vec_averages):

    def per_stream(totals, stream_item):
        tokens, cotangent, lengths = stream_item
        carry_mask = build_mask(lengths)

        def closed(tokens_f, full_mats, vectors_f):
            return network(tokens_f, full_mats, vectors_f, carry_mask)
        output, pullback = jax.vjp(closed, tokens.astype(jnp.float32), mats, vectors)
        grad_tokens, grad_full, grad_vecs = pullback(cotangent.astype(jnp.float32))
        return ((totals[0] + grad_full, totals[1] + grad_vecs), (output.astype(jnp.bfloat16), grad_tokens))
    zero_sums = (jnp.zeros_like(mats), jnp.zeros_like(vectors))
    (mat_grads, vec_grads), (activations, input_grad) = lax.scan(per_stream, zero_sums, (stream_in, out_grad, doc_lengths))
    new_momenta = MOMENTUM_DECAY * mat_momenta + mat_grads
    row_counts = [H, H, H, H, FF, FF]
    orthogonal = [[newton_schulz(matrix) * (0.2 * math.sqrt(max(row_counts[member], D))) for member, matrix in enumerate(matrices)] for matrices in split_full(new_momenta)]
    new_mats = mats - MATRIX_RATE * pack_full(orthogonal)
    new_averages = AVERAGE_DECAY * mat_averages + (1.0 - AVERAGE_DECAY) * new_mats
    new_vec_momenta = MOMENTUM_DECAY * vec_momenta + vec_grads
    new_vectors = vectors - vector_steps(new_vec_momenta)
    new_vec_averages = AVERAGE_DECAY * vec_averages + (1.0 - AVERAGE_DECAY) * new_vectors
    return (activations, input_grad, mat_grads, new_momenta, new_mats, new_averages, vec_grads, new_vec_momenta, new_vectors, new_vec_averages)
```

```python
import functools
import math

import jax
import jax.numpy as jnp
from jax import lax
from jax.experimental import pallas as pl
from jax.experimental.pallas import tpu as pltpu
from jax.sharding import PartitionSpec as P

H = 1024
FF = 2048
NS_STEPS = 2
MESH = pl.DeviceIdType.MESH
F32 = jnp.float32
BF16 = jnp.bfloat16

EPSILON = 1e-05
MOMENTUM_DECAY = 0.5
AVERAGE_DECAY = 0.9
MATRIX_RATE = 0.3
SEGMENT_RATES = (0.3, 0.3, 0.5, 2.0)
QUINTIC = (3.4445, -4.775, 2.0315)
GELU_A = 0.7978845608
GELU_B = 0.044715


class Geometry:
    def __init__(self, n_seq, n_batch):
        self.n_seq, self.n_batch = n_seq, n_batch
        self.nz, self.ny, self.stride_z, self.stride_y = {
            8: (4, 2, 2, 1),
            32: (8, 4, 1, 8),
        }.get(n_seq, (n_seq, 1, 1, n_seq))
        self.nx = n_batch // 2
        self.swaps = self.ny == self.nx
        self.nu, self.nv = self.ny, self.nx

    def seq_of(self, z, y):
        return z * self.stride_z + y * self.stride_y

    def here(self):
        seq, batch = lax.axis_index("seq"), lax.axis_index("batch")
        z = seq // self.stride_z % self.nz
        y = seq // self.stride_y % self.ny
        return seq, batch, z, y, batch // 2, batch % 2

    def to_yx(self, u, v, core):
        if not self.swaps:
            return u, v
        return u + core * (v - u), v + core * (u - v)


def dot_nn(a, b):
    return lax.dot_general(a, b, (((1,), (0,)), ((), ())), preferred_element_type=F32)


def dot_nt(a, b):
    return lax.dot_general(a, b, (((1,), (1,)), ((), ())), preferred_element_type=F32)


def dot_tn(a, b):
    return lax.dot_general(a, b, (((0,), (0,)), ((), ())), preferred_element_type=F32)


def other(mine, step, count):
    return lax.rem(mine + step, count)


def enter(geo):
    seq, batch, z, y, x, core = geo.here()
    barrier = pltpu.get_barrier_semaphore()

    def greet(seq_id, batch_id):
        pl.semaphore_signal(barrier, inc=1, device_id=(seq_id, batch_id), device_id_type=MESH)

    for step in range(1, geo.n_seq):
        greet(other(seq, step, geo.n_seq), batch)
    for step in range(1, geo.nx):
        greet(seq, other(x, step, geo.nx) * 2 + core)
    greet(seq, x * 2 + 1 - core)
    pl.semaphore_wait(barrier, geo.n_seq - 1 + geo.nx - 1 + 1)


class Gather:
    def __init__(self, geo, weights, rows, send_z, send_u, send_v, send_s, recv, recv_s):
        self.geo, self.weights, self.rows = geo, weights, rows
        self.sems = (send_z, send_u, send_v, send_s, recv, recv_s)
        self.seq, self.batch, self.z, self.y, self.x, self.core = geo.here()
        if geo.swaps:
            self.u = self.y + self.core * (self.x - self.y)
            self.v = self.x + self.core * (self.y - self.x)
        else:
            self.u, self.v = self.y, self.x

    def slot(self, layer, z, u, v):
        y, x = self.geo.to_yx(u, v, self.core)
        start = pl.multiple_of(self.geo.seq_of(z, y) * self.rows, self.rows)
        return self.weights.at[layer, x * 2 + self.core, pl.ds(start, self.rows)]

    def number(self, layer, z, u, v):
        return ((layer * self.geo.nz + z) * self.geo.nu + u) * self.geo.nv + v

    def device(self, z, u, v, core):
        y, x = self.geo.to_yx(u, v, self.core)
        return (self.geo.seq_of(z, y), x * 2 + core)

    def copy(self, layer, z, u, v, device, send, recv):
        part = self.slot(layer, z, u, v)
        return pltpu.make_async_remote_copy(
            src_ref=part, dst_ref=part, send_sem=send, recv_sem=recv, device_id=device, device_id_type=MESH
        )

    def arrived(self, layer, z, u, v):
        recv = self.sems[4]
        self.copy(
            layer, z, u, v, self.device(self.z, self.u, self.v, 1 - self.core),
            self.sems[3].at[layer], recv.at[self.number(layer, z, u, v)],
        ).wait_recv()

    def to_z(self, layer):
        geo = self.geo
        for step in range(1, geo.nz):
            self.copy(
                layer, self.z, self.u, self.v,
                self.device(other(self.z, step, geo.nz), self.u, self.v, self.core),
                self.sems[0].at[layer, step - 1], self.sems[4].at[self.number(layer, self.z, self.u, self.v)],
            ).start()

    def to_u(self, layer, z):
        geo = self.geo
        for step in range(1, geo.nu):
            self.copy(
                layer, z, self.u, self.v,
                self.device(self.z, other(self.u, step, geo.nu), self.v, self.core),
                self.sems[1].at[layer, step - 1], self.sems[4].at[self.number(layer, z, self.u, self.v)],
            ).start()

    def to_v(self, layer, z, u):
        geo = self.geo
        for step in range(1, geo.nv):
            self.copy(
                layer, z, u, self.v,
                self.device(self.z, self.u, other(self.v, step, geo.nv), self.core),
                self.sems[2].at[layer, step - 1], self.sems[4].at[self.number(layer, z, u, self.v)],
            ).start()

    def to_sibling(self, layer, z, u, v):
        self.copy(
            layer, z, u, v, self.device(self.z, self.u, self.v, 1 - self.core),
            self.sems[3].at[layer], self.sems[5].at[layer],
        ).start()

    def begin(self, layer):
        self.to_z(layer)
        self.to_u(layer, self.z)
        self.to_v(layer, self.z, self.u)
        self.to_sibling(layer, self.z, self.u, self.v)

    def column(self, layer, step):
        z = lax.rem(self.z - step + self.geo.nz, self.geo.nz)
        self.arrived(layer, z, self.u, self.v)
        self.to_u(layer, z)
        self.to_v(layer, z, self.u)
        self.to_sibling(layer, z, self.u, self.v)

    def plane(self, layer, step):
        z = lax.rem(self.z - step + self.geo.nz, self.geo.nz)

        def one(k, _):
            u = other(self.u, k, self.geo.nu)
            self.arrived(layer, z, u, self.v)
            self.to_v(layer, z, u)
            self.to_sibling(layer, z, u, self.v)
            return 0

        lax.fori_loop(1, self.geo.nu, one, 0)

    def whole(self, layer, step_u, step_z):
        z = lax.rem(self.z - step_z + self.geo.nz, self.geo.nz)
        u = other(self.u, step_u, self.geo.nu)

        def one(k, _):
            v = other(self.v, k, self.geo.nv)
            self.arrived(layer, z, u, v)
            self.to_sibling(layer, z, u, v)
            return 0

        lax.fori_loop(1, self.geo.nv, one, 0)

    def finish(self, layer):
        geo = self.geo
        send_z, send_u, send_v, send_s, recv, recv_s = self.sems
        away = self.device(self.z, self.u, self.v, 1 - self.core)

        def drain(part, sem):
            pltpu.make_async_remote_copy(
                src_ref=part, dst_ref=part, send_sem=sem, recv_sem=recv_s.at[layer], device_id=away,
                device_id_type=MESH,
            ).wait_send()

        for step in range(1, geo.nz):
            drain(self.slot(layer, self.z, self.u, self.v), send_z.at[layer, step - 1])
        for step in range(1, geo.nu):
            drain(self.weights.at[layer, 0, pl.ds(0, geo.nz * self.rows)], send_u.at[layer, step - 1])
        for step in range(1, geo.nv):
            drain(self.weights.at[layer, 0, pl.ds(0, geo.nz * geo.nu * self.rows)], send_v.at[layer, step - 1])
        family = self.weights.at[layer, pl.ds(0, geo.nx)]
        drain(family, send_s.at[layer])
        pltpu.make_async_remote_copy(
            src_ref=family, dst_ref=family, send_sem=send_s.at[layer], recv_sem=recv_s.at[layer], device_id=away,
            device_id_type=MESH,
        ).wait_recv()

    def run(self, layer):
        geo = self.geo
        self.begin(layer)
        for step in range(1, geo.nz):
            self.column(layer, step)
            self.plane(layer, step - 1)
        self.plane(layer, geo.nz - 1)

        def one(k, _):
            self.whole(layer, k // geo.nz, k % geo.nz)
            return 0

        lax.fori_loop(0, geo.nu * geo.nz, one, 0)
        self.finish(layer)


def sigmoid(values):
    return 1.0 / (1.0 + jnp.exp(-values))


def widen(column_tile, width):
    return jnp.concatenate([column_tile] * (width // 128), axis=1)


def network_scratch(geo, sizes):
    layers, streams, span, width, hid, ffn, rows, docs = sizes
    tokens, nb = streams * span, geo.n_batch
    block = 4 * hid + 2 * ffn

    def full(dtype, *shape):
        return pltpu.VMEM(shape, dtype)

    dma = pltpu.SemaphoreType.DMA
    return [
        full(BF16, layers, nb, block, width),
        full(F32, layers + 1, tokens, width),
        full(BF16, layers, tokens, width),
        full(F32, layers, nb, tokens, hid),
        full(F32, layers, nb, tokens, hid),
        full(F32, layers, nb, tokens, hid),
        full(F32, layers, nb, tokens, hid),
        full(F32, layers, tokens, width),
        full(BF16, layers, tokens, width),
        full(F32, layers, nb, tokens, ffn),
        full(F32, layers, nb, 8, hid),
        full(F32, nb, tokens, hid),
        full(F32, tokens, 128),
        full(F32, 2 * layers, nb, 8, hid),
        full(F32, 2 * layers, geo.n_seq, nb, 8, hid),
        full(F32, tokens, width),
        full(BF16, tokens, width),
        full(F32, tokens, width),
        full(F32, tokens, hid),
        full(F32, tokens, hid),
        full(F32, nb, tokens, hid),
        full(F32, nb, tokens, hid),
        full(F32, nb, 8, hid),
        full(BF16, tokens, hid),
        full(BF16, tokens, hid),
        full(BF16, tokens, hid),
        full(F32, tokens, ffn),
        full(BF16, tokens, ffn),
        full(BF16, tokens, ffn),
        full(BF16, nb, block, width),
        full(F32, layers, 2, width),
        full(F32, layers, nb, 2, hid),
        full(F32, layers, 2, width),
        full(F32, layers, nb, 2, hid),
        dma((layers, max(geo.nz - 1, 1))),
        dma((layers, max(geo.nu - 1, 1))),
        dma((layers, max(geo.nv - 1, 1))),
        dma((layers,)),
        dma((layers * geo.nz * geo.nu * geo.nv,)),
        dma((layers,)),
        dma((2 * layers, geo.n_seq)),
        dma((2 * layers, geo.n_seq)),
        dma((1,)),
    ]


def network_kernel(
    geo, sizes, mats_ref, x_ref, out_grad_ref, doc_ref, vec_ref, act_ref, dx_ref, grads_ref, vgrad_ref, *scratch
):
    (
        weights, resid, gated, fgate, igate, cand, states, middle, normed, inner, carry_in, prods, mask, summary,
        mailbox, dgrad, low_grad, acc, tmp1, tmp2, gstates, deltas, incoming, low1, low2, low3, wide, wide_low1,
        wide_low2, gstage, gains, biases, ggains, gbiases, send_z, send_u, send_v, send_s, recv, recv_s, mail_send, mail_recv, out_sem,
    ) = scratch
    layers, streams, span, width, hid, ffn, rows, docs = sizes
    tokens = streams * span
    nb = geo.n_batch
    seq, batch, z, y, x, core = geo.here()
    hid_all, tile = hid * nb, 32

    def each_tile(body):
        lax.fori_loop(0, tokens // tile, lambda k, _: body(pl.ds(pl.multiple_of(k * tile, tile), tile)) or 0, 0)

    def each_block(body):
        lax.fori_loop(0, nb, lambda b, _: body(b) or 0, 0)

    for layer in range(layers):
        weights[layer, batch, pl.ds(pl.multiple_of(seq * rows, rows), rows), :] = mats_ref[layer, 0].astype(BF16)
    enter(geo)
    gather = Gather(geo, weights, rows, send_z, send_u, send_v, send_s, recv, recv_s)
    for layer in range(layers):
        gather.run(layer)

    def each_piece(body):
        for layer in range(layers):
            for k in range(2):
                body(slice(layer, layer + 1), slice(k * width, (k + 1) * width), k, gains, ggains, (layer,))
                for b in range(nb):
                    first = 2 * width + k * hid_all + b * hid
                    body(slice(layer, layer + 1), slice(first, first + hid), k, biases, gbiases, (layer, b))

    def read_piece(row, columns, k, kept, made, at):
        kept[(*at, slice(k, k + 1), slice(None))] = vec_ref[row, columns]

    def write_piece(row, columns, k, kept, made, at):
        vgrad_ref[row, columns] = made[(*at, slice(k, k + 1), slice(None))]

    each_piece(read_piece)

    for stream in range(streams):
        position = seq * span + lax.broadcasted_iota(jnp.int32, (span, 128), 0)
        begin, keep = jnp.int32(0), jnp.ones((span, 128), F32)
        for doc in range(docs):
            keep = jnp.where(position == begin, 0.0, keep)
            begin = begin + doc_ref[stream, doc]
        mask[stream * span : (stream + 1) * span, :] = keep

    def load_input(at):
        flat = x_ref[at, :].astype(F32)
        resid[0, at, :] = flat

    each_tile(load_input)

    def mail(number, forward):
        first, last = (seq + 1, geo.n_seq) if forward else (0, seq)

        def copy(peer, source):
            return pltpu.make_async_remote_copy(
                src_ref=summary.at[number], dst_ref=mailbox.at[number, source],
                send_sem=mail_send.at[number, peer], recv_sem=mail_recv.at[number, source],
                device_id=(peer, batch), device_id_type=MESH,
            )

        def start(peer, _):
            copy(peer, seq).start()
            return 0

        lax.fori_loop(first, last, start, 0)
        hops = seq if forward else geo.n_seq - 1 - seq

        def fold(k, before):
            source = k if forward else geo.n_seq - 1 - k
            copy(source, source).wait_recv()
            packed = mailbox[number, source]
            return packed[:, 2 : 2 + streams] + packed[:, 0:streams] * before

        total = lax.fori_loop(0, hops, fold, jnp.zeros((nb, streams, hid), F32))

        def finish(peer, _):
            copy(peer, seq).wait_send()
            return 0

        lax.fori_loop(first, last, finish, 0)
        return total

    groups = span // 8
    row8 = lax.broadcasted_iota(jnp.int32, (8, hid), 0)

    def forward(layer):
        gain_one = gains[layer, 0:1, :]
        gain_two = gains[layer, 1:2, :]

        def norm_one(at):
            values = resid[layer, at, :]
            scale = lax.rsqrt(jnp.mean(values * values, axis=-1, keepdims=True) + EPSILON)
            gated[layer, at, :] = (values * scale * gain_one).astype(BF16)

        each_tile(norm_one)

        def front(b):
            shift_f = biases[layer, b, 0:1, :]
            shift_i = biases[layer, b, 1:2, :]
            source = gated[layer]
            tmp1[...] = dot_nt(source, weights[layer, b, 0:hid, :]) + shift_f
            tmp2[...] = dot_nt(source, weights[layer, b, hid : 2 * hid, :]) + shift_i
            cand[layer, b] = dot_nt(source, weights[layer, b, 2 * hid : 3 * hid, :])

            def group(k, carried):
                new = []
                for stream in range(streams):
                    at = pl.ds(pl.multiple_of(stream * span + k * 8, 8), 8)
                    f, i = sigmoid(tmp1[at, :]), sigmoid(tmp2[at, :])
                    share = 1.0 / (f + i)
                    decay = f * share * widen(mask[at, :], hid)
                    term = i * share * cand[layer, b, at, :]
                    fgate[layer, b, at, :] = f
                    igate[layer, b, at, :] = i
                    for step in (1, 2, 4):
                        reach = row8 >= step
                        term = term + decay * jnp.where(reach, pltpu.roll(term, step, 0), 0.0)
                        decay = decay * jnp.where(reach, pltpu.roll(decay, step, 0), 1.0)
                    prod_in, state_in = carried[stream]
                    term = term + decay * state_in
                    decay = decay * prod_in
                    states[layer, b, at, :] = term
                    prods[b, at, :] = decay
                    new.append((decay[7:8], term[7:8]))
                return tuple(new)

            start = tuple((jnp.ones((1, hid), F32), jnp.zeros((1, hid), F32)) for _ in range(streams))
            last = lax.fori_loop(0, groups, group, start)
            for stream in range(streams):
                summary[layer, b, stream : stream + 1, :] = last[stream][0]
                summary[layer, b, 2 + stream : 3 + stream, :] = last[stream][1]

        each_block(front)
        carry_in[layer, :, 0:streams, :] = mail(layer, True)
        acc[...] = jnp.zeros_like(acc)

        def rear(b):
            for stream in range(streams):
                at = slice(stream * span, (stream + 1) * span)
                full = states[layer, b, at, :] + prods[b, at, :] * carry_in[layer, b, stream : stream + 1, :]
                states[layer, b, at, :] = full
                low1[at, :] = full.astype(BF16)
            acc[...] += dot_nn(low1[...], weights[layer, b, 3 * hid : 4 * hid, :])

        each_block(rear)

        def norm_two(at):
            values = resid[layer, at, :] + acc[at, :]
            middle[layer, at, :] = values
            scale = lax.rsqrt(jnp.mean(values * values, axis=-1, keepdims=True) + EPSILON)
            normed[layer, at, :] = (values * scale * gain_two).astype(BF16)

        each_tile(norm_two)
        acc[...] = middle[layer]

        def mlp(b):
            inner[layer, b] = dot_nt(normed[layer], weights[layer, b, 4 * hid : 4 * hid + ffn, :])

            def act(at):
                v = inner[layer, b, at, :]
                t = jnp.tanh(GELU_A * (v + GELU_B * (v * v * v)))
                wide_low1[at, :] = (0.5 * v * (1.0 + t)).astype(BF16)

            each_tile(act)
            acc[...] += dot_nn(wide_low1[...], weights[layer, b, 4 * hid + ffn : 4 * hid + 2 * ffn, :])

        each_block(mlp)
        resid[layer + 1] = acc[...]

    def put_grad(layer, b, first, count, value):
        gstage[b, pl.ds(first, count), :] = value.astype(BF16)

    def backward(layer):
        gain_one = gains[layer, 0:1, :]
        gain_two = gains[layer, 1:2, :]
        low_grad[...] = dgrad[...].astype(BF16)
        acc[...] = jnp.zeros_like(acc)

        def mlp(b):
            wide[...] = dot_nt(low_grad[...], weights[layer, b, 4 * hid + ffn : 4 * hid + 2 * ffn, :])

            def act(at):
                v = inner[layer, b, at, :]
                square = v * v
                t = jnp.tanh(GELU_A * (v + GELU_B * (v * square)))
                half = 0.5 * (1.0 + t)
                wide_low1[at, :] = (v * half).astype(BF16)
                slope = half + 0.5 * v * (1.0 - t * t) * (GELU_A * (1.0 + 3.0 * GELU_B * square))
                wide_low2[at, :] = (wide[at, :] * slope).astype(BF16)

            each_tile(act)
            put_grad(layer, b, 4 * hid + ffn, ffn, dot_tn(wide_low1[...], low_grad[...]))
            put_grad(layer, b, 4 * hid, ffn, dot_tn(wide_low2[...], normed[layer]))
            acc[...] += dot_nn(wide_low2[...], weights[layer, b, 4 * hid : 4 * hid + ffn, :])

        each_block(mlp)
        row_sum = jnp.zeros((1, width), F32)

        def norm_two(k, total):
            at = pl.ds(pl.multiple_of(k * tile, tile), tile)
            values, grad = middle[layer, at, :], acc[at, :]
            scale = lax.rsqrt(jnp.mean(values * values, axis=-1, keepdims=True) + EPSILON)
            unit = values * scale
            gunit = grad * gain_two
            full = dgrad[at, :] + scale * (gunit - unit * jnp.mean(gunit * unit, axis=-1, keepdims=True))
            dgrad[at, :] = full
            low_grad[at, :] = full.astype(BF16)
            return total + jnp.sum(grad * unit, axis=0, keepdims=True)

        ggains[layer, 1:2, :] = lax.fori_loop(0, tokens // tile, norm_two, row_sum)
        number = layers + layer

        def front(b):
            low1[...] = states[layer, b].astype(BF16)
            put_grad(layer, b, 3 * hid, hid, dot_tn(low1[...], low_grad[...]))
            gstates[b] = dot_nt(low_grad[...], weights[layer, b, 3 * hid : 4 * hid, :])

            def group(k, carried):
                new = []
                for stream in range(streams):
                    at = pl.ds(pl.multiple_of(stream * span + (groups - 1 - k) * 8, 8), 8)
                    f, i = fgate[layer, b, at, :], igate[layer, b, at, :]
                    decay = f * (1.0 / (f + i)) * widen(mask[at, :], hid)
                    term = decay * gstates[b, at, :]
                    for step in (1, 2, 4):
                        reach = row8 < 8 - step
                        term = term + decay * jnp.where(reach, pltpu.roll(term, 8 - step, 0), 0.0)
                        decay = decay * jnp.where(reach, pltpu.roll(decay, 8 - step, 0), 1.0)
                    prod_in, state_in = carried[stream]
                    term = term + decay * state_in
                    decay = decay * prod_in
                    deltas[b, at, :] = term
                    prods[b, at, :] = decay
                    new.append((decay[0:1], term[0:1]))
                return tuple(new)

            start = tuple((jnp.ones((1, hid), F32), jnp.zeros((1, hid), F32)) for _ in range(streams))
            last = lax.fori_loop(0, groups, group, start)
            for stream in range(streams):
                summary[number, b, stream : stream + 1, :] = last[stream][0]
                summary[number, b, 2 + stream : 3 + stream, :] = last[stream][1]

        each_block(front)
        incoming[:, 0:streams, :] = mail(number, False)
        acc[...] = jnp.zeros_like(acc)
        span_row = lax.broadcasted_iota(jnp.int32, (span, hid), 0)

        def rear(b):
            sum_f, sum_i = jnp.zeros((1, hid), F32), jnp.zeros((1, hid), F32)
            for stream in range(streams):
                at = slice(stream * span, (stream + 1) * span)
                late = incoming[b, stream : stream + 1, :]
                linked = deltas[b, at, :] + prods[b, at, :] * late
                linked = jnp.where(span_row == span - 1, late, pltpu.roll(linked, span - 1, 0))
                delta = gstates[b, at, :] + linked
                early = carry_in[layer, b, stream : stream + 1, :]
                before = jnp.where(span_row == 0, early, pltpu.roll(states[layer, b, at, :], 1, 0))
                f, i = fgate[layer, b, at, :], igate[layer, b, at, :]
                share = 1.0 / (f + i)
                fshare, ishare = f * share, i * share
                gap = delta * (before * widen(mask[at, :], hid) - cand[layer, b, at, :]) * fshare * ishare
                gf = (gap * (1.0 - f)).astype(BF16)
                gi = (gap * (i - 1.0)).astype(BF16)
                low1[at, :], low2[at, :], low3[at, :] = gf, gi, (delta * ishare).astype(BF16)
                sum_f = sum_f + jnp.sum(gf.astype(F32), axis=0, keepdims=True)
                sum_i = sum_i + jnp.sum(gi.astype(F32), axis=0, keepdims=True)
            gbiases[layer, b, 0:1, :] = sum_f
            gbiases[layer, b, 1:2, :] = sum_i
            total = acc[...]
            for member, low in enumerate((low1, low2, low3)):
                put_grad(layer, b, member * hid, hid, dot_tn(low[...], gated[layer]))
                total = total + dot_nn(low[...], weights[layer, b, member * hid : (member + 1) * hid, :])
            acc[...] = total

        each_block(rear)

        def norm_one(k, total):
            at = pl.ds(pl.multiple_of(k * tile, tile), tile)
            values, grad = resid[layer, at, :], acc[at, :]
            scale = lax.rsqrt(jnp.mean(values * values, axis=-1, keepdims=True) + EPSILON)
            unit = values * scale
            gunit = grad * gain_one
            full = dgrad[at, :] + scale * (gunit - unit * jnp.mean(gunit * unit, axis=-1, keepdims=True))
            dgrad[at, :] = full
            return total + jnp.sum(grad * unit, axis=0, keepdims=True)

        ggains[layer, 0:1, :] = lax.fori_loop(0, tokens // tile, norm_one, row_sum)

    def take_out(layer):
        return pltpu.make_async_copy(gstage, grads_ref.at[layer], out_sem.at[0])

    def back_step(k, _):
        layer = layers - 1 - k

        @pl.when(k > 0)
        def _():
            take_out(layer + 1).wait()

        backward(layer)
        take_out(layer).start()
        return 0

    lax.fori_loop(0, layers, lambda layer, _: forward(layer) or 0, 0)

    def turn(at):
        act_ref[at, :] = resid[layers, at, :].astype(BF16)
        dgrad[at, :] = out_grad_ref[at, :].astype(F32)

    each_tile(turn)
    lax.fori_loop(0, layers, back_step, 0)
    dx_ref[...] = dgrad[...]
    each_piece(write_piece)
    take_out(0).wait()


def run_network(geo, mats, stream_in, out_grad, doc_lengths, vectors):
    layers, _, rows, width = mats.shape
    streams, span, _ = stream_in.shape
    hid, ffn = H // geo.n_batch, FF // geo.n_batch
    sizes = (layers, streams, span, width, hid, ffn, rows, doc_lengths.shape[1])
    tokens = streams * span
    vmem = pl.BlockSpec(memory_space=pltpu.VMEM)
    return pl.pallas_call(
        functools.partial(network_kernel, geo, sizes),
        out_shape=(
            jax.ShapeDtypeStruct((tokens, width), BF16),
            jax.ShapeDtypeStruct((tokens, width), F32),
            jax.ShapeDtypeStruct((layers, geo.n_batch, 4 * hid + 2 * ffn, width), BF16),
            jax.ShapeDtypeStruct(vectors.shape, F32),
        ),
        in_specs=[vmem, vmem, vmem, pl.BlockSpec(memory_space=pltpu.SMEM), vmem],
        out_specs=(vmem, vmem, pl.BlockSpec(memory_space=pl.ANY), vmem),
        scratch_shapes=network_scratch(geo, sizes),
        compiler_params=pltpu.CompilerParams(
            collective_id=0, has_side_effects=True, vmem_limit_bytes=62 * 2**20
        ),
        name="network",
    )(mats, stream_in.reshape(tokens, width), out_grad.reshape(tokens, width), doc_lengths, vectors)


def vector_steps(moments, model_width, hidden):
    edge_list = [0, model_width, 2 * model_width, 2 * model_width + hidden, 2 * model_width + 2 * hidden]
    pieces = []
    for member in range(4):
        segment = moments[:, edge_list[member] : edge_list[member + 1]]
        pieces.append(
            SEGMENT_RATES[member]
            * segment
            * lax.rsqrt(jnp.mean(segment * segment, axis=1, keepdims=True) + 1e-06)
        )
    return jnp.concatenate(pieces, axis=1)


def per_device(
    geo, stream_in, out_grad, doc_lengths, mats, mat_momenta, mat_averages, vectors, vec_momenta, vec_averages
):
    layer_count, _, shard_rows, model_width = mats.shape
    activations, grad_resid, full_grads, vec_part = run_network(
        geo, mats, stream_in, out_grad, doc_lengths, vectors
    )
    offsets = [0]
    for count in [H // geo.n_batch] * 4 + [FF // geo.n_batch] * 2:
        offsets.append(offsets[-1] + count)
    block_rows = offsets[6]
    grad_shard = lax.psum_scatter(
        full_grads.astype(F32).reshape(layer_count, geo.n_batch * block_rows, model_width),
        ("batch", "seq"), scatter_dimension=1, tiled=True,
    )
    vec_grads = lax.psum(vec_part, ("batch", "seq"))
    mom_shard = MOMENTUM_DECAY * mat_momenta.reshape(layer_count, shard_rows, model_width) + grad_shard
    mom_block = lax.all_gather(mom_shard.astype(BF16), "seq", axis=1, tiled=True).astype(F32)
    pieces = [
        mom_block[layer_idx, offsets[member] : offsets[member + 1]]
        for layer_idx in range(layer_count)
        for member in range(6)
    ]
    local_squares = jnp.stack([jnp.sum(piece * piece) for piece in pieces])
    frob_norms = jnp.sqrt(lax.psum(local_squares, "batch"))
    iterates = [(piece / (frob_norms[n] + 1e-07)).astype(BF16) for n, piece in enumerate(pieces)]
    for step_idx in range(NS_STEPS):
        partials = jnp.stack([dot_tn(iterate, iterate) for iterate in iterates])
        gram_sums = lax.psum(partials.astype(BF16), "batch").astype(F32)
        gram_low = gram_sums.astype(BF16)
        polynomial = QUINTIC[1] * gram_sums + QUINTIC[2] * jnp.einsum(
            "nde,nef->ndf", gram_low, gram_low, preferred_element_type=F32
        )
        poly_low = polynomial.astype(BF16)
        iterates = [
            (QUINTIC[0] * iterate.astype(F32) + dot_nn(iterate, poly_low[n])).astype(BF16)
            for n, iterate in enumerate(iterates)
        ]
    factors = [0.2 * math.sqrt(max(count, model_width)) for count in [H] * 4 + [FF] * 2]
    ortho_block = jnp.stack(
        [
            jnp.concatenate([iterates[6 * l + m].astype(F32) * factors[m] for m in range(6)], axis=0)
            for l in range(layer_count)
        ]
    )
    own_rows = lax.dynamic_slice_in_dim(ortho_block, lax.axis_index("seq") * shard_rows, shard_rows, axis=1)
    new_flat = mats.reshape(layer_count, shard_rows, model_width) - MATRIX_RATE * own_rows
    new_avg_flat = (
        AVERAGE_DECAY * mat_averages.reshape(layer_count, shard_rows, model_width)
        + (1.0 - AVERAGE_DECAY) * new_flat
    )
    new_vec_momenta = MOMENTUM_DECAY * vec_momenta + vec_grads
    new_vectors = vectors - vector_steps(new_vec_momenta, model_width, H)
    new_vec_averages = AVERAGE_DECAY * vec_averages + (1.0 - AVERAGE_DECAY) * new_vectors
    out_shape = (layer_count, 1, shard_rows, model_width)
    return (
        activations.reshape(stream_in.shape),
        grad_resid.reshape(stream_in.shape),
        grad_shard.reshape(out_shape),
        mom_block.reshape(layer_count, 1, block_rows, model_width),
        new_flat.reshape(out_shape),
        new_avg_flat.reshape(out_shape),
        vec_grads,
        new_vec_momenta,
        new_vectors,
        new_vec_averages,
    )


def solution(mesh):
    geo = Geometry(mesh.shape["seq"], mesh.shape["batch"])
    rows = P(None, "batch", "seq", None)
    tokens = P("batch", "seq", None)
    return jax.shard_map(
        functools.partial(per_device, geo),
        mesh=mesh,
        in_specs=(tokens, tokens, P("batch", None), rows, rows, rows, P(), P(), P()),
        out_specs=(tokens, tokens, rows, P(None, "batch", None, None), rows, rows, P(), P(), P(), P()),
        check_vma=False,
    )
```

```python
import functools
import math

import jax
import jax.numpy as jnp
from jax import lax
from jax.experimental import pallas as pl
from jax.experimental.pallas import tpu as pltpu
from jax.sharding import PartitionSpec as P

H = 1024
FF = 2048
NS_STEPS = 2
MESH = pl.DeviceIdType.MESH
F32 = jnp.float32
BF16 = jnp.bfloat16

EPSILON = 1e-05
MOMENTUM_DECAY = 0.5
AVERAGE_DECAY = 0.9
MATRIX_RATE = 0.3
SEGMENT_RATES = (0.3, 0.3, 0.5, 2.0)
QUINTIC = (3.4445, -4.775, 2.0315)
GELU_A = 0.7978845608
GELU_B = 0.044715


class Geometry:
    def __init__(self, n_seq, n_batch):
        self.n_seq, self.n_batch = n_seq, n_batch
        self.nz, self.ny, self.stride_z, self.stride_y = {
            8: (4, 2, 2, 1),
            32: (8, 4, 1, 8),
        }.get(n_seq, (n_seq, 1, 1, n_seq))
        self.nx = n_batch // 2
        self.swaps = self.ny == self.nx
        self.nu, self.nv = self.ny, self.nx

    def seq_of(self, z, y):
        return z * self.stride_z + y * self.stride_y

    def here(self):
        seq, batch = lax.axis_index("seq"), lax.axis_index("batch")
        z = seq // self.stride_z % self.nz
        y = seq // self.stride_y % self.ny
        return seq, batch, z, y, batch // 2, batch % 2

    def to_yx(self, u, v, core):
        if not self.swaps:
            return u, v
        return u + core * (v - u), v + core * (u - v)


def dot_nn(a, b):
    return lax.dot_general(a, b, (((1,), (0,)), ((), ())), preferred_element_type=F32)


def dot_nt(a, b):
    return lax.dot_general(a, b, (((1,), (1,)), ((), ())), preferred_element_type=F32)


def dot_tn(a, b):
    return lax.dot_general(a, b, (((0,), (0,)), ((), ())), preferred_element_type=F32)


def other(mine, step, count):
    return lax.rem(mine + step, count)


def enter(geo):
    seq, batch, z, y, x, core = geo.here()
    barrier = pltpu.get_barrier_semaphore()

    def greet(seq_id, batch_id):
        pl.semaphore_signal(barrier, inc=1, device_id=(seq_id, batch_id), device_id_type=MESH)

    for step in range(1, geo.n_seq):
        greet(other(seq, step, geo.n_seq), batch)
    for step in range(1, geo.nx):
        greet(seq, other(x, step, geo.nx) * 2 + core)
    greet(seq, x * 2 + 1 - core)
    pl.semaphore_wait(barrier, geo.n_seq - 1 + geo.nx - 1 + 1)


class Gather:
    def __init__(self, geo, weights, rows, send_z, send_u, send_v, send_s, recv, recv_s):
        self.geo, self.weights, self.rows = geo, weights, rows
        self.sems = (send_z, send_u, send_v, send_s, recv, recv_s)
        self.seq, self.batch, self.z, self.y, self.x, self.core = geo.here()
        if geo.swaps:
            self.u = self.y + self.core * (self.x - self.y)
            self.v = self.x + self.core * (self.y - self.x)
        else:
            self.u, self.v = self.y, self.x

    def slot(self, layer, z, u, v):
        y, x = self.geo.to_yx(u, v, self.core)
        start = pl.multiple_of(self.geo.seq_of(z, y) * self.rows, self.rows)
        return self.weights.at[layer, x * 2 + self.core, pl.ds(start, self.rows)]

    def number(self, layer, z, u, v):
        return ((layer * self.geo.nz + z) * self.geo.nu + u) * self.geo.nv + v

    def device(self, z, u, v, core):
        y, x = self.geo.to_yx(u, v, self.core)
        return (self.geo.seq_of(z, y), x * 2 + core)

    def copy(self, layer, z, u, v, device, send, recv):
        part = self.slot(layer, z, u, v)
        return pltpu.make_async_remote_copy(
            src_ref=part, dst_ref=part, send_sem=send, recv_sem=recv, device_id=device, device_id_type=MESH
        )

    def arrived(self, layer, z, u, v):
        recv = self.sems[4]
        self.copy(
            layer, z, u, v, self.device(self.z, self.u, self.v, 1 - self.core),
            self.sems[3].at[layer], recv.at[self.number(layer, z, u, v)],
        ).wait_recv()

    def to_z(self, layer):
        geo = self.geo
        for step in range(1, geo.nz):
            self.copy(
                layer, self.z, self.u, self.v,
                self.device(other(self.z, step, geo.nz), self.u, self.v, self.core),
                self.sems[0].at[layer, step - 1], self.sems[4].at[self.number(layer, self.z, self.u, self.v)],
            ).start()

    def to_u(self, layer, z):
        geo = self.geo
        for step in range(1, geo.nu):
            self.copy(
                layer, z, self.u, self.v,
                self.device(self.z, other(self.u, step, geo.nu), self.v, self.core),
                self.sems[1].at[layer, step - 1], self.sems[4].at[self.number(layer, z, self.u, self.v)],
            ).start()

    def to_v(self, layer, z, u):
        geo = self.geo
        for step in range(1, geo.nv):
            self.copy(
                layer, z, u, self.v,
                self.device(self.z, self.u, other(self.v, step, geo.nv), self.core),
                self.sems[2].at[layer, step - 1], self.sems[4].at[self.number(layer, z, u, self.v)],
            ).start()

    def to_sibling(self, layer, z, u, v):
        self.copy(
            layer, z, u, v, self.device(self.z, self.u, self.v, 1 - self.core),
            self.sems[3].at[layer], self.sems[5].at[layer],
        ).start()

    def begin(self, layer):
        self.to_z(layer)
        self.to_u(layer, self.z)
        self.to_v(layer, self.z, self.u)
        self.to_sibling(layer, self.z, self.u, self.v)

    def column(self, layer, step):
        z = lax.rem(self.z - step + self.geo.nz, self.geo.nz)
        self.arrived(layer, z, self.u, self.v)
        self.to_u(layer, z)
        self.to_v(layer, z, self.u)
        self.to_sibling(layer, z, self.u, self.v)

    def plane(self, layer, step):
        z = lax.rem(self.z - step + self.geo.nz, self.geo.nz)

        def one(k, _):
            u = other(self.u, k, self.geo.nu)
            self.arrived(layer, z, u, self.v)
            self.to_v(layer, z, u)
            self.to_sibling(layer, z, u, self.v)
            return 0

        lax.fori_loop(1, self.geo.nu, one, 0)

    def whole(self, layer, step_u, step_z):
        z = lax.rem(self.z - step_z + self.geo.nz, self.geo.nz)
        u = other(self.u, step_u, self.geo.nu)

        def one(k, _):
            v = other(self.v, k, self.geo.nv)
            self.arrived(layer, z, u, v)
            self.to_sibling(layer, z, u, v)
            return 0

        lax.fori_loop(1, self.geo.nv, one, 0)

    def finish(self, layer):
        geo = self.geo
        send_z, send_u, send_v, send_s, recv, recv_s = self.sems
        away = self.device(self.z, self.u, self.v, 1 - self.core)

        def drain(part, sem):
            pltpu.make_async_remote_copy(
                src_ref=part, dst_ref=part, send_sem=sem, recv_sem=recv_s.at[layer], device_id=away,
                device_id_type=MESH,
            ).wait_send()

        for step in range(1, geo.nz):
            drain(self.slot(layer, self.z, self.u, self.v), send_z.at[layer, step - 1])
        for step in range(1, geo.nu):
            drain(self.weights.at[layer, 0, pl.ds(0, geo.nz * self.rows)], send_u.at[layer, step - 1])
        for step in range(1, geo.nv):
            drain(self.weights.at[layer, 0, pl.ds(0, geo.nz * geo.nu * self.rows)], send_v.at[layer, step - 1])
        family = self.weights.at[layer, pl.ds(0, geo.nx)]
        drain(family, send_s.at[layer])
        pltpu.make_async_remote_copy(
            src_ref=family, dst_ref=family, send_sem=send_s.at[layer], recv_sem=recv_s.at[layer], device_id=away,
            device_id_type=MESH,
        ).wait_recv()

    def run(self, layer):
        geo = self.geo
        self.begin(layer)
        for step in range(1, geo.nz):
            self.column(layer, step)
            self.plane(layer, step - 1)
        self.plane(layer, geo.nz - 1)

        def one(k, _):
            self.whole(layer, k // geo.nz, k % geo.nz)
            return 0

        lax.fori_loop(0, geo.nu * geo.nz, one, 0)
        self.finish(layer)


def sigmoid(values):
    return 1.0 / (1.0 + jnp.exp(-values))


def widen(column_tile, width):
    return jnp.concatenate([column_tile] * (width // 128), axis=1)


def network_scratch(geo, sizes):
    layers, streams, span, width, hid, ffn, rows, docs = sizes
    tokens, nb = streams * span, geo.n_batch
    block = 4 * hid + 2 * ffn

    def full(dtype, *shape):
        return pltpu.VMEM(shape, dtype)

    dma = pltpu.SemaphoreType.DMA
    return [
        full(BF16, layers, nb, block, width),
        full(F32, layers + 1, tokens, width),
        full(BF16, layers, tokens, width),
        full(F32, layers, nb, tokens, hid),
        full(F32, layers, nb, tokens, hid),
        full(F32, layers, nb, tokens, hid),
        full(F32, layers, nb, tokens, hid),
        full(F32, layers, tokens, width),
        full(BF16, layers, tokens, width),
        full(F32, layers, nb, tokens, ffn),
        full(F32, layers, nb, 8, hid),
        full(F32, nb, tokens, hid),
        full(F32, tokens, 128),
        full(F32, 2 * layers, nb, 8, hid),
        full(F32, 2 * layers, geo.n_seq, nb, 8, hid),
        full(F32, tokens, width),
        full(BF16, tokens, width),
        full(F32, tokens, width),
        full(F32, tokens, hid),
        full(F32, tokens, hid),
        full(F32, nb, tokens, hid),
        full(F32, nb, tokens, hid),
        full(F32, nb, 8, hid),
        full(BF16, tokens, hid),
        full(BF16, tokens, hid),
        full(BF16, tokens, hid),
        full(F32, tokens, ffn),
        full(BF16, tokens, ffn),
        full(BF16, tokens, ffn),
        full(BF16, nb, block, width),
        full(F32, layers, 2, width),
        full(F32, layers, nb, 2, hid),
        full(F32, layers, 2, width),
        full(F32, layers, nb, 2, hid),
        dma((layers, max(geo.nz - 1, 1))),
        dma((layers, max(geo.nu - 1, 1))),
        dma((layers, max(geo.nv - 1, 1))),
        dma((layers,)),
        dma((layers * geo.nz * geo.nu * geo.nv,)),
        dma((layers,)),
        dma((2 * layers, geo.n_seq)),
        dma((2 * layers, geo.n_seq)),
        dma((1,)),
    ]


def network_kernel(
    geo, sizes, mats_ref, x_ref, out_grad_ref, doc_ref, vec_ref, act_ref, dx_ref, grads_ref, vgrad_ref, *scratch
):
    (
        weights, resid, gated, fgate, igate, cand, states, middle, normed, inner, carry_in, prods, mask, summary,
        mailbox, dgrad, low_grad, acc, tmp1, tmp2, gstates, deltas, incoming, low1, low2, low3, wide, wide_low1,
        wide_low2, gstage, gains, biases, ggains, gbiases, send_z, send_u, send_v, send_s, recv, recv_s, mail_send, mail_recv, out_sem,
    ) = scratch
    layers, streams, span, width, hid, ffn, rows, docs = sizes
    tokens = streams * span
    nb = geo.n_batch
    seq, batch, z, y, x, core = geo.here()
    hid_all, tile = hid * nb, 32

    def each_tile(body):
        lax.fori_loop(0, tokens // tile, lambda k, _: body(pl.ds(pl.multiple_of(k * tile, tile), tile)) or 0, 0)

    def each_block(body):
        lax.fori_loop(0, nb, lambda b, _: body(b) or 0, 0)

    for layer in range(layers):
        weights[layer, batch, pl.ds(pl.multiple_of(seq * rows, rows), rows), :] = mats_ref[layer, 0].astype(BF16)
    enter(geo)
    gather = Gather(geo, weights, rows, send_z, send_u, send_v, send_s, recv, recv_s)
    for layer in range(layers):
        gather.run(layer)

    def each_piece(body):
        for layer in range(layers):
            for k in range(2):
                body(slice(layer, layer + 1), slice(k * width, (k + 1) * width), k, gains, ggains, (layer,))
                for b in range(nb):
                    first = 2 * width + k * hid_all + b * hid
                    body(slice(layer, layer + 1), slice(first, first + hid), k, biases, gbiases, (layer, b))

    def read_piece(row, columns, k, kept, made, at):
        kept[(*at, slice(k, k + 1), slice(None))] = vec_ref[row, columns]

    def write_piece(row, columns, k, kept, made, at):
        vgrad_ref[row, columns] = made[(*at, slice(k, k + 1), slice(None))]

    each_piece(read_piece)

    for stream in range(streams):
        position = seq * span + lax.broadcasted_iota(jnp.int32, (span, 128), 0)
        begin, keep = jnp.int32(0), jnp.ones((span, 128), F32)
        for doc in range(docs):
            keep = jnp.where(position == begin, 0.0, keep)
            begin = begin + doc_ref[stream, doc]
        mask[stream * span : (stream + 1) * span, :] = keep

    def load_input(at):
        flat = x_ref[at, :].astype(F32)
        resid[0, at, :] = flat

    each_tile(load_input)

    def mail(number, forward):
        first, last = (seq + 1, geo.n_seq) if forward else (0, seq)

        def copy(peer, source):
            return pltpu.make_async_remote_copy(
                src_ref=summary.at[number], dst_ref=mailbox.at[number, source],
                send_sem=mail_send.at[number, peer], recv_sem=mail_recv.at[number, source],
                device_id=(peer, batch), device_id_type=MESH,
            )

        def start(peer, _):
            copy(peer, seq).start()
            return 0

        lax.fori_loop(first, last, start, 0)
        hops = seq if forward else geo.n_seq - 1 - seq

        def fold(k, before):
            source = k if forward else geo.n_seq - 1 - k
            copy(source, source).wait_recv()
            packed = mailbox[number, source]
            return packed[:, 2 : 2 + streams] + packed[:, 0:streams] * before

        total = lax.fori_loop(0, hops, fold, jnp.zeros((nb, streams, hid), F32))

        def finish(peer, _):
            copy(peer, seq).wait_send()
            return 0

        lax.fori_loop(first, last, finish, 0)
        return total

    groups = span // 8
    row8 = lax.broadcasted_iota(jnp.int32, (8, hid), 0)

    def forward(layer):
        gain_one = gains[layer, 0:1, :]
        gain_two = gains[layer, 1:2, :]

        def norm_one(at):
            values = resid[layer, at, :]
            scale = lax.rsqrt(jnp.mean(values * values, axis=-1, keepdims=True) + EPSILON)
            gated[layer, at, :] = (values * scale * gain_one).astype(BF16)

        each_tile(norm_one)

        def front(b):
            shift_f = biases[layer, b, 0:1, :]
            shift_i = biases[layer, b, 1:2, :]
            source = gated[layer]
            tmp1[...] = dot_nt(source, weights[layer, b, 0:hid, :]) + shift_f
            tmp2[...] = dot_nt(source, weights[layer, b, hid : 2 * hid, :]) + shift_i
            cand[layer, b] = dot_nt(source, weights[layer, b, 2 * hid : 3 * hid, :])

            def group(k, carried):
                new = []
                for stream in range(streams):
                    at = pl.ds(pl.multiple_of(stream * span + k * 8, 8), 8)
                    f, i = sigmoid(tmp1[at, :]), sigmoid(tmp2[at, :])
                    share = 1.0 / (f + i)
                    decay = f * share * widen(mask[at, :], hid)
                    term = i * share * cand[layer, b, at, :]
                    fgate[layer, b, at, :] = f
                    igate[layer, b, at, :] = i
                    for step in (1, 2, 4):
                        reach = row8 >= step
                        term = term + decay * jnp.where(reach, pltpu.roll(term, step, 0), 0.0)
                        decay = decay * jnp.where(reach, pltpu.roll(decay, step, 0), 1.0)
                    prod_in, state_in = carried[stream]
                    term = term + decay * state_in
                    decay = decay * prod_in
                    states[layer, b, at, :] = term
                    prods[b, at, :] = decay
                    new.append((decay[7:8], term[7:8]))
                return tuple(new)

            start = tuple((jnp.ones((1, hid), F32), jnp.zeros((1, hid), F32)) for _ in range(streams))
            last = lax.fori_loop(0, groups, group, start)
            for stream in range(streams):
                summary[layer, b, stream : stream + 1, :] = last[stream][0]
                summary[layer, b, 2 + stream : 3 + stream, :] = last[stream][1]

        each_block(front)
        carry_in[layer, :, 0:streams, :] = mail(layer, True)
        acc[...] = jnp.zeros_like(acc)

        def rear(b):
            for stream in range(streams):
                at = slice(stream * span, (stream + 1) * span)
                full = states[layer, b, at, :] + prods[b, at, :] * carry_in[layer, b, stream : stream + 1, :]
                states[layer, b, at, :] = full
                low1[at, :] = full.astype(BF16)
            acc[...] += dot_nn(low1[...], weights[layer, b, 3 * hid : 4 * hid, :])

        each_block(rear)

        def norm_two(at):
            values = resid[layer, at, :] + acc[at, :]
            middle[layer, at, :] = values
            scale = lax.rsqrt(jnp.mean(values * values, axis=-1, keepdims=True) + EPSILON)
            normed[layer, at, :] = (values * scale * gain_two).astype(BF16)

        each_tile(norm_two)
        acc[...] = middle[layer]

        def mlp(b):
            inner[layer, b] = dot_nt(normed[layer], weights[layer, b, 4 * hid : 4 * hid + ffn, :])

            def act(at):
                v = inner[layer, b, at, :]
                t = jnp.tanh(GELU_A * (v + GELU_B * (v * v * v)))
                wide_low1[at, :] = (0.5 * v * (1.0 + t)).astype(BF16)

            each_tile(act)
            acc[...] += dot_nn(wide_low1[...], weights[layer, b, 4 * hid + ffn : 4 * hid + 2 * ffn, :])

        each_block(mlp)
        resid[layer + 1] = acc[...]

    def put_grad(layer, b, first, count, value):
        gstage[b, pl.ds(first, count), :] = value.astype(BF16)

    def backward(layer):
        gain_one = gains[layer, 0:1, :]
        gain_two = gains[layer, 1:2, :]
        low_grad[...] = dgrad[...].astype(BF16)
        acc[...] = jnp.zeros_like(acc)

        def mlp(b):
            wide[...] = dot_nt(low_grad[...], weights[layer, b, 4 * hid + ffn : 4 * hid + 2 * ffn, :])

            def act(at):
                v = inner[layer, b, at, :]
                square = v * v
                t = jnp.tanh(GELU_A * (v + GELU_B * (v * square)))
                half = 0.5 * (1.0 + t)
                wide_low1[at, :] = (v * half).astype(BF16)
                slope = half + 0.5 * v * (1.0 - t * t) * (GELU_A * (1.0 + 3.0 * GELU_B * square))
                wide_low2[at, :] = (wide[at, :] * slope).astype(BF16)

            each_tile(act)
            put_grad(layer, b, 4 * hid + ffn, ffn, dot_tn(wide_low1[...], low_grad[...]))
            put_grad(layer, b, 4 * hid, ffn, dot_tn(wide_low2[...], normed[layer]))
            acc[...] += dot_nn(wide_low2[...], weights[layer, b, 4 * hid : 4 * hid + ffn, :])

        each_block(mlp)
        row_sum = jnp.zeros((1, width), F32)

        def norm_two(k, total):
            at = pl.ds(pl.multiple_of(k * tile, tile), tile)
            values, grad = middle[layer, at, :], acc[at, :]
            scale = lax.rsqrt(jnp.mean(values * values, axis=-1, keepdims=True) + EPSILON)
            unit = values * scale
            gunit = grad * gain_two
            full = dgrad[at, :] + scale * (gunit - unit * jnp.mean(gunit * unit, axis=-1, keepdims=True))
            dgrad[at, :] = full
            low_grad[at, :] = full.astype(BF16)
            return total + jnp.sum(grad * unit, axis=0, keepdims=True)

        ggains[layer, 1:2, :] = lax.fori_loop(0, tokens // tile, norm_two, row_sum)
        number = layers + layer

        def front(b):
            low1[...] = states[layer, b].astype(BF16)
            put_grad(layer, b, 3 * hid, hid, dot_tn(low1[...], low_grad[...]))
            gstates[b] = dot_nt(low_grad[...], weights[layer, b, 3 * hid : 4 * hid, :])

            def group(k, carried):
                new = []
                for stream in range(streams):
                    at = pl.ds(pl.multiple_of(stream * span + (groups - 1 - k) * 8, 8), 8)
                    f, i = fgate[layer, b, at, :], igate[layer, b, at, :]
                    decay = f * (1.0 / (f + i)) * widen(mask[at, :], hid)
                    term = decay * gstates[b, at, :]
                    for step in (1, 2, 4):
                        reach = row8 < 8 - step
                        term = term + decay * jnp.where(reach, pltpu.roll(term, 8 - step, 0), 0.0)
                        decay = decay * jnp.where(reach, pltpu.roll(decay, 8 - step, 0), 1.0)
                    prod_in, state_in = carried[stream]
                    term = term + decay * state_in
                    decay = decay * prod_in
                    deltas[b, at, :] = term
                    prods[b, at, :] = decay
                    new.append((decay[0:1], term[0:1]))
                return tuple(new)

            start = tuple((jnp.ones((1, hid), F32), jnp.zeros((1, hid), F32)) for _ in range(streams))
            last = lax.fori_loop(0, groups, group, start)
            for stream in range(streams):
                summary[number, b, stream : stream + 1, :] = last[stream][0]
                summary[number, b, 2 + stream : 3 + stream, :] = last[stream][1]

        each_block(front)
        incoming[:, 0:streams, :] = mail(number, False)
        acc[...] = jnp.zeros_like(acc)
        span_row = lax.broadcasted_iota(jnp.int32, (span, hid), 0)

        def rear(b):
            sum_f, sum_i = jnp.zeros((1, hid), F32), jnp.zeros((1, hid), F32)
            for stream in range(streams):
                at = slice(stream * span, (stream + 1) * span)
                late = incoming[b, stream : stream + 1, :]
                linked = deltas[b, at, :] + prods[b, at, :] * late
                linked = jnp.where(span_row == span - 1, late, pltpu.roll(linked, span - 1, 0))
                delta = gstates[b, at, :] + linked
                early = carry_in[layer, b, stream : stream + 1, :]
                before = jnp.where(span_row == 0, early, pltpu.roll(states[layer, b, at, :], 1, 0))
                f, i = fgate[layer, b, at, :], igate[layer, b, at, :]
                share = 1.0 / (f + i)
                fshare, ishare = f * share, i * share
                gap = delta * (before * widen(mask[at, :], hid) - cand[layer, b, at, :]) * fshare * ishare
                gf = (gap * (1.0 - f)).astype(BF16)
                gi = (gap * (i - 1.0)).astype(BF16)
                low1[at, :], low2[at, :], low3[at, :] = gf, gi, (delta * ishare).astype(BF16)
                sum_f = sum_f + jnp.sum(gf.astype(F32), axis=0, keepdims=True)
                sum_i = sum_i + jnp.sum(gi.astype(F32), axis=0, keepdims=True)
            gbiases[layer, b, 0:1, :] = sum_f
            gbiases[layer, b, 1:2, :] = sum_i
            total = acc[...]
            for member, low in enumerate((low1, low2, low3)):
                put_grad(layer, b, member * hid, hid, dot_tn(low[...], gated[layer]))
                total = total + dot_nn(low[...], weights[layer, b, member * hid : (member + 1) * hid, :])
            acc[...] = total

        each_block(rear)

        def norm_one(k, total):
            at = pl.ds(pl.multiple_of(k * tile, tile), tile)
            values, grad = resid[layer, at, :], acc[at, :]
            scale = lax.rsqrt(jnp.mean(values * values, axis=-1, keepdims=True) + EPSILON)
            unit = values * scale
            gunit = grad * gain_one
            full = dgrad[at, :] + scale * (gunit - unit * jnp.mean(gunit * unit, axis=-1, keepdims=True))
            dgrad[at, :] = full
            return total + jnp.sum(grad * unit, axis=0, keepdims=True)

        ggains[layer, 0:1, :] = lax.fori_loop(0, tokens // tile, norm_one, row_sum)

    def take_out(layer):
        return pltpu.make_async_copy(gstage, grads_ref.at[layer], out_sem.at[0])

    def back_step(k, _):
        layer = layers - 1 - k

        @pl.when(k > 0)
        def _():
            take_out(layer + 1).wait()

        backward(layer)
        take_out(layer).start()
        return 0

    lax.fori_loop(0, layers, lambda layer, _: forward(layer) or 0, 0)

    def turn(at):
        act_ref[at, :] = resid[layers, at, :].astype(BF16)
        dgrad[at, :] = out_grad_ref[at, :].astype(F32)

    each_tile(turn)
    lax.fori_loop(0, layers, back_step, 0)
    dx_ref[...] = dgrad[...]
    each_piece(write_piece)
    take_out(0).wait()


def run_network(geo, mats, stream_in, out_grad, doc_lengths, vectors):
    layers, _, rows, width = mats.shape
    streams, span, _ = stream_in.shape
    hid, ffn = H // geo.n_batch, FF // geo.n_batch
    sizes = (layers, streams, span, width, hid, ffn, rows, doc_lengths.shape[1])
    tokens = streams * span
    vmem = pl.BlockSpec(memory_space=pltpu.VMEM)
    return pl.pallas_call(
        functools.partial(network_kernel, geo, sizes),
        out_shape=(
            jax.ShapeDtypeStruct((tokens, width), BF16),
            jax.ShapeDtypeStruct((tokens, width), F32),
            jax.ShapeDtypeStruct((layers, geo.n_batch, 4 * hid + 2 * ffn, width), BF16),
            jax.ShapeDtypeStruct(vectors.shape, F32),
        ),
        in_specs=[vmem, vmem, vmem, pl.BlockSpec(memory_space=pltpu.SMEM), vmem],
        out_specs=(vmem, vmem, pl.BlockSpec(memory_space=pl.ANY), vmem),
        scratch_shapes=network_scratch(geo, sizes),
        compiler_params=pltpu.CompilerParams(
            collective_id=0, has_side_effects=True, vmem_limit_bytes=62 * 2**20
        ),
        name="network",
    )(mats, stream_in.reshape(tokens, width), out_grad.reshape(tokens, width), doc_lengths, vectors)


def update_scratch(geo, sizes):
    layers, rows, width, hid, ffn = sizes
    block = 4 * hid + 2 * ffn
    nz, nu, nv, nx, ny = geo.nz, geo.nu, geo.nv, geo.nx, geo.ny
    half, most = width // 2, max(ffn // rows - 1, 1)
    vec = 2 * width + 2 * hid * geo.n_batch

    def full(dtype, *shape):
        return pltpu.VMEM(shape, dtype)

    dma = pltpu.SemaphoreType.DMA
    return [
        full(BF16, layers, nz * nu * nv, rows, width),
        full(BF16, layers, nv - 1, nu * nz, rows, width),
        full(BF16, layers, nu - 1, nz, rows, width),
        full(BF16, layers, nz - 1, rows, width),
        full(F32, layers, rows, width),
        full(BF16, layers, rows, width),
        full(BF16, 3, 3, half, half),
        full(BF16, 1, 3, half, half),
        full(BF16, nx - 1, 3, half, half),
        full(BF16, most, 3, half, half),
        full(F32, 3, 8, 128),
        full(F32, 1, 8, 128),
        full(F32, nx - 1, 8, 128),
        full(F32, most, 8, 128),
        full(F32, 3, half, half),
        full(F32, width, width),
        full(F32, width, width),
        full(BF16, layers, 2, width, width),
        full(F32, layers, 8, 128),
        full(F32, 3, layers, vec),
        full(F32, 1, layers, vec),
        full(F32, nx, layers, vec),
        full(F32, geo.n_seq, layers, vec),
        dma((layers,)),
        dma((layers, nv - 1)),
        dma((layers, nu - 1)),
        dma((layers, nz - 1)),
        dma((layers, nz * nu * nv)),
        dma((layers, nv - 1, nu * nz)),
        dma((layers, nu - 1, nz)),
        dma((layers, nz - 1)),
        dma((layers, nz - 1)),
        dma((layers, ny - 1)),
        dma((layers, geo.n_seq)),
        dma((2,)),
        dma((2, nx - 1)),
        dma((2, most)),
        dma((2,)),
        dma((2, nx - 1)),
        dma((2, most)),
        dma((2,)),
        dma((2,)),
        dma((1,)),
        dma((nx,)),
        dma((geo.n_seq,)),
        dma((1,)),
        dma((nx,)),
        dma((geo.n_seq,)),
    ]


def update_kernel(
    geo, sizes, grads, old_ref, vpart_ref, vectors_ref, vmom_ref, vavg_ref,
    shard_ref, block_ref, ortho_ref, vgrad_ref, new_vmom_ref, new_vec_ref, new_vavg_ref, *scratch
):
    (
        in_s, in_v, in_u, in_z, moments, low_moments, gram_out, gram_s, gram_x, gram_g, square_out, square_s, square_x,
        square_g, gram, even, odd, polys, inverses, vec_out, vec_s, vec_x, vec_q, send_s, send_v, send_u, send_z,
        recv_s, recv_v, recv_u, recv_z, block_send_z, block_send_y, block_recv, gram_send_s, gram_send_x, gram_send_g,
        gram_recv_s, gram_recv_x, gram_recv_g, poly_send, poly_recv, vec_send_s, vec_send_x, vec_send_q, vec_recv_s,
        vec_recv_x, vec_recv_q,
    ) = scratch
    layers, rows, width, hid, ffn = sizes
    nz, nu, nv, nx, ny = geo.nz, geo.nu, geo.nv, geo.nx, geo.ny
    seq, batch, z, y, x, core = geo.here()
    if geo.swaps:
        u, v = y + core * (x - y), x + core * (y - x)
    else:
        u, v = y, x
    half, tile = width // 2, min(rows, 32)
    sibling = (seq, x * 2 + 1 - core)

    def remote(src, dst, send, recv, device):
        return pltpu.make_async_remote_copy(
            src_ref=src, dst_ref=dst, send_sem=send, recv_sem=recv, device_id=device, device_id_type=MESH
        )

    def each_tile(body):
        lax.fori_loop(0, rows // tile, lambda k, _: body(k * tile) or 0, 0)

    def count(first, last, body):
        lax.fori_loop(first, last, lambda k, _: body(k) or 0, 0)

    def offsets(k):
        return (k // (nu * nz) + 1) % nv, (k // nz + 1) % nu, (k + 1) % nz

    def place(k, side):
        dv, du, dz = offsets(k)
        if geo.swaps:
            u_side, v_side = y + side * (x - y), x + side * (y - x)
        else:
            u_side, v_side = y, x
        y_at, x_at = geo.to_yx(other(u_side, du, nu), other(v_side, dv, nv), side)
        start = pl.multiple_of(geo.seq_of(other(z, dz, nz), y_at) * rows, rows)
        return x_at * 2 + side, start

    def peer(dz, du, dv):
        y_at, x_at = geo.to_yx(other(u, du, nu), other(v, dv, nv), core)
        return (geo.seq_of(other(z, dz, nz), y_at), x_at * 2 + core)

    def slot(layer, k, side):
        b, start = place(k, side)
        return grads.at[layer, b, pl.ds(start, rows)]

    def swap_cores(layer):
        def one(k):
            remote(
                slot(layer, k, 1 - core), in_s.at[layer, k], send_s.at[layer], recv_s.at[layer, k], sibling
            ).start()

        count(0, nz * nu * nv, one)

    def wait_s(layer, k):
        remote(slot(layer, k, core), in_s.at[layer, k], send_s.at[layer], recv_s.at[layer, k], sibling).wait_recv()

    def wait_v(layer, j):
        for dv in range(1, nv):
            remote(
                in_v.at[layer, dv - 1, j], in_v.at[layer, dv - 1, j], send_v.at[layer, dv - 1],
                recv_v.at[layer, dv - 1, j], sibling,
            ).wait_recv()

    def wait_u(layer, i):
        for du in range(1, nu):
            remote(
                in_u.at[layer, du - 1, i], in_u.at[layer, du - 1, i], send_u.at[layer, du - 1],
                recv_u.at[layer, du - 1, i], sibling,
            ).wait_recv()

    def add_up(layer, k, extra):
        b, start = place(k, core)

        def one(first):
            at = pl.ds(pl.multiple_of(start + first, tile), tile)
            inner = pl.ds(pl.multiple_of(first, tile), tile)
            total = grads[layer, b, at, :].astype(F32) + in_s[layer, k, inner, :].astype(F32)
            for ref, index in extra:
                total = total + ref[(*index, inner, slice(None))].astype(F32)
            grads[layer, b, at, :] = total.astype(BF16)

        each_tile(one)

    def from_v(layer, j):
        return [(in_v, (layer, dv - 1, j)) for dv in range(1, nv)]

    def from_u(layer, i):
        return [(in_u, (layer, du - 1, i)) for du in range(1, nu)]

    def stage_v(layer):
        def one(k):
            wait_s(layer, k)
            add_up(layer, k, [])
            dv = k // (nu * nz) + 1
            j = k % (nu * nz)
            remote(
                slot(layer, k, core), in_v.at[layer, dv - 1, j], send_v.at[layer, dv - 1],
                recv_v.at[layer, dv - 1, j], peer(0, 0, dv),
            ).start()

        count(0, (nv - 1) * nu * nz, one)

    def stage_u(layer):
        def one(j):
            k = (nv - 1) * nu * nz + j
            wait_s(layer, k)
            wait_v(layer, j)
            add_up(layer, k, from_v(layer, j))
            du = j // nz + 1
            i = j % nz
            remote(
                slot(layer, k, core), in_u.at[layer, du - 1, i], send_u.at[layer, du - 1],
                recv_u.at[layer, du - 1, i], peer(0, du, 0),
            ).start()

        count(0, (nu - 1) * nz, one)

    def stage_z(layer):
        def one(i):
            j = (nu - 1) * nz + i
            k = (nv - 1) * nu * nz + j
            wait_s(layer, k)
            wait_v(layer, j)
            wait_u(layer, i)
            add_up(layer, k, from_v(layer, j) + from_u(layer, i))
            remote(
                slot(layer, k, core), in_z.at[layer, i], send_z.at[layer, i], recv_z.at[layer, i], peer(i + 1, 0, 0)
            ).start()

        count(0, nz - 1, one)

    def block_slot(layer, z_at, y_at):
        start = pl.multiple_of(geo.seq_of(z_at, y_at) * rows, rows)
        return block_ref.at[layer, pl.ds(start, rows)]

    def block_to_y(layer, z_at):
        part = block_slot(layer, z_at, y)
        for step in range(1, ny):
            remote(
                part, part, block_send_y.at[layer, step - 1], block_recv.at[layer, geo.seq_of(z_at, y)],
                (geo.seq_of(z, other(y, step, ny)), batch),
            ).start()

    def own_grad(layer):
        i = nz - 1
        j = (nu - 1) * nz + i
        k = (nv - 1) * nu * nz + j
        wait_s(layer, k)
        wait_v(layer, j)
        wait_u(layer, i)
        for dz in range(1, nz):
            remote(
                in_z.at[layer, dz - 1], in_z.at[layer, dz - 1], send_z.at[layer, dz - 1],
                recv_z.at[layer, dz - 1], sibling,
            ).wait_recv()
        b, start = place(k, core)
        extra = from_v(layer, j) + from_u(layer, i) + [(in_z, (layer, dz - 1)) for dz in range(1, nz)]

        def one(k_tile, squares):
            first = k_tile * tile
            at = pl.ds(pl.multiple_of(start + first, tile), tile)
            inner = pl.ds(pl.multiple_of(first, tile), tile)
            total = grads[layer, b, at, :].astype(F32) + in_s[layer, k, inner, :].astype(F32)
            for ref, index in extra:
                total = total + ref[(*index, inner, slice(None))].astype(F32)
            shard_ref[layer, inner, :] = total
            moment = MOMENTUM_DECAY * old_ref[layer, 0, inner, :] + total
            moments[layer, inner, :] = moment
            low = moment.astype(BF16)
            low_moments[layer, inner, :] = low
            block_ref[layer, at, :] = low
            return squares + jnp.sum(moment * moment, axis=0, keepdims=True)

        squares = lax.fori_loop(0, rows // tile, one, jnp.zeros((1, width), F32))
        part = block_slot(layer, z, y)
        for step in range(1, nz):
            remote(
                part, part, block_send_z.at[layer, step - 1], block_recv.at[layer, seq],
                (geo.seq_of(other(z, step, nz), y), batch),
            ).start()
        block_to_y(layer, z)
        return jnp.broadcast_to(jnp.sum(squares, axis=1, keepdims=True), (8, 128))

    def wait_block(layer, z_at, y_at):
        part = block_slot(layer, z_at, y_at)
        remote(
            part, part, block_send_z.at[layer, 0], block_recv.at[layer, geo.seq_of(z_at, y_at)], sibling
        ).wait_recv()

    def spread_block(layer):
        for step in range(1, nz):
            z_at = lax.rem(z - step + nz, nz)
            wait_block(layer, z_at, y)
            block_to_y(layer, z_at)

    def finish_block(layer):
        for step in range(0, nz):
            z_at = lax.rem(z - step + nz, nz)
            count(1, ny, lambda k: wait_block(layer, z_at, other(y, k, ny)))

    def vec_start():
        vec_out[0] = vpart_ref[...]
        remote(vec_out.at[0], vec_s.at[0], vec_send_s.at[0], vec_recv_s.at[0], sibling).start()

    def vec_second():
        remote(vec_out.at[0], vec_s.at[0], vec_send_s.at[0], vec_recv_s.at[0], sibling).wait_recv()
        total = vec_out[0] + vec_s[0]
        vec_out[1] = total
        vec_x[x] = total
        for step in range(1, nx):
            x_at = other(x, step, nx)
            remote(
                vec_out.at[1], vec_x.at[x], vec_send_x.at[x_at], vec_recv_x.at[x], (seq, x_at * 2 + core)
            ).start()

    def vec_third():
        for step in range(1, nx):
            x_at = other(x, step, nx)
            remote(
                vec_out.at[1], vec_x.at[x_at], vec_send_x.at[x_at], vec_recv_x.at[x_at], sibling
            ).wait_recv()
        total = vec_x[0]
        for k in range(1, nx):
            total = total + vec_x[k]
        vec_out[2] = total
        vec_q[seq] = total

        def one(k):
            to = other(seq, k, geo.n_seq)
            remote(vec_out.at[2], vec_q.at[seq], vec_send_q.at[to], vec_recv_q.at[seq], (to, batch)).start()

        count(1, geo.n_seq, one)

    def vec_last():
        def one(k):
            source = other(seq, k, geo.n_seq)
            remote(
                vec_out.at[2], vec_q.at[source], vec_send_q.at[source], vec_recv_q.at[source], sibling
            ).wait_recv()

        count(1, geo.n_seq, one)
        total = lax.fori_loop(1, geo.n_seq, lambda k, t: t + vec_q[k], vec_q[0])
        vgrad_ref[...] = total
        new_vmom_ref[...] = MOMENTUM_DECAY * vmom_ref[...] + total
        first = 0
        for member, length in enumerate((width, width, hid * geo.n_batch, hid * geo.n_batch)):
            at = slice(first, first + length)
            segment = new_vmom_ref[:, at]
            scale = lax.rsqrt(jnp.mean(segment * segment, axis=1, keepdims=True) + 1e-06)
            fresh = vectors_ref[:, at] - SEGMENT_RATES[member] * segment * scale
            new_vec_ref[:, at] = fresh
            new_vavg_ref[:, at] = AVERAGE_DECAY * vavg_ref[:, at] + (1.0 - AVERAGE_DECAY) * fresh
            first += length

    hid_devices, ffn_devices = hid // rows, ffn // rows
    in_group = jnp.where(seq < 4 * hid_devices, hid_devices, ffn_devices)
    rank = lax.rem(seq, in_group)
    group_first = seq - rank

    def pack_gram(stage, value):
        gram_out[stage, 0] = value[0:half, 0:half].astype(BF16)
        gram_out[stage, 1] = value[0:half, half:].astype(BF16)
        gram_out[stage, 2] = value[half:, half:].astype(BF16)

    def gram_pair(stage, into, squares_into, sends, recvs, device):
        return (
            remote(gram_out.at[stage], into, sends[0], recvs[0], device),
            remote(square_out.at[stage], squares_into, sends[1], recvs[1], device),
        )

    def gram_round(stage, parts, squares):
        for n in range(3):
            total = gram_out[stage, n].astype(F32)
            for ref in parts:
                total = total + ref[n].astype(F32)
            gram[n] = total
            gram_out[stage + 1, n] = total.astype(BF16)
        total = square_out[stage]
        for ref in squares:
            total = total + ref[...]
        square_out[stage + 1] = total

    def group_copies(k):
        here_at = lax.rem(rank - k - 1 + in_group, in_group)
        return gram_pair(
            2, gram_g.at[here_at], square_g.at[here_at],
            (gram_send_g.at[0, here_at], gram_send_g.at[1, here_at]),
            (gram_recv_g.at[0, here_at], gram_recv_g.at[1, here_at]), (group_first + k, batch),
        )

    def newton_schulz(squares):
        mine, theirs = core, 1 - core
        pack_gram(0, dot_tn(low_moments[theirs], low_moments[theirs]))
        square_out[0] = jnp.where(core == 0, squares[1], squares[0])
        to_core = gram_pair(
            0, gram_s.at[0], square_s.at[0], (gram_send_s.at[0], gram_send_s.at[1]),
            (gram_recv_s.at[0], gram_recv_s.at[1]), sibling,
        )
        for copy in to_core:
            copy.start()
        partial = dot_tn(low_moments[mine], low_moments[mine])
        for copy in to_core:
            copy.wait()
        pack_gram(0, partial)
        square_out[0] = jnp.where(core == 0, squares[0], squares[1])
        gram_round(0, [gram_s.at[0]], [square_s.at[0]])
        to_x = []
        for step in range(1, nx):
            to_x += gram_pair(
                1, gram_x.at[step - 1], square_x.at[step - 1],
                (gram_send_x.at[0, step - 1], gram_send_x.at[1, step - 1]),
                (gram_recv_x.at[0, step - 1], gram_recv_x.at[1, step - 1]),
                (seq, other(x, step, nx) * 2 + core),
            )
        for copy in to_x:
            copy.start()
        for copy in to_x:
            copy.wait()
        gram_round(1, [gram_x.at[k] for k in range(nx - 1)], [square_x.at[k] for k in range(nx - 1)])

        def to_member(k):
            for copy in group_copies(lax.rem(rank + k, in_group)):
                copy.start()

        def from_member(k):
            k = k - 1
            pltpu.make_async_remote_copy(
                src_ref=gram_out.at[2], dst_ref=gram_g.at[k], send_sem=gram_send_g.at[0, k],
                recv_sem=gram_recv_g.at[0, k], device_id=sibling, device_id_type=MESH,
            ).wait()
            pltpu.make_async_remote_copy(
                src_ref=square_out.at[2], dst_ref=square_g.at[k], send_sem=gram_send_g.at[1, k],
                recv_sem=gram_recv_g.at[1, k], device_id=sibling, device_id_type=MESH,
            ).wait()

        count(1, in_group, to_member)
        for n in range(3):
            gram[n] = gram_out[2, n].astype(F32)
        count(1, in_group, from_member)

        def add_member(k, total):
            for n in range(3):
                gram[n] += gram_g[k - 1, n].astype(F32)
            return total + square_g[k - 1]

        square = lax.fori_loop(1, in_group, add_member, square_out[2])
        inverse = 1.0 / (jnp.sqrt(square) + 1e-07)
        inverses[mine] = inverse
        scale = inverse[0:1, 0:1] * inverse[0:1, 0:1]
        even[0:half, 0:half] = gram[0] * scale
        even[0:half, half:] = gram[1] * scale
        even[half:, 0:half] = gram[1].T * scale
        even[half:, half:] = gram[2] * scale

        def polynomial(step):
            low = even[...].astype(BF16)
            value = QUINTIC[1] * even[...] + QUINTIC[2] * dot_nn(low, low)
            polys[mine, step] = value.astype(BF16)

        polynomial(0)
        lead = QUINTIC[0]
        high = even[...].astype(BF16)
        rest = (even[...] - high.astype(F32)).astype(BF16)
        poly = polys[mine, 0]
        odd[...] = dot_nn(poly, high) + dot_nn(poly, rest)
        high = odd[...].astype(BF16)
        rest = (odd[...] - high.astype(F32)).astype(BF16)
        even[...] = (
            lead * lead * even[...] + 2.0 * lead * odd[...] + (dot_nn(poly, high) + dot_nn(poly, rest))
        )
        polynomial(1)
        give = (
            remote(polys.at[mine], polys.at[mine], poly_send.at[0], poly_recv.at[0], sibling),
            remote(inverses.at[mine], inverses.at[mine], poly_send.at[1], poly_recv.at[1], sibling),
        )
        for copy in give:
            copy.start()

        def apply(layer):
            begin = (moments[layer] * inverses[layer, 0:1, 0:1]).astype(BF16)
            for step in range(NS_STEPS):
                begin = (lead * begin.astype(F32) + dot_nn(begin, polys[layer, step])).astype(BF16)
            ortho_ref[layer] = begin

        apply(mine)
        for copy in give:
            copy.wait_send()
        remote(polys.at[theirs], polys.at[theirs], poly_send.at[0], poly_recv.at[0], sibling).wait_recv()
        remote(inverses.at[theirs], inverses.at[theirs], poly_send.at[1], poly_recv.at[1], sibling).wait_recv()
        apply(theirs)

    enter(geo)
    vec_start()
    order = list(reversed(range(layers)))
    for layer in order:
        swap_cores(layer)
    squares = [None] * layers
    vec_step = [vec_second, vec_third, vec_last]
    for layer in order:
        stage_v(layer)
        if vec_step:
            vec_step.pop(0)()
        stage_u(layer)
        stage_z(layer)
        if vec_step:
            vec_step.pop(0)()
        squares[layer] = own_grad(layer)
    for layer in order:
        spread_block(layer)
    newton_schulz(squares)
    for layer in order:
        finish_block(layer)

    def drain(part, sem):
        pltpu.make_async_remote_copy(
            src_ref=part, dst_ref=part, send_sem=sem, recv_sem=vec_recv_s.at[0], device_id=sibling,
            device_id_type=MESH,
        ).wait_send()

    for layer in range(layers):
        drain(grads.at[layer, pl.ds(0, nx)], send_s.at[layer])
        for dv in range(1, nv):
            drain(grads.at[layer, 0], send_v.at[layer, dv - 1])
        for du in range(1, nu):
            drain(grads.at[layer, 0, pl.ds(0, nz * rows)], send_u.at[layer, du - 1])
        for dz in range(1, nz):
            drain(in_z.at[layer, 0], send_z.at[layer, dz - 1])
            drain(in_z.at[layer, 0], block_send_z.at[layer, dz - 1])
        for dy in range(1, ny):
            drain(block_ref.at[layer, pl.ds(0, nz * rows)], block_send_y.at[layer, dy - 1])
    drain(vec_out.at[0], vec_send_s.at[0])
    for step in range(1, nx):
        drain(vec_out.at[1], vec_send_x.at[other(x, step, nx)])
    count(1, geo.n_seq, lambda k: drain(vec_out.at[2], vec_send_q.at[other(seq, k, geo.n_seq)]))


def run_update(geo, grads, mat_momenta, vec_part, vectors, vec_momenta, vec_averages):
    layers, _, block, width = grads.shape
    rows = mat_momenta.shape[2]
    sizes = (layers, rows, width, H // geo.n_batch, FF // geo.n_batch)
    vmem = pl.BlockSpec(memory_space=pltpu.VMEM)
    vec = jax.ShapeDtypeStruct(vectors.shape, F32)
    return pl.pallas_call(
        functools.partial(update_kernel, geo, sizes),
        out_shape=(
            jax.ShapeDtypeStruct((layers, rows, width), F32),
            jax.ShapeDtypeStruct((layers, block, width), BF16),
            jax.ShapeDtypeStruct((layers, rows, width), BF16),
            vec, vec, vec, vec,
        ),
        in_specs=[vmem] * 6,
        out_specs=(vmem,) * 7,
        scratch_shapes=update_scratch(geo, sizes),
        compiler_params=pltpu.CompilerParams(
            collective_id=1, has_side_effects=True, vmem_limit_bytes=60 * 2**20
        ),
        name="update",
    )(grads, mat_momenta, vec_part, vectors, vec_momenta, vec_averages)


def per_device(
    geo, stream_in, out_grad, doc_lengths, mats, mat_momenta, mat_averages, vectors, vec_momenta, vec_averages
):
    layers, _, rows, width = mats.shape
    activations, grad_resid, grads, vec_part = run_network(geo, mats, stream_in, out_grad, doc_lengths, vectors)
    shard, block, ortho, vec_grads, new_vec_momenta, new_vectors, new_vec_averages = run_update(
        geo, grads, mat_momenta, vec_part, vectors, vec_momenta, vec_averages
    )
    small = lax.axis_index("seq") * rows < 4 * (H // geo.n_batch)
    factor = jnp.where(small, 0.2 * math.sqrt(max(H, width)), 0.2 * math.sqrt(max(FF, width)))
    new_mats = mats - MATRIX_RATE * (ortho.astype(F32) * factor).reshape(mats.shape)
    new_averages = AVERAGE_DECAY * mat_averages + (1.0 - AVERAGE_DECAY) * new_mats
    return (
        activations.reshape(stream_in.shape),
        grad_resid.reshape(stream_in.shape),
        shard.reshape(mats.shape),
        block.astype(F32).reshape(layers, 1, *block.shape[1:]),
        new_mats,
        new_averages,
        vec_grads,
        new_vec_momenta,
        new_vectors,
        new_vec_averages,
    )


def solution(mesh):
    geo = Geometry(mesh.shape["seq"], mesh.shape["batch"])
    rows = P(None, "batch", "seq", None)
    tokens = P("batch", "seq", None)
    return jax.shard_map(
        functools.partial(per_device, geo),
        mesh=mesh,
        in_specs=(tokens, tokens, P("batch", None), rows, rows, rows, P(), P(), P()),
        out_specs=(tokens, tokens, rows, P(None, "batch", None, None), rows, rows, P(), P(), P(), P()),
        check_vma=False,
    )
```

```python
import functools
import math

import jax
import jax.numpy as jnp
from jax import lax
from jax.experimental import pallas as pl
from jax.experimental.pallas import tpu as pltpu
from jax.sharding import PartitionSpec as P

H = 1024
FF = 2048
NS_STEPS = 2
MESH = pl.DeviceIdType.MESH
F32 = jnp.float32
BF16 = jnp.bfloat16

EPSILON = 1e-05
MOMENTUM_DECAY = 0.5
AVERAGE_DECAY = 0.9
MATRIX_RATE = 0.3
SEGMENT_RATES = (0.3, 0.3, 0.5, 2.0)
QUINTIC = (3.4445, -4.775, 2.0315)
GELU_A = 0.7978845608
GELU_B = 0.044715


class Geometry:
    def __init__(self, n_seq, n_batch):
        self.n_seq, self.n_batch = n_seq, n_batch
        self.nz, self.ny, self.stride_z, self.stride_y = {
            8: (4, 2, 2, 1),
            32: (8, 4, 1, 8),
        }.get(n_seq, (n_seq, 1, 1, n_seq))
        self.nx = n_batch // 2
        self.swaps = self.ny == self.nx
        self.nu, self.nv = self.ny, self.nx

    def seq_of(self, z, y):
        return z * self.stride_z + y * self.stride_y

    def here(self):
        seq, batch = lax.axis_index("seq"), lax.axis_index("batch")
        z = seq // self.stride_z % self.nz
        y = seq // self.stride_y % self.ny
        return seq, batch, z, y, batch // 2, batch % 2

    def to_yx(self, u, v, core):
        if not self.swaps:
            return u, v
        return u + core * (v - u), v + core * (u - v)


def dot_nn(a, b):
    return lax.dot_general(a, b, (((1,), (0,)), ((), ())), preferred_element_type=F32)


def dot_nt(a, b):
    return lax.dot_general(a, b, (((1,), (1,)), ((), ())), preferred_element_type=F32)


def dot_tn(a, b):
    return lax.dot_general(a, b, (((0,), (0,)), ((), ())), preferred_element_type=F32)


def other(mine, step, count):
    return lax.rem(mine + step, count)


def sigmoid(values):
    return 1.0 / (1.0 + jnp.exp(-values))


def widen(column_tile, width):
    return jnp.concatenate([column_tile] * (width // 128), axis=1)


def count(first, last, body):
    lax.fori_loop(first, last, lambda k, _: body(k) or 0, 0)


def remote(src, dst, send, recv, device):
    return pltpu.make_async_remote_copy(
        src_ref=src, dst_ref=dst, send_sem=send, recv_sem=recv, device_id=device, device_id_type=MESH
    )


class Gather:
    def __init__(self, geo, weights, rows, refs):
        self.geo, self.weights, self.rows, self.half_rows = geo, weights, rows, rows // 2
        self.send_z, self.send_u, self.send_v, self.send_s = refs.send_z, refs.send_u, refs.send_v, refs.send_s
        self.recv, self.recv_s = refs.recv, refs.recv_s
        self.seq, self.batch, self.z, self.y, self.x, self.core = geo.here()
        if geo.swaps:
            self.u = self.y + self.core * (self.x - self.y)
            self.v = self.x + self.core * (self.y - self.x)
        else:
            self.u, self.v = self.y, self.x
        self.sibling = (self.seq, self.x * 2 + 1 - self.core)

    def part(self, layer, half, z, u, v):
        y, x = self.geo.to_yx(u, v, self.core)
        start = self.geo.seq_of(z, y) * self.rows + half * self.half_rows
        return self.weights.at[layer, x * 2 + self.core, pl.ds(pl.multiple_of(start, self.half_rows), self.half_rows)]

    def arrival(self, layer, half, z, u, v):
        geo = self.geo
        return self.recv.at[(((layer * 2 + half) * geo.nz + z) * geo.nu + u) * geo.nv + v]

    def device(self, z, u, v):
        y, x = self.geo.to_yx(u, v, self.core)
        return (self.geo.seq_of(z, y), x * 2 + self.core)

    def push(self, layer, half, z, u, device, send):
        part = self.part(layer, half, z, u, self.v)
        remote(part, part, send, self.arrival(layer, half, z, u, self.v), device).start()

    def arrived(self, layer, half, z, u, v):
        part = self.part(layer, half, z, u, v)
        remote(part, part, self.send_s.at[layer], self.arrival(layer, half, z, u, v), self.sibling).wait_recv()

    def along_z(self, layer, half, z, u, go):
        for way, passes, to in (
            (0, jnp.logical_and(z <= self.z, self.z + 1 < self.geo.nz), self.z + 1),
            (1, jnp.logical_and(z >= self.z, self.z >= 1), self.z - 1),
        ):
            sem = self.send_z.at[layer, (half * 2 + way) * self.geo.nz + z, u]

            @pl.when(passes)
            def _():
                go(to, sem)

    def to_z(self, layer, half, z, u):
        self.along_z(
            layer, half, z, u,
            lambda to, sem: self.push(layer, half, z, u, self.device(to, self.u, self.v), sem),
        )

    def to_u(self, layer, half, z):
        for step in range(1, self.geo.nu):
            self.push(
                layer, half, z, self.u, self.device(self.z, other(self.u, step, self.geo.nu), self.v),
                self.send_u.at[layer, half, step - 1],
            )

    def to_v(self, layer, half, z, u):
        for step in range(1, self.geo.nv):
            self.push(
                layer, half, z, u, self.device(self.z, self.u, other(self.v, step, self.geo.nv)),
                self.send_v.at[layer, step - 1],
            )

    def to_sibling(self, layer, half, z, u, v):
        part = self.part(layer, half, z, u, v)
        remote(part, part, self.send_s.at[layer], self.recv_s.at[layer], self.sibling).start()

    def begin(self, layer):
        for half in range(2):
            self.to_z(layer, half, self.z, self.u)
            self.to_u(layer, half, self.z)
            self.to_v(layer, half, self.z, self.u)
            self.to_sibling(layer, half, self.z, self.u, self.v)

        def one(k):
            u = other(self.u, k, self.geo.nu)
            self.arrived(layer, 1, self.z, u, self.v)
            self.to_z(layer, 1, self.z, u)
            self.to_v(layer, 1, self.z, u)
            self.to_sibling(layer, 1, self.z, u, self.v)

        count(1, self.geo.nu, one)

    def at_distance(self, distance, body):
        if distance == 0:
            body(self.z)
            return

        @pl.when(self.z >= distance)
        def _():
            body(self.z - distance)

        @pl.when(self.z + distance < self.geo.nz)
        def _():
            body(self.z + distance)

    def from_z(self, layer, z):
        self.arrived(layer, 0, z, self.u, self.v)
        self.to_z(layer, 0, z, self.u)
        self.to_u(layer, 0, z)
        self.to_v(layer, 0, z, self.u)
        self.to_sibling(layer, 0, z, self.u, self.v)

        def one(k):
            u = other(self.u, k, self.geo.nu)
            self.arrived(layer, 1, z, u, self.v)
            self.to_z(layer, 1, z, u)
            self.to_v(layer, 1, z, u)
            self.to_sibling(layer, 1, z, u, self.v)

        count(0, self.geo.nu, one)

    def from_u(self, layer, z):
        def one(k):
            u = other(self.u, k, self.geo.nu)
            self.arrived(layer, 0, z, u, self.v)
            self.to_v(layer, 0, z, u)
            self.to_sibling(layer, 0, z, u, self.v)

        count(1, self.geo.nu, one)

    def from_v(self, layer, z):
        def one(k):
            half = k % 2
            u = other(self.u, k // 2 // (self.geo.nv - 1), self.geo.nu)
            v = other(self.v, k // 2 % (self.geo.nv - 1) + 1, self.geo.nv)
            self.arrived(layer, half, z, u, v)
            self.to_sibling(layer, half, z, u, v)

        count(0, 2 * self.geo.nu * (self.geo.nv - 1), one)

    def step(self, layer, t):
        nz = self.geo.nz
        if t == 0:
            self.begin(layer)
        if 1 <= t < nz:
            self.at_distance(t, lambda z: self.from_z(layer, z))
        if 1 <= t <= nz:
            self.at_distance(t - 1, lambda z: self.from_u(layer, z))
        if 2 <= t <= nz + 1:
            self.at_distance(t - 2, lambda z: self.from_v(layer, z))

    def steps(self, layers):
        last = self.geo.nz + 1
        order = []
        for layer in range(layers):
            order += [(layer, t) for t in range(0 if layer == 0 else 1, last)]
            if layer + 1 < layers:
                order.append((layer + 1, 0))
            order.append((layer, last))
        return order

    def ready(self, layer):
        part = self.weights.at[layer, pl.ds(0, self.geo.nx)]
        remote(part, part, self.send_s.at[layer], self.recv_s.at[layer], self.sibling).wait_recv()

    def finish(self, layer):
        geo = self.geo

        def drain(part, sem):
            remote(part, part, sem, self.recv_s.at[layer], self.sibling).wait_send()

        one = self.part(layer, 0, self.z, self.u, self.v)
        for z in range(geo.nz):
            self.along_z(layer, 0, z, self.u, lambda to, sem: drain(one, sem))
            for u in range(geo.nu):
                self.along_z(layer, 1, z, u, lambda to, sem: drain(one, sem))
        for step in range(1, geo.nu):
            drain(self.weights.at[layer, 0, pl.ds(0, geo.nz * self.half_rows)], self.send_u.at[layer, 0, step - 1])
            drain(one, self.send_u.at[layer, 1, step - 1])
        for step in range(1, geo.nv):
            drain(self.weights.at[layer, 0, pl.ds(0, geo.nz * geo.nu * self.rows)], self.send_v.at[layer, step - 1])
        drain(self.weights.at[layer, pl.ds(0, geo.nx)], self.send_s.at[layer])


class Scratch:
    def __init__(self):
        self.names, self.shapes = [], []

    def add(self, name, kind, *shape):
        self.names.append(name)
        self.shapes.append(pltpu.SemaphoreType.DMA(shape) if kind is None else pltpu.VMEM(shape, kind))

    def bind(self, refs):
        return dict(zip(self.names, refs, strict=True))


class Sizes:
    def __init__(self, geo, layers, streams, span, width, rows, docs):
        self.layers, self.streams, self.span, self.width = layers, streams, span, width
        self.rows, self.docs = rows, docs
        self.tokens = streams * span
        self.hid, self.ffn = H // geo.n_batch, FF // geo.n_batch
        self.block = 4 * self.hid + 2 * self.ffn
        self.vec = 2 * width + 2 * H


def make_scratch(geo, sz):
    layers, tokens, width, rows, hid, ffn = sz.layers, sz.tokens, sz.width, sz.rows, sz.hid, sz.ffn
    nb, nx, ny, nz, n_seq = geo.n_batch, geo.nx, geo.ny, geo.nz, geo.n_seq
    half, most = width // 2, max(ffn // rows - 1, 1)
    s = Scratch()
    add = s.add
    add("weights", BF16, layers, nb, sz.block, width)
    add("resid", F32, layers + 1, tokens, width)
    for name in ("fgate", "igate", "cand", "states"):
        add(name, F32, layers, nb, tokens, hid)
    add("slope", F32, layers, nb, tokens, ffn)
    add("middle", F32, layers, tokens, width)
    add("gated", BF16, layers, 2 * tokens, width)
    add("normed", BF16, layers, 2 * tokens, width)
    add("states_low", BF16, layers, nx, 2 * tokens, hid)
    add("active", BF16, layers, nx, 2 * tokens, ffn)
    add("ginner", BF16, nx, 2 * tokens, ffn)
    add("gmlp", BF16, 2 * tokens, width)
    add("gy", BF16, 2 * tokens, width)
    add("ggate", BF16, 3, nx, 2 * tokens, hid)
    add("states_out", BF16, nx, tokens, hid)
    add("active_out", BF16, nx, tokens, ffn)
    add("ginner_out", BF16, nx, tokens, ffn)
    add("ggate_out", BF16, 3, nx, tokens, hid)
    add("carry_in", F32, layers, nb, sz.streams, hid)
    add("incoming", F32, nb, sz.streams, hid)
    for name in ("prods", "gstates", "deltas"):
        add(name, F32, nb, tokens, hid)
    add("mask", F32, tokens, 128)
    add("summary", F32, 2 * layers, nb, 2 * sz.streams, hid)
    add("mailbox", F32, 2 * layers, n_seq, nb, 2 * sz.streams, hid)
    add("dgrad", F32, tokens, width)
    add("acc", F32, tokens, width)
    add("wide", F32, tokens, ffn)
    add("gains", F32, layers, 2, width)
    add("biases", F32, layers, nb, 2, hid)
    add("ggains", F32, layers, 2, width)
    add("gbiases", F32, layers, nb, 2, hid)
    add("landing", BF16, nx, sz.block, width)
    add("low_moments", BF16, layers, rows, width)
    add("gram_out", BF16, 3, 3, half, half)
    add("gram_s", BF16, 1, 3, half, half)
    add("gram_x", BF16, nx - 1, 3, half, half)
    add("gram_g", BF16, most, 3, half, half)
    add("square_own", F32, layers, 8, 128)
    add("square_out", F32, 3, 8, 128)
    add("square_s", F32, 1, 8, 128)
    add("square_x", F32, nx - 1, 8, 128)
    add("square_g", F32, most, 8, 128)
    add("odd", F32, width, width)
    add("polys", BF16, layers, 2, width, width)
    add("inverses", F32, layers, 8, 128)
    add("vec_out", F32, 3, layers, sz.vec)
    add("vec_s", F32, 1, layers, sz.vec)
    add("vec_x", F32, nx, layers, sz.vec)
    add("vec_q", F32, n_seq, layers, sz.vec)
    for name, shape in (
        ("load", (4,)),
        ("send_z", (layers, 4 * nz, geo.nu)),
        ("send_u", (layers, 2, geo.nu - 1)),
        ("send_v", (layers, geo.nv - 1)),
        ("send_s", (layers,)),
        ("recv", (layers * 2 * nz * geo.nu * geo.nv,)),
        ("recv_s", (layers,)),
        ("mail_send", (2 * layers, n_seq)),
        ("mail_recv", (2 * layers, n_seq)),
        ("gated_send", (layers,)),
        ("gated_recv", (layers,)),
        ("normed_send", (layers,)),
        ("normed_recv", (layers,)),
        ("states_send", (nx,)),
        ("states_recv", (layers, nx)),
        ("active_send", (nx,)),
        ("active_recv", (layers, nx)),
        ("gmlp_send", (1,)),
        ("gmlp_recv", (1,)),
        ("gy_send", (1,)),
        ("gy_recv", (1,)),
        ("ginner_send", (nx,)),
        ("ginner_recv", (nx,)),
        ("ggate_send", (3, nx)),
        ("ggate_recv", (3, nx)),
        ("sum_send_x", (layers, nx - 1, n_seq)),
        ("sum_send_y", (layers, ny - 1)),
        ("sum_send_z", (layers, nz - 1)),
        ("sum_recv_x", (layers, nx - 1, n_seq)),
        ("sum_recv_y", (layers, ny - 1, nz)),
        ("sum_recv_z", (layers, nz - 1)),
        ("block_send_z", (layers, nz, 2)),
        ("block_send_y", (layers, ny - 1)),
        ("block_recv", (layers, n_seq)),
        ("block_own", (layers,)),
        ("gram_send_s", (2,)),
        ("gram_send_x", (2, nx - 1)),
        ("gram_send_g", (2, most)),
        ("gram_recv_s", (2,)),
        ("gram_recv_x", (2, nx - 1)),
        ("gram_recv_g", (2, most)),
        ("poly_send", (2,)),
        ("poly_recv", (2,)),
        ("vec_send_s", (1,)),
        ("vec_send_x", (nx,)),
        ("vec_send_q", (n_seq,)),
        ("vec_recv_s", (1,)),
        ("vec_recv_x", (nx,)),
        ("vec_recv_q", (n_seq,)),
        ("store", (4,)),
    ):
        add(name, None, *shape)
    for name in ("credit_mlp", "credit_gate", "credit_x", "credit_y", "credit_z"):
        s.names.append(name)
        s.shapes.append(pltpu.SemaphoreType.REGULAR)
    return s

WINDOW = 3
DELAYS = (3, 6, 12)


def step_kernel(
    geo, sz, names, mats_ref, old_ref, x_ref, out_grad_ref, doc_ref, vec_ref, vmom_ref, vavg_ref,
    act_ref, dx_ref, shard_ref, block_ref, ortho_ref, vgrad_ref, new_vmom_ref, new_vec_ref, new_vavg_ref, *scratch
):
    r = type("Refs", (), names.bind(scratch))
    layers, streams, span, width, rows = sz.layers, sz.streams, sz.span, sz.width, sz.rows
    tokens, hid, ffn = sz.tokens, sz.hid, sz.ffn
    nb, nx, ny, nz, n_seq = geo.n_batch, geo.nx, geo.ny, geo.nz, geo.n_seq
    seq, batch, z, y, x, core = geo.here()
    sibling = (seq, x * 2 + 1 - core)
    tile, half, groups = 32, width // 2, span // 8
    weights = r.weights
    at_out, at_up, at_down = 3 * hid, 4 * hid, 4 * hid + ffn
    own_part, far_part = slice(0, tokens), slice(tokens, 2 * tokens)

    def rows_at(k, size):
        return pl.ds(pl.multiple_of(k * size, size), size)

    def each_tile(body):
        count(0, tokens // tile, lambda k: body(rows_at(k, tile)))

    barrier = pltpu.get_barrier_semaphore()

    def greet(seq_id, batch_id):
        pl.semaphore_signal(barrier, inc=1, device_id=(seq_id, batch_id), device_id_type=MESH)

    for step in range(1, n_seq):
        greet(other(seq, step, n_seq), batch)
    for step in range(1, nx):
        greet(seq, other(x, step, nx) * 2 + core)
    greet(*sibling)
    for layer in range(layers):
        pltpu.make_async_copy(
            mats_ref.at[layer, 0], r.resid.at[layer, pl.ds(0, rows)], r.load.at[layer]
        ).start()
    for layer in range(layers):
        pltpu.make_async_copy(
            mats_ref.at[layer, 0], r.resid.at[layer, pl.ds(0, rows)], r.load.at[layer]
        ).wait()
        weights[layer, batch, rows_at(seq, rows), :] = r.resid[layer, 0:rows, :].astype(BF16)
    pl.semaphore_wait(barrier, n_seq - 1 + nx - 1 + 1)

    gather = Gather(geo, weights, rows, r)
    gather_steps = gather.steps(layers)

    def advance(steps):
        for _ in range(min(steps, len(gather_steps))):
            gather.step(*gather_steps.pop(0))

    def need(layer):
        while any(step[0] == layer for step in gather_steps):
            advance(1)
        gather.ready(layer)

    advance(1)

    def each_piece(body):
        for layer in range(layers):
            for k in range(2):
                body(slice(layer, layer + 1), slice(k * width, (k + 1) * width), k, r.gains, r.ggains, (layer,))
                for b in range(nb):
                    first = 2 * width + k * H + b * hid
                    body(slice(layer, layer + 1), slice(first, first + hid), k, r.biases, r.gbiases, (layer, b))

    def read_piece(row, columns, k, kept, made, at):
        kept[(*at, slice(k, k + 1), slice(None))] = vec_ref[row, columns]

    def write_piece(row, columns, k, kept, made, at):
        r.vec_out[0, row, columns] = made[(*at, slice(k, k + 1), slice(None))]

    each_piece(read_piece)
    for stream in range(streams):
        position = seq * span + lax.broadcasted_iota(jnp.int32, (span, 128), 0)
        begin, keep = jnp.int32(0), jnp.ones((span, 128), F32)
        for doc in range(sz.docs):
            keep = jnp.where(position == begin, 0.0, keep)
            begin = begin + doc_ref[stream, doc]
        r.mask[stream * span : (stream + 1) * span, :] = keep

    def load_input(at):
        r.resid[0, at, :] = x_ref[at, :].astype(F32)

    each_tile(load_input)

    def give(src, dst, send, recv):
        remote(src, dst, send, recv, sibling).start()

    def given(dst, recv):
        remote(dst, dst, r.gmlp_send.at[0], recv, sibling).wait_recv()

    def gone(src, send):
        remote(src, src, send, r.gmlp_recv.at[0], sibling).wait_send()

    def blocks(k):
        f = other(x, k + 1, nx)
        return f, 2 * f + core, 2 * f + 1 - core

    def mail(number, forward):
        first, last = (seq + 1, n_seq) if forward else (0, seq)

        def copy(peer, source):
            return remote(
                r.summary.at[number], r.mailbox.at[number, source], r.mail_send.at[number, peer],
                r.mail_recv.at[number, source], (peer, batch),
            )

        hops = seq if forward else n_seq - 1 - seq

        def fold(k, before):
            source = k if forward else n_seq - 1 - k
            copy(source, source).wait_recv()
            packed = r.mailbox[number, source]
            return packed[:, streams:] + packed[:, 0:streams] * before

        def post():
            count(first, last, lambda peer: copy(peer, seq).start())

        def collect():
            total = lax.fori_loop(0, hops, fold, jnp.zeros((nb, streams, hid), F32))
            count(first, last, lambda peer: copy(peer, seq).wait_send())
            return total

        return post, collect

    row8 = lax.broadcasted_iota(jnp.int32, (8, hid), 0)
    start_scan = tuple((jnp.ones((1, hid), F32), jnp.zeros((1, hid), F32)) for _ in range(streams))

    def put_summary(number, b, last):
        for stream in range(streams):
            r.summary[number, b, stream : stream + 1, :] = last[stream][0]
            r.summary[number, b, streams + stream : streams + stream + 1, :] = last[stream][1]

    def forward(layer, pumps):
        gain_one, gain_two = r.gains[layer, 0:1, :], r.gains[layer, 1:2, :]

        def norm_one(at):
            values = r.resid[layer, at, :]
            scale = lax.rsqrt(jnp.mean(values * values, axis=-1, keepdims=True) + EPSILON)
            r.gated[layer, at, :] = (values * scale * gain_one).astype(BF16)

        each_tile(norm_one)
        near = r.gated.at[layer, own_part]
        give(near, r.gated.at[layer, far_part], r.gated_send.at[layer], r.gated_recv.at[layer])
        need(layer)

        def front(b):
            source = r.gated[layer, own_part, :]
            r.wide[:, 0:hid] = dot_nt(source, weights[layer, b, 0:hid, :]) + r.biases[layer, b, 0:1, :]
            r.wide[:, hid : 2 * hid] = dot_nt(source, weights[layer, b, hid : 2 * hid, :]) + r.biases[layer, b, 1:2, :]
            r.cand[layer, b] = dot_nt(source, weights[layer, b, 2 * hid : at_out, :])

            def group(k, carried):
                new = []
                for stream in range(streams):
                    at = pl.ds(pl.multiple_of(stream * span + k * 8, 8), 8)
                    f, i = sigmoid(r.wide[at, 0:hid]), sigmoid(r.wide[at, hid : 2 * hid])
                    share = 1.0 / (f + i)
                    decay = f * share * widen(r.mask[at, :], hid)
                    term = i * share * r.cand[layer, b, at, :]
                    r.fgate[layer, b, at, :] = f
                    r.igate[layer, b, at, :] = i
                    for step in (1, 2, 4):
                        reach = row8 >= step
                        term = term + decay * jnp.where(reach, pltpu.roll(term, step, 0), 0.0)
                        decay = decay * jnp.where(reach, pltpu.roll(decay, step, 0), 1.0)
                    prod_in, state_in = carried[stream]
                    term = term + decay * state_in
                    decay = decay * prod_in
                    r.states[layer, b, at, :] = term
                    r.prods[b, at, :] = decay
                    new.append((decay[7:8], term[7:8]))
                return tuple(new)

            put_summary(layer, b, lax.fori_loop(0, groups, group, start_scan))

        count(0, nb // 2, front)
        pumps[0]()
        count(nb // 2, nb, front)
        post, collect = mail(layer, True)
        post()
        pumps[1]()
        r.carry_in[layer] = collect()
        r.acc[...] = jnp.zeros_like(r.acc)

        def rear(k):
            f, b_own, b_far = blocks(k)

            def states_of(b, put):
                for stream in range(streams):
                    at = slice(stream * span, (stream + 1) * span)
                    full = r.states[layer, b, at, :] + r.prods[b, at, :] * r.carry_in[layer, b, stream : stream + 1, :]
                    r.states[layer, b, at, :] = full
                    put(at, full.astype(BF16))

            def put_far(at, low):
                r.states_out[f, at, :] = low

            def put_own(at, low):
                r.states_low[layer, f, at, :] = low

            states_of(b_far, put_far)
            give(
                r.states_out.at[f], r.states_low.at[layer, f, far_part], r.states_send.at[f],
                r.states_recv.at[layer, f],
            )
            states_of(b_own, put_own)
            r.acc[...] += dot_nn(r.states_out[f], weights[layer, b_far, at_out:at_up, :]) + dot_nn(
                r.states_low[layer, f, own_part, :], weights[layer, b_own, at_out:at_up, :]
            )

        count(0, nx, rear)
        pumps[2]()

        def norm_two(at):
            values = r.resid[layer, at, :] + r.acc[at, :]
            r.middle[layer, at, :] = values
            scale = lax.rsqrt(jnp.mean(values * values, axis=-1, keepdims=True) + EPSILON)
            r.normed[layer, at, :] = (values * scale * gain_two).astype(BF16)

        each_tile(norm_two)
        near = r.normed.at[layer, own_part]
        give(near, r.normed.at[layer, far_part], r.normed_send.at[layer], r.normed_recv.at[layer])
        r.acc[...] = r.middle[layer]

        def mlp(k):
            f, b_own, b_far = blocks(k)

            def active_of(b, put):
                r.wide[...] = dot_nt(r.normed[layer, own_part, :], weights[layer, b, at_up:at_down, :])

                def act(at):
                    v = r.wide[at, :]
                    square = v * v
                    t = jnp.tanh(GELU_A * (v + GELU_B * (v * square)))
                    share = 0.5 * (1.0 + t)
                    put(at, (v * share).astype(BF16))
                    r.slope[layer, b, at, :] = share + 0.5 * v * (1.0 - t * t) * (
                        GELU_A * (1.0 + 3.0 * GELU_B * square)
                    )

                each_tile(act)

            def put_far(at, low):
                r.active_out[f, at, :] = low

            def put_own(at, low):
                r.active[layer, f, at, :] = low

            active_of(b_far, put_far)
            give(r.active_out.at[f], r.active.at[layer, f, far_part], r.active_send.at[f], r.active_recv.at[layer, f])
            r.acc[...] += dot_nn(r.active_out[f], weights[layer, b_far, at_down:, :])
            active_of(b_own, put_own)
            r.acc[...] += dot_nn(r.active[layer, f, own_part, :], weights[layer, b_own, at_down:, :])

        count(0, nx - 1, mlp)
        pumps[3]()
        count(nx - 1, nx, mlp)
        pumps[4]()
        r.resid[layer + 1] = r.acc[...]
        gone(r.gated.at[layer, own_part], r.gated_send.at[layer])
        gone(r.normed.at[layer, own_part], r.normed_send.at[layer])
        for f in range(nx):
            gone(r.states_out.at[f], r.states_send.at[f])
            gone(r.active_out.at[f], r.active_send.at[f])

    def landing_at(layer, j, at):
        blk, first = j // n_seq, pl.multiple_of(j % n_seq * rows, rows)
        if layer == layers - 1:
            return r.landing, (blk, pl.ds(pl.multiple_of(first + at[0], at[1]), at[1]))
        return weights, (layer + 1, 2 * blk + 1 - core, pl.ds(pl.multiple_of(first + at[0], at[1]), at[1]))

    def landing(layer, j):
        ref, index = landing_at(layer, j, (0, rows))
        return ref.at[index]

    base_y, base_z = (nx - 1) * n_seq, (nx - 1) * n_seq + (ny - 1) * nz

    def credit(sem, peers):
        for device in peers:
            pl.semaphore_signal(sem, inc=1, device_id=device, device_id_type=MESH)

    def line_x():
        return [(seq, other(x, step, nx) * 2 + core) for step in range(1, nx)]

    def line_y():
        return [(geo.seq_of(z, other(y, step, ny)), batch) for step in range(1, ny)]

    def line_z():
        return [(geo.seq_of(other(z, step, nz), y), batch) for step in range(1, nz)]

    taken = set()

    def take_credit(name, sem, layer, amount):
        if layer < layers - 1 and (name, layer) not in taken:
            taken.add((name, layer))
            pl.semaphore_wait(sem, amount)

    def slot(layer, s):
        return weights.at[layer, batch, rows_at(s, rows)]

    per_layer, window = n_seq * (nx - 1), WINDOW

    def entry(idx):
        return idx % (nx - 1), n_seq - 1 - idx // (nx - 1)

    def copy_x(layer, idx):
        k, s = entry(idx)
        f, b_own, _ = blocks(k)
        return remote(
            weights.at[layer, b_own, rows_at(s, rows)], landing(layer, k * n_seq + s), r.sum_send_x.at[layer, k, s],
            r.sum_recv_x.at[layer, k, s], (seq, b_own),
        )

    def arrival_x(layer, idx):
        k, s = entry(idx)

        @pl.when(k == nx - 2)
        def _():
            wait_x(layer, s)
            z_at, y_at = s // geo.stride_z % nz, s // geo.stride_y % ny

            @pl.when(y_at != y)
            def _():
                sum_y(layer, z_at, y_at, s)

    def last_index(z_at):
        return max((n_seq - 1 - geo.seq_of(z_at, y_at)) * (nx - 1) + nx - 2 for y_at in range(ny))

    queue = [0, []]

    def place(g):
        return layers - 1 - g // per_layer, g % per_layer

    def x_steps(steps):
        for _ in range(steps):
            g = queue[0]
            if g >= layers * per_layer + window:
                break
            if g >= window:
                copy_x(*place(g - window)).wait_send()
            if g < layers * per_layer:
                layer, idx = place(g)
                if idx == 0:
                    take_credit("x", r.credit_x, layer, nx - 1)
                    take_credit("y", r.credit_y, layer, ny - 1)
                copy_x(layer, idx).start()
            if g >= window:
                layer, idx = place(g - window)
                arrival_x(layer, idx)
                for z_at in reversed(range(nz)):
                    if last_index(z_at) == idx:
                        queue[1].append((g + DELAYS[0], sum_z, layer, z_at))
                        queue[1].append((g + DELAYS[1], own_sum, layer, z_at))
                        queue[1].append((g + DELAYS[2], spread_block, layer, z_at))
            queue[0] += 1
            due = [event for event in queue[1] if event[0] <= g]
            queue[1] = [event for event in queue[1] if event[0] > g]
            for _, body, layer, z_at in due:
                body(layer, z_at)

    def put_grad(layer, b, first, size, value):
        weights[layer, b, first : first + size, :] = value.astype(BF16)

    def backward(layer, pumps):
        gain_one, gain_two = r.gains[layer, 0:1, :], r.gains[layer, 1:2, :]

        def low_grad(at):
            r.gmlp[at, :] = r.dgrad[at, :].astype(BF16)

        each_tile(low_grad)
        take_credit("mlp", r.credit_mlp, layer, 1)
        give(r.gmlp.at[own_part], r.gmlp.at[far_part], r.gmlp_send.at[0], r.gmlp_recv.at[0])
        r.acc[...] = jnp.zeros_like(r.acc)

        def mlp(k):
            f, b_own, b_far = blocks(k)

            def inner_of(b, put):
                r.wide[...] = dot_nt(r.gmlp[own_part, :], weights[layer, b, at_down:, :])

                def act(at):
                    put(at, (r.wide[at, :] * r.slope[layer, b, at, :]).astype(BF16))

                each_tile(act)

            def put_far(at, low):
                r.ginner_out[f, at, :] = low

            def put_own(at, low):
                r.ginner[f, at, :] = low

            inner_of(b_far, put_far)
            give(r.ginner_out.at[f], r.ginner.at[f, far_part], r.ginner_send.at[f], r.ginner_recv.at[f])
            r.acc[...] += dot_nn(r.ginner_out[f], weights[layer, b_far, at_up:at_down, :])
            inner_of(b_own, put_own)
            r.acc[...] += dot_nn(r.ginner[f, own_part, :], weights[layer, b_own, at_up:at_down, :])

            @pl.when(k == 0)
            def _():
                given(r.gmlp.at[far_part], r.gmlp_recv.at[0])
                given(r.normed.at[layer, far_part], r.normed_recv.at[layer])

            given(r.active.at[layer, f, far_part], r.active_recv.at[layer, f])
            put_grad(layer, b_own, at_down, ffn, dot_tn(r.active[layer, f], r.gmlp[...]))
            given(r.ginner.at[f, far_part], r.ginner_recv.at[f])
            put_grad(layer, b_own, at_up, ffn, dot_tn(r.ginner[f], r.normed[layer]))

        count(0, nx, mlp)
        gone(r.gmlp.at[own_part], r.gmlp_send.at[0])
        for f in range(nx):
            gone(r.ginner_out.at[f], r.ginner_send.at[f])
        if layer > 0:
            credit(r.credit_mlp, [sibling])
        pumps[0]()

        def norm_two(k, total):
            at = rows_at(k, tile)
            values, grad = r.middle[layer, at, :], r.acc[at, :]
            scale = lax.rsqrt(jnp.mean(values * values, axis=-1, keepdims=True) + EPSILON)
            unit = values * scale
            gunit = grad * gain_two
            full = r.dgrad[at, :] + scale * (gunit - unit * jnp.mean(gunit * unit, axis=-1, keepdims=True))
            r.dgrad[at, :] = full
            r.gy[at, :] = full.astype(BF16)
            return total + jnp.sum(grad * unit, axis=0, keepdims=True)

        row_sum = jnp.zeros((1, width), F32)
        r.ggains[layer, 1:2, :] = lax.fori_loop(0, tokens // tile, norm_two, row_sum)
        take_credit("gate", r.credit_gate, layer, 1)
        give(r.gy.at[own_part], r.gy.at[far_part], r.gy_send.at[0], r.gy_recv.at[0])
        number = layers + layer

        def front(k):
            f, b_own, b_far = blocks(k)

            def scan(b):
                r.gstates[b] = dot_nt(r.gy[own_part, :], weights[layer, b, at_out:at_up, :])

                def group(k, carried):
                    new = []
                    for stream in range(streams):
                        at = pl.ds(pl.multiple_of(stream * span + (groups - 1 - k) * 8, 8), 8)
                        f, i = r.fgate[layer, b, at, :], r.igate[layer, b, at, :]
                        decay = f * (1.0 / (f + i)) * widen(r.mask[at, :], hid)
                        term = decay * r.gstates[b, at, :]
                        for step in (1, 2, 4):
                            reach = row8 < 8 - step
                            term = term + decay * jnp.where(reach, pltpu.roll(term, 8 - step, 0), 0.0)
                            decay = decay * jnp.where(reach, pltpu.roll(decay, 8 - step, 0), 1.0)
                        prod_in, state_in = carried[stream]
                        term = term + decay * state_in
                        decay = decay * prod_in
                        r.deltas[b, at, :] = term
                        r.prods[b, at, :] = decay
                        new.append((decay[0:1], term[0:1]))
                    return tuple(new)

                put_summary(number, b, lax.fori_loop(0, groups, group, start_scan))

            scan(b_far)
            scan(b_own)

            @pl.when(k == 0)
            def _():
                given(r.gy.at[far_part], r.gy_recv.at[0])

            given(r.states_low.at[layer, f, far_part], r.states_recv.at[layer, f])
            put_grad(layer, b_own, at_out, hid, dot_tn(r.states_low[layer, f], r.gy[...]))

        count(0, nx, front)
        post, collect = mail(number, False)
        post()
        pumps[1]()
        r.incoming[...] = collect()
        r.acc[...] = jnp.zeros_like(r.acc)
        span_row = lax.broadcasted_iota(jnp.int32, (span, hid), 0)
        given(r.gated.at[layer, far_part], r.gated_recv.at[layer])

        def rear(k):
            f, b_own, b_far = blocks(k)

            def gates_of(b, put):
                sum_f, sum_i = jnp.zeros((1, hid), F32), jnp.zeros((1, hid), F32)
                for stream in range(streams):
                    at = slice(stream * span, (stream + 1) * span)
                    late = r.incoming[b, stream : stream + 1, :]
                    linked = r.deltas[b, at, :] + r.prods[b, at, :] * late
                    linked = jnp.where(span_row == span - 1, late, pltpu.roll(linked, span - 1, 0))
                    delta = r.gstates[b, at, :] + linked
                    early = r.carry_in[layer, b, stream : stream + 1, :]
                    before = jnp.where(span_row == 0, early, pltpu.roll(r.states[layer, b, at, :], 1, 0))
                    fg, ig = r.fgate[layer, b, at, :], r.igate[layer, b, at, :]
                    share = 1.0 / (fg + ig)
                    fshare, ishare = fg * share, ig * share
                    gap = delta * (before * widen(r.mask[at, :], hid) - r.cand[layer, b, at, :]) * fshare * ishare
                    gf = (gap * (1.0 - fg)).astype(BF16)
                    gi = (gap * (ig - 1.0)).astype(BF16)
                    put(at, (gf, gi, (delta * ishare).astype(BF16)))
                    sum_f = sum_f + jnp.sum(gf.astype(F32), axis=0, keepdims=True)
                    sum_i = sum_i + jnp.sum(gi.astype(F32), axis=0, keepdims=True)
                r.gbiases[layer, b, 0:1, :] = sum_f
                r.gbiases[layer, b, 1:2, :] = sum_i

            def put_far(at, lows):
                for member in range(3):
                    r.ggate_out[member, f, at, :] = lows[member]

            def put_own(at, lows):
                for member in range(3):
                    r.ggate[member, f, at, :] = lows[member]

            gates_of(b_far, put_far)
            for member in range(3):
                give(
                    r.ggate_out.at[member, f], r.ggate.at[member, f, far_part], r.ggate_send.at[member, f],
                    r.ggate_recv.at[member, f],
                )
            gates_of(b_own, put_own)
            total = r.acc[...]
            for member in range(3):
                at = slice(member * hid, (member + 1) * hid)
                total = total + dot_nn(r.ggate_out[member, f], weights[layer, b_far, at, :])
                total = total + dot_nn(r.ggate[member, f, own_part, :], weights[layer, b_own, at, :])
            r.acc[...] = total
            for member in range(3):
                given(r.ggate.at[member, f, far_part], r.ggate_recv.at[member, f])
                put_grad(layer, b_own, member * hid, hid, dot_tn(r.ggate[member, f], r.gated[layer]))

        count(0, nx, rear)
        gone(r.gy.at[own_part], r.gy_send.at[0])
        for f in range(nx):
            for member in range(3):
                gone(r.ggate_out.at[member, f], r.ggate_send.at[member, f])
        if layer > 0:
            credit(r.credit_gate, [sibling])
            credit(r.credit_x, line_x())
            credit(r.credit_y, line_y())
            credit(r.credit_z, line_z())

        def norm_one(k, total):
            at = rows_at(k, tile)
            values, grad = r.resid[layer, at, :], r.acc[at, :]
            scale = lax.rsqrt(jnp.mean(values * values, axis=-1, keepdims=True) + EPSILON)
            unit = values * scale
            gunit = grad * gain_one
            full = r.dgrad[at, :] + scale * (gunit - unit * jnp.mean(gunit * unit, axis=-1, keepdims=True))
            r.dgrad[at, :] = full
            return total + jnp.sum(grad * unit, axis=0, keepdims=True)

        r.ggains[layer, 0:1, :] = lax.fori_loop(0, tokens // tile, norm_one, row_sum)
        if layer > 0:
            load_old(layer - 1).start()
        pumps[3]()

    def load_old(layer):
        return pltpu.make_async_copy(old_ref.at[layer, 0], r.resid.at[layer + 1, pl.ds(0, rows)], r.load.at[layer])

    def wait_x(layer, s):
        for k in range(nx - 1):
            part = landing(layer, k * n_seq + s)
            remote(part, part, r.sum_send_x.at[layer, k], r.sum_recv_x.at[layer, k, s], sibling).wait_recv()

    def from_x(s):
        return [k * n_seq + s for k in range(nx - 1)]

    def wait_y(layer, z_at):
        for dy in range(1, ny):
            part = landing(layer, base_y + (dy - 1) * nz + z_at)
            remote(
                part, part, r.sum_send_y.at[layer, dy - 1], r.sum_recv_y.at[layer, dy - 1, z_at], sibling
            ).wait_recv()

    def from_y(z_at):
        return [base_y + (dy - 1) * nz + z_at for dy in range(1, ny)]

    part_rows = min(rows, tile)

    def total_of(layer, s, sources, first):
        total = weights[layer, batch, pl.ds(pl.multiple_of(s * rows + first, part_rows), part_rows), :].astype(F32)
        for j in sources:
            ref, index = landing_at(layer, j, (first, part_rows))
            total = total + ref[(*index, slice(None))].astype(F32)
        return total

    def add_up(layer, s, sources):
        def one(k):
            first = k * part_rows
            weights[layer, batch, pl.ds(pl.multiple_of(s * rows + first, part_rows), part_rows), :] = total_of(
                layer, s, sources, first
            ).astype(BF16)

        count(0, rows // part_rows, one)

    def sum_y(layer, z_at, y_at, s):
        add_up(layer, s, from_x(s))
        away = lax.rem(y_at - y + ny, ny) - 1
        remote(
            slot(layer, s), landing(layer, base_y + away * nz + z_at), r.sum_send_y.at[layer, away],
            r.sum_recv_y.at[layer, away, z_at], (geo.seq_of(z, y_at), batch),
        ).start()

    def sum_z(layer, z_at):
        take_credit("z", r.credit_z, layer, nz - 1)
        s = geo.seq_of(z_at, y)
        wait_y(layer, z_at)

        @pl.when(z != z_at)
        def _():
            add_up(layer, s, from_x(s) + from_y(z_at))
            away = lax.rem(z_at - z + nz, nz) - 1
            remote(
                slot(layer, s), landing(layer, base_z + away), r.sum_send_z.at[layer, away],
                r.sum_recv_z.at[layer, away], (s, batch),
            ).start()

    def block_slot(layer, z_at, y_at):
        return block_ref.at[layer, rows_at(geo.seq_of(z_at, y_at), rows)]

    def block_to_y(layer, z_at, part):
        for step in range(1, ny):
            remote(
                part, block_slot(layer, z_at, y), r.block_send_y.at[layer, step - 1],
                r.block_recv.at[layer, geo.seq_of(z_at, y)], (geo.seq_of(z, other(y, step, ny)), batch),
            ).start()

    def own_sum(layer, z_at):
        @pl.when(z == z_at)
        def _():
            for dz in range(1, nz):
                part = landing(layer, base_z + dz - 1)
                remote(
                    part, part, r.sum_send_z.at[layer, dz - 1], r.sum_recv_z.at[layer, dz - 1], sibling
                ).wait_recv()
            load_old(layer).wait()
            sources = from_x(seq) + from_y(z_at) + [base_z + dz - 1 for dz in range(1, nz)]

            def one(k, squares):
                first = k * part_rows
                at = rows_at(k, part_rows)
                total = total_of(layer, seq, sources, first)
                r.middle[layer, at, :] = total
                moment = MOMENTUM_DECAY * r.resid[layer + 1, at, :] + total
                r.resid[layer + 1, at, :] = moment
                r.low_moments[layer, at, :] = moment.astype(BF16)
                return squares + jnp.sum(moment * moment, axis=0, keepdims=True)

            squares = lax.fori_loop(0, rows // part_rows, one, jnp.zeros((1, width), F32))
            r.square_own[layer] = jnp.broadcast_to(jnp.sum(squares, axis=1, keepdims=True), (8, 128))
            part = r.low_moments.at[layer]
            block_to_z(layer, z, part)
            block_to_y(layer, z, part)
            pltpu.make_async_copy(part, block_slot(layer, z, y), r.block_own.at[layer]).start()
            pltpu.make_async_copy(
                r.middle.at[layer, pl.ds(0, rows)], shard_ref.at[layer], r.store.at[layer]
            ).start()

    def along_z(layer, z_at, go):
        for way, passes, to in (
            (0, jnp.logical_and(z_at <= z, z + 1 < nz), z + 1),
            (1, jnp.logical_and(z_at >= z, z >= 1), z - 1),
        ):
            sem = r.block_send_z.at[layer, z_at, way]

            @pl.when(passes)
            def _():
                go(to, sem)

    def block_to_z(layer, z_at, part):
        along_z(
            layer, z_at,
            lambda to, sem: remote(
                part, block_slot(layer, z_at, y), sem, r.block_recv.at[layer, geo.seq_of(z_at, y)],
                (geo.seq_of(to, y), batch),
            ).start(),
        )

    def wait_block(layer, z_at, y_at):
        part = block_slot(layer, z_at, y_at)
        remote(
            part, part, r.block_send_z.at[layer, 0, 0], r.block_recv.at[layer, geo.seq_of(z_at, y_at)], sibling
        ).wait_recv()

    def spread_block(layer, z_at):
        @pl.when(z != z_at)
        def _():
            wait_block(layer, z_at, y)
            block_to_z(layer, z_at, block_slot(layer, z_at, y))
            block_to_y(layer, z_at, block_slot(layer, z_at, y))

    def finish_block(layer):
        for z_at in range(nz):
            count(1, ny, lambda k: wait_block(layer, z_at, other(y, k, ny)))
        pltpu.make_async_copy(r.low_moments.at[layer], block_slot(layer, z, y), r.block_own.at[layer]).wait()
        pltpu.make_async_copy(r.middle.at[layer, pl.ds(0, rows)], shard_ref.at[layer], r.store.at[layer]).wait()

    def vec_start():
        each_piece(write_piece)
        remote(r.vec_out.at[0], r.vec_s.at[0], r.vec_send_s.at[0], r.vec_recv_s.at[0], sibling).start()

    def vec_second():
        remote(r.vec_out.at[0], r.vec_s.at[0], r.vec_send_s.at[0], r.vec_recv_s.at[0], sibling).wait_recv()
        total = r.vec_out[0] + r.vec_s[0]
        r.vec_out[1] = total
        r.vec_x[x] = total
        for step in range(1, nx):
            x_at = other(x, step, nx)
            remote(
                r.vec_out.at[1], r.vec_x.at[x], r.vec_send_x.at[x_at], r.vec_recv_x.at[x], (seq, x_at * 2 + core)
            ).start()

    def vec_third():
        for step in range(1, nx):
            x_at = other(x, step, nx)
            remote(
                r.vec_out.at[1], r.vec_x.at[x_at], r.vec_send_x.at[x_at], r.vec_recv_x.at[x_at], sibling
            ).wait_recv()
        total = r.vec_x[0]
        for k in range(1, nx):
            total = total + r.vec_x[k]
        r.vec_out[2] = total
        r.vec_q[seq] = total

        def one(k):
            to = other(seq, k, n_seq)
            remote(r.vec_out.at[2], r.vec_q.at[seq], r.vec_send_q.at[to], r.vec_recv_q.at[seq], (to, batch)).start()

        count(1, n_seq, one)

    def vec_last():
        def one(k):
            source = other(seq, k, n_seq)
            remote(
                r.vec_out.at[2], r.vec_q.at[source], r.vec_send_q.at[source], r.vec_recv_q.at[source], sibling
            ).wait_recv()

        count(1, n_seq, one)
        total = lax.fori_loop(1, n_seq, lambda k, t: t + r.vec_q[k], r.vec_q[0])
        vgrad_ref[...] = total
        new_vmom_ref[...] = MOMENTUM_DECAY * vmom_ref[...] + total
        first = 0
        for member, length in enumerate((width, width, H, H)):
            at = slice(first, first + length)
            segment = new_vmom_ref[:, at]
            scale = lax.rsqrt(jnp.mean(segment * segment, axis=1, keepdims=True) + 1e-06)
            fresh = vec_ref[:, at] - SEGMENT_RATES[member] * segment * scale
            new_vec_ref[:, at] = fresh
            new_vavg_ref[:, at] = AVERAGE_DECAY * vavg_ref[:, at] + (1.0 - AVERAGE_DECAY) * fresh
            first += length

    hid_devices, ffn_devices = hid // rows, ffn // rows
    in_group = jnp.where(seq < 4 * hid_devices, hid_devices, ffn_devices)
    rank = lax.rem(seq, in_group)
    group_first = seq - rank

    def pack_gram(stage, value):
        r.gram_out[stage, 0] = value[0:half, 0:half].astype(BF16)
        r.gram_out[stage, 1] = value[0:half, half:].astype(BF16)
        r.gram_out[stage, 2] = value[half:, half:].astype(BF16)

    def gram_pair(stage, into, squares_into, sends, recvs, device):
        return (
            remote(r.gram_out.at[stage], into, sends[0], recvs[0], device),
            remote(r.square_out.at[stage], squares_into, sends[1], recvs[1], device),
        )

    def gram_round(stage, parts, squares):
        for n in range(3):
            total = r.gram_out[stage, n].astype(F32)
            for ref in parts:
                total = total + ref[n].astype(F32)
            r.gram_out[stage + 1, n] = total.astype(BF16)
        total = r.square_out[stage]
        for ref in squares:
            total = total + ref[...]
        r.square_out[stage + 1] = total

    def group_copies(k):
        here_at = lax.rem(rank - k - 1 + in_group, in_group)
        return gram_pair(
            2, r.gram_g.at[here_at], r.square_g.at[here_at],
            (r.gram_send_g.at[0, here_at], r.gram_send_g.at[1, here_at]),
            (r.gram_recv_g.at[0, here_at], r.gram_recv_g.at[1, here_at]), (group_first + k, batch),
        )

    def even():
        return jnp.concatenate([r.acc[...], r.resid[0]], axis=0)

    def put_even(value):
        r.acc[...] = value[0:half]
        r.resid[0] = value[half:]

    def newton_schulz(pumps):
        mine, theirs = core, 1 - core
        pack_gram(0, dot_tn(r.low_moments[theirs], r.low_moments[theirs]))
        r.square_out[0] = r.square_own[theirs]
        to_core = gram_pair(
            0, r.gram_s.at[0], r.square_s.at[0], (r.gram_send_s.at[0], r.gram_send_s.at[1]),
            (r.gram_recv_s.at[0], r.gram_recv_s.at[1]), sibling,
        )
        for copy in to_core:
            copy.start()
        put_even(dot_tn(r.low_moments[mine], r.low_moments[mine]))
        for copy in to_core:
            copy.wait()
        pack_gram(0, even())
        r.square_out[0] = r.square_own[mine]
        gram_round(0, [r.gram_s.at[0]], [r.square_s.at[0]])
        to_x = []
        for step in range(1, nx):
            to_x += gram_pair(
                1, r.gram_x.at[step - 1], r.square_x.at[step - 1],
                (r.gram_send_x.at[0, step - 1], r.gram_send_x.at[1, step - 1]),
                (r.gram_recv_x.at[0, step - 1], r.gram_recv_x.at[1, step - 1]),
                (seq, other(x, step, nx) * 2 + core),
            )
        for copy in to_x:
            copy.start()
        pumps[0]()
        for copy in to_x:
            copy.wait()
        gram_round(1, [r.gram_x.at[k] for k in range(nx - 1)], [r.square_x.at[k] for k in range(nx - 1)])

        def to_member(k):
            for copy in group_copies(lax.rem(rank + k, in_group)):
                copy.start()

        def from_member(k):
            k = k - 1
            remote(r.gram_out.at[2], r.gram_g.at[k], r.gram_send_g.at[0, k], r.gram_recv_g.at[0, k], sibling).wait()
            remote(
                r.square_out.at[2], r.square_g.at[k], r.gram_send_g.at[1, k], r.gram_recv_g.at[1, k], sibling
            ).wait()

        count(1, in_group, to_member)
        pumps[1]()
        count(1, in_group, from_member)
        square = lax.fori_loop(1, in_group, lambda k, t: t + r.square_g[k - 1], r.square_out[2])
        inverse = 1.0 / (jnp.sqrt(square) + 1e-07)
        r.inverses[mine] = inverse
        scale = inverse[0:1, 0:1] * inverse[0:1, 0:1]

        def corner(n):
            total = r.gram_out[2, n].astype(F32)
            return lax.fori_loop(1, in_group, lambda k, t: t + r.gram_g[k - 1, n].astype(F32), total) * scale

        r.acc[:, 0:half] = corner(0)
        r.acc[:, half:] = corner(1)
        r.resid[0, :, 0:half] = r.acc[:, half:].T
        r.resid[0, :, half:] = corner(2)

        def polynomial(step):
            low = even().astype(BF16)
            r.polys[mine, step] = (QUINTIC[1] * even() + QUINTIC[2] * dot_nn(low, low)).astype(BF16)

        def precise(low, value):
            high = value.astype(BF16)
            rest = (value - high.astype(F32)).astype(BF16)
            return dot_nn(low, high) + dot_nn(low, rest)

        polynomial(0)
        lead = QUINTIC[0]
        poly = r.polys[mine, 0]
        r.odd[...] = precise(poly, even())
        put_even(lead * lead * even() + 2.0 * lead * r.odd[...] + precise(poly, r.odd[...]))
        polynomial(1)
        out = (
            remote(r.polys.at[mine], r.polys.at[mine], r.poly_send.at[0], r.poly_recv.at[0], sibling),
            remote(r.inverses.at[mine], r.inverses.at[mine], r.poly_send.at[1], r.poly_recv.at[1], sibling),
        )
        for copy in out:
            copy.start()

        def apply(layer):
            begin = (r.resid[layer + 1, 0:rows, :] * r.inverses[layer, 0:1, 0:1]).astype(BF16)
            for step in range(NS_STEPS):
                begin = (lead * begin.astype(F32) + dot_nn(begin, r.polys[layer, step])).astype(BF16)
            ortho_ref[layer] = begin

        apply(mine)
        for copy in out:
            copy.wait_send()
        remote(r.polys.at[theirs], r.polys.at[theirs], r.poly_send.at[0], r.poly_recv.at[0], sibling).wait_recv()
        remote(
            r.inverses.at[theirs], r.inverses.at[theirs], r.poly_send.at[1], r.poly_recv.at[1], sibling
        ).wait_recv()
        apply(theirs)

    def ahead(steps):
        return lambda: advance(steps)

    def nothing():
        pass

    for layer in range(layers):
        pump = ahead(1) if layer < layers - 1 else nothing
        forward(layer, [pump] * 5)
    for layer in range(layers):
        gather.finish(layer)

    def turn(at):
        act_ref[at, :] = r.resid[layers, at, :].astype(BF16)
        r.dgrad[at, :] = out_grad_ref[at, :].astype(F32)

    each_tile(turn)
    load_old(layers - 1).start()

    def starts(steps):
        return lambda: x_steps(steps)

    share = per_layer // 8
    for layer in reversed(range(layers)):
        backward(layer, [starts(2 * share), starts(2 * share), nothing, starts(2 * share)])
    out_dx = pltpu.make_async_copy(r.dgrad, dx_ref, r.store.at[layers])
    out_dx.start()
    vec_start()
    x_steps(share)
    vec_second()
    x_steps(share)
    vec_third()
    x_steps(layers * per_layer + window)
    held = [event for event in queue[1] if event[1] is spread_block]
    for _, body, layer, z_at in sorted(queue[1], key=lambda event: event[0]):
        if body is not spread_block:
            body(layer, z_at)

    def spread(events):
        for _, body, layer, z_at in events:
            body(layer, z_at)

    cut = len(held) // 2
    newton_schulz([lambda: spread(held[:cut]), lambda: spread(held[cut:])])
    vec_last()
    for layer in range(layers):
        finish_block(layer)
    out_dx.wait()

    def drain(part, sem):
        remote(part, part, sem, r.vec_recv_s.at[0], sibling).wait_send()

    for layer in range(layers):
        for dy in range(1, ny):
            drain(weights.at[layer, 0, pl.ds(0, nz * rows)], r.sum_send_y.at[layer, dy - 1])
            drain(weights.at[layer, 0, pl.ds(0, nz * rows)], r.block_send_y.at[layer, dy - 1])
        for dz in range(1, nz):
            drain(r.low_moments.at[layer], r.sum_send_z.at[layer, dz - 1])
        for z_at in range(nz):
            along_z(layer, z_at, lambda to, sem: drain(r.low_moments.at[layer], sem))
    drain(r.vec_out.at[0], r.vec_send_s.at[0])
    for step in range(1, nx):
        drain(r.vec_out.at[1], r.vec_send_x.at[other(x, step, nx)])
    count(1, n_seq, lambda k: drain(r.vec_out.at[2], r.vec_send_q.at[other(seq, k, n_seq)]))


def run_step(geo, stream_in, out_grad, doc_lengths, mats, mat_momenta, vectors, vec_momenta, vec_averages):
    layers, _, rows, width = mats.shape
    streams, span, _ = stream_in.shape
    sz = Sizes(geo, layers, streams, span, width, rows, doc_lengths.shape[1])
    names = make_scratch(geo, sz)
    vmem, anywhere = pl.BlockSpec(memory_space=pltpu.VMEM), pl.BlockSpec(memory_space=pl.ANY)
    smem = pl.BlockSpec(memory_space=pltpu.SMEM)
    vec = jax.ShapeDtypeStruct(vectors.shape, F32)
    return pl.pallas_call(
        functools.partial(step_kernel, geo, sz, names),
        out_shape=(
            jax.ShapeDtypeStruct((sz.tokens, width), BF16),
            jax.ShapeDtypeStruct((sz.tokens, width), F32),
            jax.ShapeDtypeStruct((layers, rows, width), F32),
            jax.ShapeDtypeStruct((layers, sz.block, width), BF16),
            jax.ShapeDtypeStruct((layers, rows, width), BF16),
            vec, vec, vec, vec,
        ),
        in_specs=[anywhere, anywhere, vmem, vmem, smem, vmem, vmem, vmem],
        out_specs=(vmem, anywhere, anywhere, anywhere, vmem, vmem, vmem, vmem, vmem),
        scratch_shapes=names.shapes,
        compiler_params=pltpu.CompilerParams(
            collective_id=0, has_side_effects=True, vmem_limit_bytes=63 * 2**20
        ),
        name="step",
    )(
        mats, mat_momenta, stream_in.reshape(sz.tokens, width), out_grad.reshape(sz.tokens, width), doc_lengths,
        vectors, vec_momenta, vec_averages,
    )


def closing_kernel(
    small_rows, act, dx, shard, block, ortho, mats, averages, vgrad, vmom, vec, vavg,
    act_out, dx_out, shard_out, block_out, mats_out, averages_out, vgrad_out, vmom_out, vec_out, vavg_out,
):
    act_out[...] = act[...]
    dx_out[...] = dx[...]
    shard_out[:, 0] = shard[...]
    block_out[:, 0] = block[...].astype(F32)
    rows, width = mats_out.shape[2] * pl.num_programs(0), mats_out.shape[3]
    small = lax.axis_index("seq") * rows < small_rows
    factor = jnp.where(small, 0.2 * math.sqrt(max(H, width)), 0.2 * math.sqrt(max(FF, width)))
    fresh = mats[:, 0] - MATRIX_RATE * (ortho[...].astype(F32) * factor)
    mats_out[:, 0] = fresh
    averages_out[:, 0] = AVERAGE_DECAY * averages[:, 0] + (1.0 - AVERAGE_DECAY) * fresh
    vgrad_out[...] = vgrad[...]
    vmom_out[...] = vmom[...]
    vec_out[...] = vec[...]
    vavg_out[...] = vavg[...]


def run_closing(geo, act, dx, shard, block, ortho, mats, averages, vecs):
    layers, _, rows, width = mats.shape
    tokens, block_rows = act.shape[0], block.shape[1]
    grid = max(min(8, rows // 16), 1)

    def flat(count):
        return pl.BlockSpec((count // grid, width), lambda k: (k, 0))

    def deep(count):
        return pl.BlockSpec((layers, count // grid, width), lambda k: (0, k, 0))

    def boxed(count):
        return pl.BlockSpec((layers, 1, count // grid, width), lambda k: (0, 0, k, 0))

    vec = pl.BlockSpec(vecs[0].shape, lambda k: (0, 0))
    vec_shape = jax.ShapeDtypeStruct(vecs[0].shape, F32)
    box = jax.ShapeDtypeStruct(mats.shape, F32)
    return pl.pallas_call(
        functools.partial(closing_kernel, 4 * (H // geo.n_batch)),
        grid=(grid,),
        out_shape=(
            jax.ShapeDtypeStruct(act.shape, BF16),
            jax.ShapeDtypeStruct(dx.shape, F32),
            box,
            jax.ShapeDtypeStruct((layers, 1, block_rows, width), F32),
            box,
            box,
            *[vec_shape] * 4,
        ),
        in_specs=[
            flat(tokens), flat(tokens), deep(rows), deep(block_rows), deep(rows), boxed(rows), boxed(rows), *[vec] * 4
        ],
        out_specs=(
            flat(tokens), flat(tokens), boxed(rows), boxed(block_rows), boxed(rows), boxed(rows), *[vec] * 4
        ),
        compiler_params=pltpu.CompilerParams(vmem_limit_bytes=60 * 2**20),
        name="closing",
    )(act, dx, shard, block, ortho, mats, averages, *vecs)


def per_device(
    geo, stream_in, out_grad, doc_lengths, mats, mat_momenta, mat_averages, vectors, vec_momenta, vec_averages
):
    act, dx, shard, block, ortho, *vecs = run_step(
        geo, stream_in, out_grad, doc_lengths, mats, mat_momenta, vectors, vec_momenta, vec_averages
    )
    act, dx, *rest = run_closing(geo, act, dx, shard, block, ortho, mats, mat_averages, vecs)
    return (act.reshape(stream_in.shape), dx.reshape(stream_in.shape), *rest)


def solution(mesh):
    geo = Geometry(mesh.shape["seq"], mesh.shape["batch"])
    rows = P(None, "batch", "seq", None)
    tokens = P("batch", "seq", None)
    return jax.shard_map(
        functools.partial(per_device, geo),
        mesh=mesh,
        in_specs=(tokens, tokens, P("batch", None), rows, rows, rows, P(), P(), P()),
        out_specs=(tokens, tokens, rows, P(None, "batch", None, None), rows, rows, P(), P(), P(), P()),
        check_vma=False,
    )
```

```python
import functools
import math

import jax
import jax.numpy as jnp
from jax import lax
from jax.experimental import pallas as pl
from jax.experimental.pallas import tpu as pltpu
from jax.sharding import PartitionSpec as P

H = 1024
FF = 2048
NS_STEPS = 2
MESH = pl.DeviceIdType.MESH
F32 = jnp.float32
BF16 = jnp.bfloat16

EPSILON = 1e-05
MOMENTUM_DECAY = 0.5
AVERAGE_DECAY = 0.9
MATRIX_RATE = 0.3
SEGMENT_RATES = (0.3, 0.3, 0.5, 2.0)
QUINTIC = (3.4445, -4.775, 2.0315)
GELU_A = 0.7978845608
GELU_B = 0.044715


class Geometry:
    def __init__(self, n_seq, n_batch):
        self.n_seq, self.n_batch = n_seq, n_batch
        self.nz, self.ny, self.stride_z, self.stride_y = {
            8: (4, 2, 2, 1),
            32: (8, 4, 1, 8),
        }.get(n_seq, (n_seq, 1, 1, n_seq))
        self.nx = n_batch // 2
        self.swaps = self.ny == self.nx
        self.nu, self.nv = self.ny, self.nx

    def seq_of(self, z, y):
        return z * self.stride_z + y * self.stride_y

    def here(self):
        seq, batch = lax.axis_index("seq"), lax.axis_index("batch")
        z = seq // self.stride_z % self.nz
        y = seq // self.stride_y % self.ny
        return seq, batch, z, y, batch // 2, batch % 2

    def to_yx(self, u, v, core):
        if not self.swaps:
            return u, v
        return u + core * (v - u), v + core * (u - v)


def dot_nn(a, b):
    return lax.dot_general(a, b, (((1,), (0,)), ((), ())), preferred_element_type=F32)


def dot_nt(a, b):
    return lax.dot_general(a, b, (((1,), (1,)), ((), ())), preferred_element_type=F32)


def dot_tn(a, b):
    return lax.dot_general(a, b, (((0,), (0,)), ((), ())), preferred_element_type=F32)


def other(mine, step, count):
    return lax.rem(mine + step, count)


def sigmoid(values):
    return 1.0 / (1.0 + jnp.exp(-values))


def widen(column_tile, width):
    return jnp.concatenate([column_tile] * (width // 128), axis=1)


def count(first, last, body):
    lax.fori_loop(first, last, lambda k, _: body(k) or 0, 0)


def remote(src, dst, send, recv, device):
    return pltpu.make_async_remote_copy(
        src_ref=src, dst_ref=dst, send_sem=send, recv_sem=recv, device_id=device, device_id_type=MESH
    )


class Gather:
    def __init__(self, geo, weights, rows, refs):
        self.geo, self.weights, self.rows, self.half_rows = geo, weights, rows, rows // 2
        self.send_z, self.send_u, self.send_v, self.send_s = refs.send_z, refs.send_u, refs.send_v, refs.send_s
        self.recv, self.recv_s = refs.recv, refs.recv_s
        self.seq, self.batch, self.z, self.y, self.x, self.core = geo.here()
        if geo.swaps:
            self.u = self.y + self.core * (self.x - self.y)
            self.v = self.x + self.core * (self.y - self.x)
        else:
            self.u, self.v = self.y, self.x
        self.sibling = (self.seq, self.x * 2 + 1 - self.core)

    def part(self, layer, half, z, u, v):
        y, x = self.geo.to_yx(u, v, self.core)
        start = self.geo.seq_of(z, y) * self.rows + half * self.half_rows
        return self.weights.at[layer, x * 2 + self.core, pl.ds(pl.multiple_of(start, self.half_rows), self.half_rows)]

    def arrival(self, layer, half, z, u, v):
        geo = self.geo
        return self.recv.at[(((layer * 2 + half) * geo.nz + z) * geo.nu + u) * geo.nv + v]

    def device(self, z, u, v):
        y, x = self.geo.to_yx(u, v, self.core)
        return (self.geo.seq_of(z, y), x * 2 + self.core)

    def push(self, layer, half, z, u, device, send):
        part = self.part(layer, half, z, u, self.v)
        remote(part, part, send, self.arrival(layer, half, z, u, self.v), device).start()

    def arrived(self, layer, half, z, u, v):
        part = self.part(layer, half, z, u, v)
        remote(part, part, self.send_s.at[layer], self.arrival(layer, half, z, u, v), self.sibling).wait_recv()

    def along_z(self, layer, half, z, u, go):
        for way, passes, to in (
            (0, jnp.logical_and(z <= self.z, self.z + 1 < self.geo.nz), self.z + 1),
            (1, jnp.logical_and(z >= self.z, self.z >= 1), self.z - 1),
        ):
            sem = self.send_z.at[layer, (half * 2 + way) * self.geo.nz + z, u]

            @pl.when(passes)
            def _():
                go(to, sem)

    def to_z(self, layer, half, z, u):
        self.along_z(
            layer, half, z, u,
            lambda to, sem: self.push(layer, half, z, u, self.device(to, self.u, self.v), sem),
        )

    def to_u(self, layer, half, z):
        for step in range(1, self.geo.nu):
            self.push(
                layer, half, z, self.u, self.device(self.z, other(self.u, step, self.geo.nu), self.v),
                self.send_u.at[layer, half, step - 1],
            )

    def to_v(self, layer, half, z, u):
        for step in range(1, self.geo.nv):
            self.push(
                layer, half, z, u, self.device(self.z, self.u, other(self.v, step, self.geo.nv)),
                self.send_v.at[layer, step - 1],
            )

    def to_sibling(self, layer, half, z, u, v):
        part = self.part(layer, half, z, u, v)
        remote(part, part, self.send_s.at[layer], self.recv_s.at[layer], self.sibling).start()

    def begin(self, layer):
        for half in range(2):
            self.to_z(layer, half, self.z, self.u)
            self.to_u(layer, half, self.z)
            self.to_v(layer, half, self.z, self.u)
            self.to_sibling(layer, half, self.z, self.u, self.v)

        def one(k):
            u = other(self.u, k, self.geo.nu)
            self.arrived(layer, 1, self.z, u, self.v)
            self.to_z(layer, 1, self.z, u)
            self.to_v(layer, 1, self.z, u)
            self.to_sibling(layer, 1, self.z, u, self.v)

        count(1, self.geo.nu, one)

    def at_distance(self, distance, body):
        if distance == 0:
            body(self.z)
            return

        @pl.when(self.z >= distance)
        def _():
            body(self.z - distance)

        @pl.when(self.z + distance < self.geo.nz)
        def _():
            body(self.z + distance)

    def from_z(self, layer, z):
        self.arrived(layer, 0, z, self.u, self.v)
        self.to_z(layer, 0, z, self.u)
        self.to_u(layer, 0, z)
        self.to_v(layer, 0, z, self.u)
        self.to_sibling(layer, 0, z, self.u, self.v)

        def one(k):
            u = other(self.u, k, self.geo.nu)
            self.arrived(layer, 1, z, u, self.v)
            self.to_z(layer, 1, z, u)
            self.to_v(layer, 1, z, u)
            self.to_sibling(layer, 1, z, u, self.v)

        count(0, self.geo.nu, one)

    def from_u(self, layer, z):
        def one(k):
            u = other(self.u, k, self.geo.nu)
            self.arrived(layer, 0, z, u, self.v)
            self.to_v(layer, 0, z, u)
            self.to_sibling(layer, 0, z, u, self.v)

        count(1, self.geo.nu, one)

    def from_v(self, layer, z):
        def one(k):
            half = k % 2
            u = other(self.u, k // 2 // (self.geo.nv - 1), self.geo.nu)
            v = other(self.v, k // 2 % (self.geo.nv - 1) + 1, self.geo.nv)
            self.arrived(layer, half, z, u, v)
            self.to_sibling(layer, half, z, u, v)

        count(0, 2 * self.geo.nu * (self.geo.nv - 1), one)

    def step(self, layer, t):
        nz = self.geo.nz
        if t == 0:
            self.begin(layer)
        if 1 <= t < nz:
            self.at_distance(t, lambda z: self.from_z(layer, z))
        if 1 <= t <= nz:
            self.at_distance(t - 1, lambda z: self.from_u(layer, z))
        if 2 <= t <= nz + 1:
            self.at_distance(t - 2, lambda z: self.from_v(layer, z))

    def steps(self, layers):
        last = self.geo.nz + 1
        order = []
        for layer in range(layers):
            order += [(layer, t) for t in range(0 if layer == 0 else 1, last)]
            if layer + 1 < layers:
                order.append((layer + 1, 0))
            order.append((layer, last))
        return order

    def ready(self, layer):
        part = self.weights.at[layer, pl.ds(0, self.geo.nx)]
        remote(part, part, self.send_s.at[layer], self.recv_s.at[layer], self.sibling).wait_recv()

    def finish(self, layer):
        geo = self.geo

        def drain(part, sem):
            remote(part, part, sem, self.recv_s.at[layer], self.sibling).wait_send()

        one = self.part(layer, 0, self.z, self.u, self.v)
        for z in range(geo.nz):
            self.along_z(layer, 0, z, self.u, lambda to, sem: drain(one, sem))
            for u in range(geo.nu):
                self.along_z(layer, 1, z, u, lambda to, sem: drain(one, sem))
        for step in range(1, geo.nu):
            drain(self.weights.at[layer, 0, pl.ds(0, geo.nz * self.half_rows)], self.send_u.at[layer, 0, step - 1])
            drain(one, self.send_u.at[layer, 1, step - 1])
        for step in range(1, geo.nv):
            drain(self.weights.at[layer, 0, pl.ds(0, geo.nz * geo.nu * self.rows)], self.send_v.at[layer, step - 1])
        drain(self.weights.at[layer, pl.ds(0, geo.nx)], self.send_s.at[layer])


class Scratch:
    def __init__(self):
        self.names, self.shapes = [], []

    def add(self, name, kind, *shape):
        self.names.append(name)
        self.shapes.append(pltpu.SemaphoreType.DMA(shape) if kind is None else pltpu.VMEM(shape, kind))

    def bind(self, refs):
        return dict(zip(self.names, refs, strict=True))


class Sizes:
    def __init__(self, geo, layers, streams, span, width, rows, docs):
        self.layers, self.streams, self.span, self.width = layers, streams, span, width
        self.rows, self.docs = rows, docs
        self.tokens = streams * span
        self.hid, self.ffn = H // geo.n_batch, FF // geo.n_batch
        self.block = 4 * self.hid + 2 * self.ffn
        self.vec = 2 * width + 2 * H


def make_scratch(geo, sz):
    layers, tokens, width, rows, hid, ffn = sz.layers, sz.tokens, sz.width, sz.rows, sz.hid, sz.ffn
    nb, nx, ny, nz, n_seq = geo.n_batch, geo.nx, geo.ny, geo.nz, geo.n_seq
    half, most = width // 2, max(ffn // rows - 1, 1)
    s = Scratch()
    add = s.add
    add("weights", BF16, layers, nb, sz.block, width)
    add("resid", F32, layers + 1, tokens, width)
    for name in ("fgate", "igate", "cand", "states"):
        add(name, F32, layers, nb, tokens, hid)
    add("slope", F32, layers, nb, tokens, ffn)
    add("middle", F32, layers, tokens, width)
    add("gated", BF16, layers, 2 * tokens, width)
    add("normed", BF16, layers, 2 * tokens, width)
    add("states_low", BF16, layers, nx, 2 * tokens, hid)
    add("active", BF16, layers, nx, 2 * tokens, ffn)
    add("ginner", BF16, nx, 2 * tokens, ffn)
    add("gmlp", BF16, 2 * tokens, width)
    add("gy", BF16, 2 * tokens, width)
    add("ggate", BF16, 3, nx, 2 * tokens, hid)
    add("states_out", BF16, nx, tokens, hid)
    add("active_out", BF16, nx, tokens, ffn)
    add("ginner_out", BF16, nx, tokens, ffn)
    add("ggate_out", BF16, 3, nx, tokens, hid)
    add("carry_in", F32, layers, nb, sz.streams, hid)
    add("incoming", F32, nb, sz.streams, hid)
    for name in ("prods", "gstates", "deltas"):
        add(name, F32, nb, tokens, hid)
    add("mask", F32, tokens, 128)
    add("summary", F32, 2 * layers, nb, 2 * sz.streams, hid)
    add("mailbox", F32, 2 * layers, n_seq, nb, 2 * sz.streams, hid)
    add("dgrad", F32, tokens, width)
    add("acc", F32, tokens, width)
    add("wide", F32, tokens, ffn)
    add("gains", F32, layers, 2, width)
    add("biases", F32, layers, nb, 2, hid)
    add("ggains", F32, layers, 2, width)
    add("gbiases", F32, layers, nb, 2, hid)
    add("landing", BF16, nx, sz.block, width)
    add("landing_below", BF16, layers, rows, width)
    add("low_moments", BF16, layers, rows, width)
    add("gram_out", BF16, 3, 3, half, half)
    add("gram_s", BF16, 1, 3, half, half)
    add("gram_x", BF16, nx - 1, 3, half, half)
    add("gram_g", BF16, most, 3, half, half)
    add("square_own", F32, layers, 8, 128)
    add("square_out", F32, 3, 8, 128)
    add("square_s", F32, 1, 8, 128)
    add("square_x", F32, nx - 1, 8, 128)
    add("square_g", F32, most, 8, 128)
    add("odd", F32, width, width)
    add("polys", BF16, layers, 2, width, width)
    add("inverses", F32, layers, 8, 128)
    add("vec_out", F32, 3, layers, sz.vec)
    add("vec_s", F32, 1, layers, sz.vec)
    add("vec_x", F32, nx, layers, sz.vec)
    add("vec_q", F32, n_seq, layers, sz.vec)
    for name, shape in (
        ("load", (4,)),
        ("send_z", (layers, 4 * nz, geo.nu)),
        ("send_u", (layers, 2, geo.nu - 1)),
        ("send_v", (layers, geo.nv - 1)),
        ("send_s", (layers,)),
        ("recv", (layers * 2 * nz * geo.nu * geo.nv,)),
        ("recv_s", (layers,)),
        ("mail_send", (2 * layers, n_seq)),
        ("mail_recv", (2 * layers, n_seq)),
        ("gated_send", (layers,)),
        ("gated_recv", (layers,)),
        ("normed_send", (layers,)),
        ("normed_recv", (layers,)),
        ("states_send", (nx,)),
        ("states_recv", (layers, nx)),
        ("active_send", (nx,)),
        ("active_recv", (layers, nx)),
        ("gmlp_send", (1,)),
        ("gmlp_recv", (1,)),
        ("gy_send", (1,)),
        ("gy_recv", (1,)),
        ("ginner_send", (nx,)),
        ("ginner_recv", (nx,)),
        ("ggate_send", (3, nx)),
        ("ggate_recv", (3, nx)),
        ("sum_send_x", (layers, nx - 1, n_seq)),
        ("sum_send_y", (layers, ny - 1)),
        ("sum_send_z", (layers, nz, PIECES)),
        ("sum_recv_x", (layers, nx - 1, n_seq)),
        ("sum_recv_y", (layers, ny - 1, nz)),
        ("sum_recv_z", (layers, nz + 1, PIECES)),
        ("block_send_z", (layers, 2, nz, PIECES)),
        ("block_send_y", (layers, ny - 1)),
        ("block_recv", (layers, n_seq, PIECES)),
        ("block_own", (layers,)),
        ("gram_send_s", (2,)),
        ("gram_send_x", (2, nx - 1)),
        ("gram_send_g", (2, most)),
        ("gram_recv_s", (2,)),
        ("gram_recv_x", (2, nx - 1)),
        ("gram_recv_g", (2, most)),
        ("poly_send", (2,)),
        ("poly_recv", (2,)),
        ("vec_send_s", (1,)),
        ("vec_send_x", (nx,)),
        ("vec_send_q", (n_seq,)),
        ("vec_recv_s", (1,)),
        ("vec_recv_x", (nx,)),
        ("vec_recv_q", (n_seq,)),
        ("store", (4,)),
    ):
        add(name, None, *shape)
    for name in ("credit_mlp", "credit_gate", "credit_x", "credit_y", "credit_z"):
        s.names.append(name)
        s.shapes.append(pltpu.SemaphoreType.REGULAR)
    return s

WINDOW = 3
PIECES = 2
DELAYS = (1, 2, 3, 2)
PUMPS = ((1, 1, 1, 1, 1), (2, 1, 1, 1, 1))


def step_kernel(
    geo, sz, names, mats_ref, old_ref, x_ref, out_grad_ref, doc_ref, vec_ref, vmom_ref, vavg_ref,
    act_ref, dx_ref, shard_ref, block_ref, ortho_ref, vgrad_ref, new_vmom_ref, new_vec_ref, new_vavg_ref, *scratch
):
    r = type("Refs", (), names.bind(scratch))
    layers, streams, span, width, rows = sz.layers, sz.streams, sz.span, sz.width, sz.rows
    tokens, hid, ffn = sz.tokens, sz.hid, sz.ffn
    nb, nx, ny, nz, n_seq = geo.n_batch, geo.nx, geo.ny, geo.nz, geo.n_seq
    seq, batch, z, y, x, core = geo.here()
    sibling = (seq, x * 2 + 1 - core)
    tile, half, groups = 32, width // 2, span // 8
    weights = r.weights
    at_out, at_up, at_down = 3 * hid, 4 * hid, 4 * hid + ffn
    own_part, far_part = slice(0, tokens), slice(tokens, 2 * tokens)

    def rows_at(k, size):
        return pl.ds(pl.multiple_of(k * size, size), size)

    def each_tile(body):
        count(0, tokens // tile, lambda k: body(rows_at(k, tile)))

    barrier = pltpu.get_barrier_semaphore()

    def greet(seq_id, batch_id):
        pl.semaphore_signal(barrier, inc=1, device_id=(seq_id, batch_id), device_id_type=MESH)

    for step in range(1, n_seq):
        greet(other(seq, step, n_seq), batch)
    for step in range(1, nx):
        greet(seq, other(x, step, nx) * 2 + core)
    greet(*sibling)
    for layer in range(layers):
        pltpu.make_async_copy(
            mats_ref.at[layer, 0], r.resid.at[layer, pl.ds(0, rows)], r.load.at[layer]
        ).start()
    for layer in range(layers):
        pltpu.make_async_copy(
            mats_ref.at[layer, 0], r.resid.at[layer, pl.ds(0, rows)], r.load.at[layer]
        ).wait()
        weights[layer, batch, rows_at(seq, rows), :] = r.resid[layer, 0:rows, :].astype(BF16)
    pl.semaphore_wait(barrier, n_seq - 1 + nx - 1 + 1)

    gather = Gather(geo, weights, rows, r)
    gather_steps = gather.steps(layers)

    def advance(steps):
        for _ in range(min(steps, len(gather_steps))):
            gather.step(*gather_steps.pop(0))

    def need(layer):
        while any(step[0] == layer for step in gather_steps):
            advance(1)
        gather.ready(layer)

    advance(1)

    def each_piece(body):
        for layer in range(layers):
            for k in range(2):
                body(slice(layer, layer + 1), slice(k * width, (k + 1) * width), k, r.gains, r.ggains, (layer,))
                for b in range(nb):
                    first = 2 * width + k * H + b * hid
                    body(slice(layer, layer + 1), slice(first, first + hid), k, r.biases, r.gbiases, (layer, b))

    def read_piece(row, columns, k, kept, made, at):
        kept[(*at, slice(k, k + 1), slice(None))] = vec_ref[row, columns]

    def write_piece(row, columns, k, kept, made, at):
        r.vec_out[0, row, columns] = made[(*at, slice(k, k + 1), slice(None))]

    each_piece(read_piece)
    for stream in range(streams):
        position = seq * span + lax.broadcasted_iota(jnp.int32, (span, 128), 0)
        begin, keep = jnp.int32(0), jnp.ones((span, 128), F32)
        for doc in range(sz.docs):
            keep = jnp.where(position == begin, 0.0, keep)
            begin = begin + doc_ref[stream, doc]
        r.mask[stream * span : (stream + 1) * span, :] = keep

    def load_input(at):
        r.resid[0, at, :] = x_ref[at, :].astype(F32)

    each_tile(load_input)

    def give(src, dst, send, recv):
        remote(src, dst, send, recv, sibling).start()

    def given(dst, recv):
        remote(dst, dst, r.gmlp_send.at[0], recv, sibling).wait_recv()

    def gone(src, send):
        remote(src, src, send, r.gmlp_recv.at[0], sibling).wait_send()

    def blocks(k):
        f = other(x, k + 1, nx)
        return f, 2 * f + core, 2 * f + 1 - core

    def mail(number, forward):
        first, last = (seq + 1, n_seq) if forward else (0, seq)

        def copy(peer, source):
            return remote(
                r.summary.at[number], r.mailbox.at[number, source], r.mail_send.at[number, peer],
                r.mail_recv.at[number, source], (peer, batch),
            )

        hops = seq if forward else n_seq - 1 - seq

        def fold(k, before):
            source = k if forward else n_seq - 1 - k
            copy(source, source).wait_recv()
            packed = r.mailbox[number, source]
            return packed[:, streams:] + packed[:, 0:streams] * before

        def post():
            count(first, last, lambda peer: copy(peer, seq).start())

        def collect():
            total = lax.fori_loop(0, hops, fold, jnp.zeros((nb, streams, hid), F32))
            count(first, last, lambda peer: copy(peer, seq).wait_send())
            return total

        return post, collect

    row8 = lax.broadcasted_iota(jnp.int32, (8, hid), 0)
    start_scan = tuple((jnp.ones((1, hid), F32), jnp.zeros((1, hid), F32)) for _ in range(streams))

    def in_fours(group):
        def four(k, carried):
            for step in range(4):
                carried = group(k * 4 + step, carried)
            return carried

        return lax.fori_loop(0, groups // 4, four, start_scan)

    def put_summary(number, b, last):
        for stream in range(streams):
            r.summary[number, b, stream : stream + 1, :] = last[stream][0]
            r.summary[number, b, streams + stream : streams + stream + 1, :] = last[stream][1]

    def forward(layer, pumps):
        gain_one, gain_two = r.gains[layer, 0:1, :], r.gains[layer, 1:2, :]

        def norm_one(at):
            values = r.resid[layer, at, :]
            scale = lax.rsqrt(jnp.mean(values * values, axis=-1, keepdims=True) + EPSILON)
            r.gated[layer, at, :] = (values * scale * gain_one).astype(BF16)

        each_tile(norm_one)
        near = r.gated.at[layer, own_part]
        give(near, r.gated.at[layer, far_part], r.gated_send.at[layer], r.gated_recv.at[layer])
        need(layer)

        def front(b):
            source = r.gated[layer, own_part, :]
            r.wide[:, 0:hid] = dot_nt(source, weights[layer, b, 0:hid, :]) + r.biases[layer, b, 0:1, :]
            r.wide[:, hid : 2 * hid] = dot_nt(source, weights[layer, b, hid : 2 * hid, :]) + r.biases[layer, b, 1:2, :]
            r.cand[layer, b] = dot_nt(source, weights[layer, b, 2 * hid : at_out, :])

            def group(k, carried):
                new = []
                for stream in range(streams):
                    at = pl.ds(pl.multiple_of(stream * span + k * 8, 8), 8)
                    f, i = sigmoid(r.wide[at, 0:hid]), sigmoid(r.wide[at, hid : 2 * hid])
                    share = 1.0 / (f + i)
                    decay = f * share * widen(r.mask[at, :], hid)
                    term = i * share * r.cand[layer, b, at, :]
                    r.fgate[layer, b, at, :] = f
                    r.igate[layer, b, at, :] = i
                    for step in (1, 2, 4):
                        reach = row8 >= step
                        term = term + decay * jnp.where(reach, pltpu.roll(term, step, 0), 0.0)
                        decay = decay * jnp.where(reach, pltpu.roll(decay, step, 0), 1.0)
                    prod_in, state_in = carried[stream]
                    term = term + decay * state_in
                    decay = decay * prod_in
                    r.states[layer, b, at, :] = term
                    r.prods[b, at, :] = decay
                    new.append((decay[7:8], term[7:8]))
                return tuple(new)

            put_summary(layer, b, in_fours(group))

        count(0, nb // 2, front)
        pumps[0]()
        count(nb // 2, nb, front)
        post, collect = mail(layer, True)
        post()
        pumps[1]()
        r.carry_in[layer] = collect()
        r.acc[...] = jnp.zeros_like(r.acc)

        def rear(k):
            f, b_own, b_far = blocks(k)

            def states_of(b, put):
                for stream in range(streams):
                    at = slice(stream * span, (stream + 1) * span)
                    full = r.states[layer, b, at, :] + r.prods[b, at, :] * r.carry_in[layer, b, stream : stream + 1, :]
                    r.states[layer, b, at, :] = full
                    put(at, full.astype(BF16))

            def put_far(at, low):
                r.states_out[f, at, :] = low

            def put_own(at, low):
                r.states_low[layer, f, at, :] = low

            states_of(b_far, put_far)
            give(
                r.states_out.at[f], r.states_low.at[layer, f, far_part], r.states_send.at[f],
                r.states_recv.at[layer, f],
            )
            states_of(b_own, put_own)
            r.acc[...] += dot_nn(r.states_out[f], weights[layer, b_far, at_out:at_up, :]) + dot_nn(
                r.states_low[layer, f, own_part, :], weights[layer, b_own, at_out:at_up, :]
            )

        count(0, nx, rear)
        pumps[2]()

        def norm_two(at):
            values = r.resid[layer, at, :] + r.acc[at, :]
            r.middle[layer, at, :] = values
            scale = lax.rsqrt(jnp.mean(values * values, axis=-1, keepdims=True) + EPSILON)
            r.normed[layer, at, :] = (values * scale * gain_two).astype(BF16)

        each_tile(norm_two)
        near = r.normed.at[layer, own_part]
        give(near, r.normed.at[layer, far_part], r.normed_send.at[layer], r.normed_recv.at[layer])
        r.acc[...] = r.middle[layer]


        def mlp(k):
            f, b_own, b_far = blocks(k)

            def active_of(b, put):
                r.wide[...] = dot_nt(r.normed[layer, own_part, :], weights[layer, b, at_up:at_down, :])

                def act(at):
                    v = r.wide[at, :]
                    square = v * v
                    t = jnp.tanh(GELU_A * (v + GELU_B * (v * square)))
                    share = 0.5 * (1.0 + t)
                    put(at, (v * share).astype(BF16))
                    r.slope[layer, b, at, :] = share + 0.5 * v * (1.0 - t * t) * (
                        GELU_A * (1.0 + 3.0 * GELU_B * square)
                    )

                each_tile(act)

            def put_far(at, low):
                r.active_out[f, at, :] = low

            def put_own(at, low):
                r.active[layer, f, at, :] = low

            active_of(b_far, put_far)
            give(r.active_out.at[f], r.active.at[layer, f, far_part], r.active_send.at[f], r.active_recv.at[layer, f])
            r.acc[...] += dot_nn(r.active_out[f], weights[layer, b_far, at_down:, :])
            active_of(b_own, put_own)
            r.acc[...] += dot_nn(r.active[layer, f, own_part, :], weights[layer, b_own, at_down:, :])

        count(0, nx - 1, mlp)
        pumps[3]()
        count(nx - 1, nx, mlp)
        pumps[4]()
        r.resid[layer + 1] = r.acc[...]
        gone(r.gated.at[layer, own_part], r.gated_send.at[layer])
        gone(r.normed.at[layer, own_part], r.normed_send.at[layer])
        for f in range(nx):
            gone(r.states_out.at[f], r.states_send.at[f])
            gone(r.active_out.at[f], r.active_send.at[f])

    u, v = gather.u, gather.v

    def at_device(z_at, u_at, v_at):
        y_at, x_at = geo.to_yx(u_at, v_at, core)
        return (geo.seq_of(z_at, y_at), 2 * x_at + core)

    def landing_at(layer, j, at):
        blk, first = j // n_seq, pl.multiple_of(j % n_seq * rows, rows)
        part = pl.ds(pl.multiple_of(first + at[0], at[1]), at[1])
        if layer == layers - 1:
            return r.landing, (blk, part)
        return weights, (layer + 1, 2 * blk + 1 - core, part)

    def landing(layer, j):
        ref, index = landing_at(layer, j, (0, rows))
        return ref.at[index]

    base_y = (nx - 1) * n_seq
    base_z = base_y + (ny - 1) * nz
    below = None

    def credit(sem, peers):
        for device in peers:
            pl.semaphore_signal(sem, inc=1, device_id=device, device_id_type=MESH)

    taken = set()

    def take_credit(name, sem, layer, amount):
        if layer < layers - 1 and (name, layer) not in taken:
            taken.add((name, layer))
            pl.semaphore_wait(sem, amount)

    def slot(layer, z_at, u_at, v_at):
        s, b = at_device(z_at, u_at, v_at)
        return weights.at[layer, b, rows_at(s, rows)]

    z_groups = [[z_at for z_at in reversed(range(nz)) if z_at >= nz // 2], list(range(nz // 2))]
    order = [
        (z_at, du, dv)
        for group in z_groups
        for du in [*range(1, ny), 0]
        for z_at in group
        for dv in range(1, nx)
    ]
    per_layer, window = len(order), WINDOW

    def entry(idx):
        return order[idx]

    def leading(good):
        return next((n for n, one in enumerate(order) if not good(*one)), per_layer)

    def from_mlp(z_at):
        return all(geo.seq_of(z_at, y_at) * rows >= at_up for y_at in range(ny))

    started = (
        leading(lambda z_at, du, dv: du and from_mlp(z_at)),
        leading(lambda z_at, du, dv: from_mlp(z_at)),
        leading(lambda z_at, du, dv: du or from_mlp(z_at)),
        per_layer,
    )

    def copy_x(layer, idx):
        z_at, du, dv = entry(idx)
        u_at, v_at = other(u, du, ny), other(v, dv, nx)
        s = z_at * ny + u_at
        return remote(
            slot(layer, z_at, u_at, v_at), landing(layer, (dv - 1) * n_seq + s),
            r.sum_send_x.at[layer, dv - 1, z_at * ny + du], r.sum_recv_x.at[layer, dv - 1, s],
            at_device(z, u, v_at),
        )

    def from_x(z_at, u_at):
        return [(dv - 1) * n_seq + z_at * ny + u_at for dv in range(1, nx)]

    def arrival_x(layer, idx):
        z_at, du, dv = entry(idx)
        if dv < nx - 1:
            return
        u_at = other(u, du, ny)
        s = z_at * ny + u_at
        for dv in range(1, nx):
            part = landing(layer, (dv - 1) * n_seq + s)
            remote(part, part, r.sum_send_x.at[layer, 0, 0], r.sum_recv_x.at[layer, dv - 1, s], sibling).wait_recv()
        if du:
            add_up(layer, z_at, u_at, from_x(z_at, u_at))
            remote(
                slot(layer, z_at, u_at, v), landing(layer, base_y + (du - 1) * nz + z_at),
                r.sum_send_y.at[layer, du - 1], r.sum_recv_y.at[layer, du - 1, z_at], at_device(z, u_at, v),
            ).start()

    queue = [0, []]

    def place(g):
        return layers - 1 - g // per_layer, g % per_layer

    def plan(g, layer, z_at):
        far = max(z_at, nz - 1 - z_at)
        at = g + DELAYS[0]
        for distance in range(far, 0, -1):
            queue[1].append((at, functools.partial(sum_z, layer, z_at, distance), False))
            at += DELAYS[1]
        queue[1].append((at, functools.partial(own_sum, layer, z_at), False))
        at += DELAYS[2]
        for distance in range(1, far + 1):
            queue[1].append((at, functools.partial(spread_block, layer, z_at, distance), layer == 0))
            at += DELAYS[3]

    def x_steps(steps, layer=0, limit=per_layer + window):
        for _ in range(steps):
            g = queue[0]
            if g >= (layers - 1 - layer) * per_layer + limit:
                break
            if g >= window:
                copy_x(*place(g - window)).wait_send()
            if g < layers * per_layer:
                to, idx = place(g)
                if idx == 0:
                    take_credit("x", r.credit_x, to, nx - 1)
                    take_credit("y", r.credit_y, to, ny - 1)
                copy_x(to, idx).start()
            if g >= window:
                to, idx = place(g - window)
                arrival_x(to, idx)
                z_at, du, dv = order[idx]
                if not du and dv == nx - 1:
                    plan(g, to, z_at)
            queue[0] += 1
            run_events(g)

    def run_events(until, held=False):
        due = sorted((e for e in queue[1] if e[0] <= until and (held or not e[2])), key=lambda e: e[0])
        queue[1] = [e for e in queue[1] if not (e[0] <= until and (held or not e[2]))]
        for event in due:
            event[1]()

    def put_grad(layer, b, first, size, value):
        weights[layer, b, first : first + size, :] = value.astype(BF16)

    def backward(layer, pumps):
        gain_one, gain_two = r.gains[layer, 0:1, :], r.gains[layer, 1:2, :]

        def low_grad(at):
            r.gmlp[at, :] = r.dgrad[at, :].astype(BF16)

        each_tile(low_grad)
        take_credit("mlp", r.credit_mlp, layer, 1)
        give(r.gmlp.at[own_part], r.gmlp.at[far_part], r.gmlp_send.at[0], r.gmlp_recv.at[0])
        r.acc[...] = jnp.zeros_like(r.acc)

        def mlp(k):
            f, b_own, b_far = blocks(k)

            def inner_of(b, put):
                r.wide[...] = dot_nt(r.gmlp[own_part, :], weights[layer, b, at_down:, :])

                def act(at):
                    put(at, (r.wide[at, :] * r.slope[layer, b, at, :]).astype(BF16))

                each_tile(act)

            def put_far(at, low):
                r.ginner_out[f, at, :] = low

            def put_own(at, low):
                r.ginner[f, at, :] = low

            inner_of(b_far, put_far)
            give(r.ginner_out.at[f], r.ginner.at[f, far_part], r.ginner_send.at[f], r.ginner_recv.at[f])
            r.acc[...] += dot_nn(r.ginner_out[f], weights[layer, b_far, at_up:at_down, :])
            inner_of(b_own, put_own)
            r.acc[...] += dot_nn(r.ginner[f, own_part, :], weights[layer, b_own, at_up:at_down, :])

            @pl.when(k == 0)
            def _():
                given(r.gmlp.at[far_part], r.gmlp_recv.at[0])
                given(r.normed.at[layer, far_part], r.normed_recv.at[layer])

            given(r.active.at[layer, f, far_part], r.active_recv.at[layer, f])
            put_grad(layer, b_own, at_down, ffn, dot_tn(r.active[layer, f], r.gmlp[...]))
            given(r.ginner.at[f, far_part], r.ginner_recv.at[f])
            put_grad(layer, b_own, at_up, ffn, dot_tn(r.ginner[f], r.normed[layer]))

        count(0, nx - 1, mlp)
        pumps[0]()
        count(nx - 1, nx, mlp)
        gone(r.gmlp.at[own_part], r.gmlp_send.at[0])
        for f in range(nx):
            gone(r.ginner_out.at[f], r.ginner_send.at[f])
        if layer > 0:
            credit(r.credit_mlp, [sibling])
        pumps[1]()

        def norm_two(k, total):
            at = rows_at(k, tile)
            values, grad = r.middle[layer, at, :], r.acc[at, :]
            scale = lax.rsqrt(jnp.mean(values * values, axis=-1, keepdims=True) + EPSILON)
            unit = values * scale
            gunit = grad * gain_two
            full = r.dgrad[at, :] + scale * (gunit - unit * jnp.mean(gunit * unit, axis=-1, keepdims=True))
            r.dgrad[at, :] = full
            r.gy[at, :] = full.astype(BF16)
            return total + jnp.sum(grad * unit, axis=0, keepdims=True)

        row_sum = jnp.zeros((1, width), F32)
        r.ggains[layer, 1:2, :] = lax.fori_loop(0, tokens // tile, norm_two, row_sum)
        take_credit("gate", r.credit_gate, layer, 1)
        give(r.gy.at[own_part], r.gy.at[far_part], r.gy_send.at[0], r.gy_recv.at[0])
        number = layers + layer

        def front(k):
            f, b_own, b_far = blocks(k)

            def scan(b):
                r.gstates[b] = dot_nt(r.gy[own_part, :], weights[layer, b, at_out:at_up, :])

                def group(k, carried):
                    new = []
                    for stream in range(streams):
                        at = pl.ds(pl.multiple_of(stream * span + (groups - 1 - k) * 8, 8), 8)
                        f, i = r.fgate[layer, b, at, :], r.igate[layer, b, at, :]
                        decay = f * (1.0 / (f + i)) * widen(r.mask[at, :], hid)
                        term = decay * r.gstates[b, at, :]
                        for step in (1, 2, 4):
                            reach = row8 < 8 - step
                            term = term + decay * jnp.where(reach, pltpu.roll(term, 8 - step, 0), 0.0)
                            decay = decay * jnp.where(reach, pltpu.roll(decay, 8 - step, 0), 1.0)
                        prod_in, state_in = carried[stream]
                        term = term + decay * state_in
                        decay = decay * prod_in
                        r.deltas[b, at, :] = term
                        r.prods[b, at, :] = decay
                        new.append((decay[0:1], term[0:1]))
                    return tuple(new)

                put_summary(number, b, in_fours(group))

            scan(b_far)
            scan(b_own)

            @pl.when(k == 0)
            def _():
                given(r.gy.at[far_part], r.gy_recv.at[0])

            given(r.states_low.at[layer, f, far_part], r.states_recv.at[layer, f])
            put_grad(layer, b_own, at_out, hid, dot_tn(r.states_low[layer, f], r.gy[...]))

        count(0, nx, front)
        post, collect = mail(number, False)
        post()
        pumps[2]()
        r.incoming[...] = collect()
        r.acc[...] = jnp.zeros_like(r.acc)
        span_row = lax.broadcasted_iota(jnp.int32, (span, hid), 0)
        given(r.gated.at[layer, far_part], r.gated_recv.at[layer])

        def rear(k):
            f, b_own, b_far = blocks(k)

            def gates_of(b, put):
                sum_f, sum_i = jnp.zeros((1, hid), F32), jnp.zeros((1, hid), F32)
                for stream in range(streams):
                    at = slice(stream * span, (stream + 1) * span)
                    late = r.incoming[b, stream : stream + 1, :]
                    linked = r.deltas[b, at, :] + r.prods[b, at, :] * late
                    linked = jnp.where(span_row == span - 1, late, pltpu.roll(linked, span - 1, 0))
                    delta = r.gstates[b, at, :] + linked
                    early = r.carry_in[layer, b, stream : stream + 1, :]
                    before = jnp.where(span_row == 0, early, pltpu.roll(r.states[layer, b, at, :], 1, 0))
                    fg, ig = r.fgate[layer, b, at, :], r.igate[layer, b, at, :]
                    share = 1.0 / (fg + ig)
                    fshare, ishare = fg * share, ig * share
                    gap = delta * (before * widen(r.mask[at, :], hid) - r.cand[layer, b, at, :]) * fshare * ishare
                    gf = (gap * (1.0 - fg)).astype(BF16)
                    gi = (gap * (ig - 1.0)).astype(BF16)
                    put(at, (gf, gi, (delta * ishare).astype(BF16)))
                    sum_f = sum_f + jnp.sum(gf.astype(F32), axis=0, keepdims=True)
                    sum_i = sum_i + jnp.sum(gi.astype(F32), axis=0, keepdims=True)
                r.gbiases[layer, b, 0:1, :] = sum_f
                r.gbiases[layer, b, 1:2, :] = sum_i

            def put_far(at, lows):
                for member in range(3):
                    r.ggate_out[member, f, at, :] = lows[member]

            def put_own(at, lows):
                for member in range(3):
                    r.ggate[member, f, at, :] = lows[member]

            gates_of(b_far, put_far)
            for member in range(3):
                give(
                    r.ggate_out.at[member, f], r.ggate.at[member, f, far_part], r.ggate_send.at[member, f],
                    r.ggate_recv.at[member, f],
                )
            gates_of(b_own, put_own)
            total = r.acc[...]
            for member in range(3):
                at = slice(member * hid, (member + 1) * hid)
                total = total + dot_nn(r.ggate_out[member, f], weights[layer, b_far, at, :])
                total = total + dot_nn(r.ggate[member, f, own_part, :], weights[layer, b_own, at, :])
            r.acc[...] = total
            for member in range(3):
                given(r.ggate.at[member, f, far_part], r.ggate_recv.at[member, f])
                put_grad(layer, b_own, member * hid, hid, dot_tn(r.ggate[member, f], r.gated[layer]))

        count(0, nx - 1, rear)
        pumps[3]()
        count(nx - 1, nx, rear)
        gone(r.gy.at[own_part], r.gy_send.at[0])
        for f in range(nx):
            for member in range(3):
                gone(r.ggate_out.at[member, f], r.ggate_send.at[member, f])
        if layer > 0:
            credit(r.credit_gate, [sibling])
            credit(r.credit_x, [(seq, 2 * other(x, step, nx) + core) for step in range(1, nx)])
            credit(r.credit_y, [(geo.seq_of(z, other(y, step, ny)), batch) for step in range(1, ny)])
            for way, ends in ((1, z + 1 < nz), (-1, z >= 1)):

                @pl.when(ends)
                def _():
                    credit(r.credit_z, [(geo.seq_of(z + way, y), batch)])


        def norm_one(k, total):
            at = rows_at(k, tile)
            values, grad = r.resid[layer, at, :], r.acc[at, :]
            scale = lax.rsqrt(jnp.mean(values * values, axis=-1, keepdims=True) + EPSILON)
            unit = values * scale
            gunit = grad * gain_one
            full = r.dgrad[at, :] + scale * (gunit - unit * jnp.mean(gunit * unit, axis=-1, keepdims=True))
            r.dgrad[at, :] = full
            return total + jnp.sum(grad * unit, axis=0, keepdims=True)

        r.ggains[layer, 0:1, :] = lax.fori_loop(0, tokens // tile, norm_one, row_sum)
        if layer > 0:
            load_old(layer - 1).start()
        pumps[4]()

    def load_old(layer):
        return pltpu.make_async_copy(old_ref.at[layer, 0], r.resid.at[layer + 1, pl.ds(0, rows)], r.load.at[layer])

    part_rows = min(rows // PIECES, tile)
    piece_rows = rows // PIECES

    def total_of(layer, z_at, u_at, sources, first):
        s, b = at_device(z_at, u_at, v)
        total = weights[layer, b, pl.ds(pl.multiple_of(s * rows + first, part_rows), part_rows), :].astype(F32)
        for j in sources:
            if j is None:
                total = total + r.landing_below[layer, pl.ds(pl.multiple_of(first, part_rows), part_rows), :].astype(F32)
            else:
                ref, index = landing_at(layer, j, (first, part_rows))
                total = total + ref[(*index, slice(None))].astype(F32)
        return total

    def add_up(layer, z_at, u_at, sources, start=0, size=rows):
        s, b = at_device(z_at, u_at, v)

        def one(k):
            first = start + k * part_rows
            weights[layer, b, pl.ds(pl.multiple_of(s * rows + first, part_rows), part_rows), :] = total_of(
                layer, z_at, u_at, sources, first
            ).astype(BF16)

        count(0, size // part_rows, one)

    def from_y(z_at):
        return [base_y + (dy - 1) * nz + z_at for dy in range(1, ny)]

    def wait_y(layer, z_at):
        for dy in range(1, ny):
            part = landing(layer, base_y + (dy - 1) * nz + z_at)
            remote(
                part, part, r.sum_send_y.at[layer, dy - 1], r.sum_recv_y.at[layer, dy - 1, z_at], sibling
            ).wait_recv()

    def piece(ref, k):
        return ref.at[pl.ds(k * piece_rows, piece_rows)]

    def wait_z(layer, number, k):
        part = piece(r.landing_below.at[layer], k)
        remote(part, part, r.sum_send_z.at[layer, 0, k], r.sum_recv_z.at[layer, number, k], sibling).wait_recv()

    def sum_z(layer, z_at, distance):
        def step(z_here, way):
            if not 0 <= z_here < nz:
                return

            @pl.when(z == z_here)
            def _():
                sources = from_x(z_at, u) + from_y(z_at)
                wait_y(layer, z_at)
                inner = 0 <= z_here + way < nz
                if inner:
                    sources = sources + [base_z + z_at]
                to = z_here - way
                if way < 0 and to == z_at:
                    into, number = r.landing_below.at[layer], nz
                else:
                    into, number = landing(layer, base_z + z_at), z_at
                for k in range(PIECES):
                    if inner:
                        wait_z(layer, z_at, k)
                    add_up(layer, z_at, u, sources, k * piece_rows, piece_rows)
                    remote(
                        piece(slot(layer, z_at, u, v), k), piece(into, k), r.sum_send_z.at[layer, z_at, k],
                        r.sum_recv_z.at[layer, number, k], at_device(to, u, v),
                    ).start()

        if ("z", layer) not in taken:
            both = lax.convert_element_type(z + 1 < nz, jnp.int32) + lax.convert_element_type(z >= 1, jnp.int32)
            take_credit("z", r.credit_z, layer, both)
        step(z_at + distance, 1)
        step(z_at - distance, -1)

    def block_slot(layer, z_at, y_at):
        return block_ref.at[layer, rows_at(geo.seq_of(z_at, y_at), rows)]

    def block_arrival(layer, z_at, y_at, k):
        return r.block_recv.at[layer, geo.seq_of(z_at, y_at), k]

    def along_z(layer, z_at, k, go):
        for way, passes, to in (
            (0, jnp.logical_and(z_at <= z, z + 1 < nz), z + 1),
            (1, jnp.logical_and(z_at >= z, z >= 1), z - 1),
        ):
            sem = r.block_send_z.at[layer, way, z_at, k]

            @pl.when(passes)
            def _():
                go(to, sem)

    def pass_block(layer, z_at, part, k):
        into, arrival = piece(block_slot(layer, z_at, y), k), block_arrival(layer, z_at, y, k)
        along_z(
            layer, z_at, k,
            lambda to, sem: remote(part, into, sem, arrival, (geo.seq_of(to, y), batch)).start(),
        )
        for step in range(1, ny):
            remote(
                part, into, r.block_send_y.at[layer, step - 1], arrival, (geo.seq_of(z, other(y, step, ny)), batch)
            ).start()

    def wait_block(layer, z_at, y_at, k):
        part = piece(block_slot(layer, z_at, y_at), k)
        remote(part, part, r.block_send_y.at[layer, 0], block_arrival(layer, z_at, y_at, k), sibling).wait_recv()

    def spread_block(layer, z_at, distance):
        far_away = jnp.logical_or(z == z_at + distance, z == z_at - distance)

        @pl.when(far_away)
        def _():
            for k in range(PIECES):
                wait_block(layer, z_at, y, k)
                pass_block(layer, z_at, piece(block_slot(layer, z_at, y), k), k)

    def own_sum(layer, z_at):
        @pl.when(z == z_at)
        def _():
            wait_y(layer, z_at)
            sources = from_x(z_at, u) + from_y(z_at)
            if z_at < nz - 1:
                sources = sources + [base_z + z_at]
            if z_at > 0:
                sources = sources + [below]
            load_old(layer).wait()
            squares = jnp.zeros((1, width), F32)
            for k in range(PIECES):
                if z_at < nz - 1:
                    wait_z(layer, z_at, k)
                if z_at > 0:
                    wait_z(layer, nz, k)

                def one(n, squares):
                    first = k * piece_rows + n * part_rows
                    at = pl.ds(pl.multiple_of(first, part_rows), part_rows)
                    total = total_of(layer, z_at, u, sources, first)
                    r.middle[layer, at, :] = total
                    moment = MOMENTUM_DECAY * r.resid[layer + 1, at, :] + total
                    r.resid[layer + 1, at, :] = moment
                    r.low_moments[layer, at, :] = moment.astype(BF16)
                    return squares + jnp.sum(moment * moment, axis=0, keepdims=True)

                squares = lax.fori_loop(0, piece_rows // part_rows, one, squares)
                pass_block(layer, z_at, piece(r.low_moments.at[layer], k), k)
            r.square_own[layer] = jnp.broadcast_to(jnp.sum(squares, axis=1, keepdims=True), (8, 128))
            pltpu.make_async_copy(r.low_moments.at[layer], own_block(layer), r.block_own.at[layer]).start()
            pltpu.make_async_copy(
                r.middle.at[layer, pl.ds(0, rows)], shard_ref.at[layer], r.store.at[layer]
            ).start()

    def own_block(layer):
        return block_ref.at[layer, rows_at(seq, rows)]

    def finish_block(layer):
        for z_at in range(nz):
            for k in range(PIECES):
                count(1, ny, lambda step: wait_block(layer, z_at, other(y, step, ny), k))
        pltpu.make_async_copy(r.low_moments.at[layer], own_block(layer), r.block_own.at[layer]).wait()
        pltpu.make_async_copy(r.middle.at[layer, pl.ds(0, rows)], shard_ref.at[layer], r.store.at[layer]).wait()

    def vec_start():
        each_piece(write_piece)
        remote(r.vec_out.at[0], r.vec_s.at[0], r.vec_send_s.at[0], r.vec_recv_s.at[0], sibling).start()

    def vec_second():
        remote(r.vec_out.at[0], r.vec_s.at[0], r.vec_send_s.at[0], r.vec_recv_s.at[0], sibling).wait_recv()
        total = r.vec_out[0] + r.vec_s[0]
        r.vec_out[1] = total
        r.vec_x[x] = total
        for step in range(1, nx):
            x_at = other(x, step, nx)
            remote(
                r.vec_out.at[1], r.vec_x.at[x], r.vec_send_x.at[x_at], r.vec_recv_x.at[x], (seq, x_at * 2 + core)
            ).start()

    def vec_third():
        for step in range(1, nx):
            x_at = other(x, step, nx)
            remote(
                r.vec_out.at[1], r.vec_x.at[x_at], r.vec_send_x.at[x_at], r.vec_recv_x.at[x_at], sibling
            ).wait_recv()
        total = r.vec_x[0]
        for k in range(1, nx):
            total = total + r.vec_x[k]
        r.vec_out[2] = total
        r.vec_q[seq] = total

        def one(k):
            to = other(seq, k, n_seq)
            remote(r.vec_out.at[2], r.vec_q.at[seq], r.vec_send_q.at[to], r.vec_recv_q.at[seq], (to, batch)).start()

        count(1, n_seq, one)

    def vec_last():
        def one(k):
            source = other(seq, k, n_seq)
            remote(
                r.vec_out.at[2], r.vec_q.at[source], r.vec_send_q.at[source], r.vec_recv_q.at[source], sibling
            ).wait_recv()

        count(1, n_seq, one)
        total = lax.fori_loop(1, n_seq, lambda k, t: t + r.vec_q[k], r.vec_q[0])
        vgrad_ref[...] = total
        new_vmom_ref[...] = MOMENTUM_DECAY * vmom_ref[...] + total
        first = 0
        for member, length in enumerate((width, width, H, H)):
            at = slice(first, first + length)
            segment = new_vmom_ref[:, at]
            scale = lax.rsqrt(jnp.mean(segment * segment, axis=1, keepdims=True) + 1e-06)
            fresh = vec_ref[:, at] - SEGMENT_RATES[member] * segment * scale
            new_vec_ref[:, at] = fresh
            new_vavg_ref[:, at] = AVERAGE_DECAY * vavg_ref[:, at] + (1.0 - AVERAGE_DECAY) * fresh
            first += length

    hid_devices, ffn_devices = hid // rows, ffn // rows
    in_group = jnp.where(seq < 4 * hid_devices, hid_devices, ffn_devices)
    rank = lax.rem(seq, in_group)
    group_first = seq - rank

    def pack_gram(stage, value):
        r.gram_out[stage, 0] = value[0:half, 0:half].astype(BF16)
        r.gram_out[stage, 1] = value[0:half, half:].astype(BF16)
        r.gram_out[stage, 2] = value[half:, half:].astype(BF16)

    def gram_pair(stage, into, squares_into, sends, recvs, device):
        return (
            remote(r.gram_out.at[stage], into, sends[0], recvs[0], device),
            remote(r.square_out.at[stage], squares_into, sends[1], recvs[1], device),
        )

    def gram_round(stage, parts, squares):
        for n in range(3):
            total = r.gram_out[stage, n].astype(F32)
            for ref in parts:
                total = total + ref[n].astype(F32)
            r.gram_out[stage + 1, n] = total.astype(BF16)
        total = r.square_out[stage]
        for ref in squares:
            total = total + ref[...]
        r.square_out[stage + 1] = total

    def group_copies(k):
        here_at = lax.rem(rank - k - 1 + in_group, in_group)
        return gram_pair(
            2, r.gram_g.at[here_at], r.square_g.at[here_at],
            (r.gram_send_g.at[0, here_at], r.gram_send_g.at[1, here_at]),
            (r.gram_recv_g.at[0, here_at], r.gram_recv_g.at[1, here_at]), (group_first + k, batch),
        )

    def even():
        return jnp.concatenate([r.acc[...], r.resid[0]], axis=0)

    def put_even(value):
        r.acc[...] = value[0:half]
        r.resid[0] = value[half:]

    def newton_schulz(pumps):
        mine, theirs = core, 1 - core
        pack_gram(0, dot_tn(r.low_moments[theirs], r.low_moments[theirs]))
        r.square_out[0] = r.square_own[theirs]
        to_core = gram_pair(
            0, r.gram_s.at[0], r.square_s.at[0], (r.gram_send_s.at[0], r.gram_send_s.at[1]),
            (r.gram_recv_s.at[0], r.gram_recv_s.at[1]), sibling,
        )
        for copy in to_core:
            copy.start()
        put_even(dot_tn(r.low_moments[mine], r.low_moments[mine]))
        for copy in to_core:
            copy.wait()
        pack_gram(0, even())
        r.square_out[0] = r.square_own[mine]
        gram_round(0, [r.gram_s.at[0]], [r.square_s.at[0]])
        to_x = []
        for step in range(1, nx):
            to_x += gram_pair(
                1, r.gram_x.at[step - 1], r.square_x.at[step - 1],
                (r.gram_send_x.at[0, step - 1], r.gram_send_x.at[1, step - 1]),
                (r.gram_recv_x.at[0, step - 1], r.gram_recv_x.at[1, step - 1]),
                (seq, other(x, step, nx) * 2 + core),
            )
        for copy in to_x:
            copy.start()
        pumps[0]()
        for copy in to_x:
            copy.wait()
        gram_round(1, [r.gram_x.at[k] for k in range(nx - 1)], [r.square_x.at[k] for k in range(nx - 1)])

        def to_member(k):
            for copy in group_copies(lax.rem(rank + k, in_group)):
                copy.start()

        def from_member(k):
            k = k - 1
            remote(r.gram_out.at[2], r.gram_g.at[k], r.gram_send_g.at[0, k], r.gram_recv_g.at[0, k], sibling).wait()
            remote(
                r.square_out.at[2], r.square_g.at[k], r.gram_send_g.at[1, k], r.gram_recv_g.at[1, k], sibling
            ).wait()

        count(1, in_group, to_member)
        pumps[1]()
        count(1, in_group, from_member)
        square = lax.fori_loop(1, in_group, lambda k, t: t + r.square_g[k - 1], r.square_out[2])
        inverse = 1.0 / (jnp.sqrt(square) + 1e-07)
        r.inverses[mine] = inverse
        scale = inverse[0:1, 0:1] * inverse[0:1, 0:1]

        def corner(n):
            total = r.gram_out[2, n].astype(F32)
            return lax.fori_loop(1, in_group, lambda k, t: t + r.gram_g[k - 1, n].astype(F32), total) * scale

        r.acc[:, 0:half] = corner(0)
        r.acc[:, half:] = corner(1)
        r.resid[0, :, 0:half] = r.acc[:, half:].T
        r.resid[0, :, half:] = corner(2)

        def polynomial(step):
            low = even().astype(BF16)
            r.polys[mine, step] = (QUINTIC[1] * even() + QUINTIC[2] * dot_nn(low, low)).astype(BF16)

        def precise(low, value):
            high = value.astype(BF16)
            rest = (value - high.astype(F32)).astype(BF16)
            return dot_nn(low, high) + dot_nn(low, rest)

        polynomial(0)
        lead = QUINTIC[0]
        poly = r.polys[mine, 0]
        r.odd[...] = precise(poly, even())
        put_even(lead * lead * even() + 2.0 * lead * r.odd[...] + precise(poly, r.odd[...]))
        polynomial(1)
        out = (
            remote(r.polys.at[mine], r.polys.at[mine], r.poly_send.at[0], r.poly_recv.at[0], sibling),
            remote(r.inverses.at[mine], r.inverses.at[mine], r.poly_send.at[1], r.poly_recv.at[1], sibling),
        )
        for copy in out:
            copy.start()

        def apply(layer):
            begin = (r.resid[layer + 1, 0:rows, :] * r.inverses[layer, 0:1, 0:1]).astype(BF16)
            for step in range(NS_STEPS):
                begin = (lead * begin.astype(F32) + dot_nn(begin, r.polys[layer, step])).astype(BF16)
            ortho_ref[layer] = begin

        apply(mine)
        for copy in out:
            copy.wait_send()
        remote(r.polys.at[theirs], r.polys.at[theirs], r.poly_send.at[0], r.poly_recv.at[0], sibling).wait_recv()
        remote(
            r.inverses.at[theirs], r.inverses.at[theirs], r.poly_send.at[1], r.poly_recv.at[1], sibling
        ).wait_recv()
        apply(theirs)

    def ahead(steps):
        return lambda: advance(steps)

    def nothing():
        pass

    for layer in range(layers):
        forward(layer, [ahead(1)] * 5)
    for layer in range(layers):
        gather.finish(layer)

    def turn(at):
        act_ref[at, :] = r.resid[layers, at, :].astype(BF16)
        r.dgrad[at, :] = out_grad_ref[at, :].astype(F32)

    each_tile(turn)
    load_old(layers - 1).start()

    def starts(layer):
        limits = (started[0], started[1], started[1], started[2], started[3])
        wanted = PUMPS[layer == layers - 1]
        return [
            functools.partial(x_steps, n * max(per_layer // 8, 1), layer, limit)
            for n, limit in zip(wanted, limits, strict=True)
        ]

    share = max(per_layer // 8, 1)
    for layer in reversed(range(layers)):
        backward(layer, starts(layer))
    out_dx = pltpu.make_async_copy(r.dgrad, dx_ref, r.store.at[layers])
    out_dx.start()
    vec_start()
    x_steps(share)
    vec_second()
    x_steps(share)
    vec_third()
    x_steps(layers * per_layer + window)
    end = max(event[0] for event in queue[1] if not event[2])
    run_events(end)
    held = sorted({event[0] for event in queue[1]})
    cut = held[len(held) // 2]
    newton_schulz([lambda: run_events(cut, True), lambda: run_events(held[-1], True)])
    vec_last()
    for layer in range(layers):
        finish_block(layer)
    out_dx.wait()

    def drain(part, sem):
        remote(part, part, sem, r.vec_recv_s.at[0], sibling).wait_send()

    for layer in range(layers):
        for dy in range(1, ny):
            drain(weights.at[layer, 0, pl.ds(0, nz * rows)], r.sum_send_y.at[layer, dy - 1])
            drain(weights.at[layer, 0, pl.ds(0, nz * rows)], r.block_send_y.at[layer, dy - 1])
        for k in range(PIECES):
            part = piece(r.low_moments.at[layer], k)
            for z_at in range(nz):
                along_z(layer, z_at, k, lambda to, sem: drain(part, sem))

                @pl.when(z != z_at)
                def _():
                    drain(part, r.sum_send_z.at[layer, z_at, k])

    drain(r.vec_out.at[0], r.vec_send_s.at[0])
    for step in range(1, nx):
        drain(r.vec_out.at[1], r.vec_send_x.at[other(x, step, nx)])
    count(1, n_seq, lambda k: drain(r.vec_out.at[2], r.vec_send_q.at[other(seq, k, n_seq)]))


def run_step(geo, stream_in, out_grad, doc_lengths, mats, mat_momenta, vectors, vec_momenta, vec_averages):
    layers, _, rows, width = mats.shape
    streams, span, _ = stream_in.shape
    sz = Sizes(geo, layers, streams, span, width, rows, doc_lengths.shape[1])
    names = make_scratch(geo, sz)
    vmem, anywhere = pl.BlockSpec(memory_space=pltpu.VMEM), pl.BlockSpec(memory_space=pl.ANY)
    smem = pl.BlockSpec(memory_space=pltpu.SMEM)
    vec = jax.ShapeDtypeStruct(vectors.shape, F32)
    return pl.pallas_call(
        functools.partial(step_kernel, geo, sz, names),
        out_shape=(
            jax.ShapeDtypeStruct((sz.tokens, width), BF16),
            jax.ShapeDtypeStruct((sz.tokens, width), F32),
            jax.ShapeDtypeStruct((layers, rows, width), F32),
            jax.ShapeDtypeStruct((layers, sz.block, width), BF16),
            jax.ShapeDtypeStruct((layers, rows, width), BF16),
            vec, vec, vec, vec,
        ),
        in_specs=[anywhere, anywhere, vmem, vmem, smem, vmem, vmem, vmem],
        out_specs=(vmem, anywhere, anywhere, anywhere, vmem, vmem, vmem, vmem, vmem),
        scratch_shapes=names.shapes,
        compiler_params=pltpu.CompilerParams(
            collective_id=0, has_side_effects=True, vmem_limit_bytes=63 * 2**20
        ),
        name="step",
    )(
        mats, mat_momenta, stream_in.reshape(sz.tokens, width), out_grad.reshape(sz.tokens, width), doc_lengths,
        vectors, vec_momenta, vec_averages,
    )


def closing_kernel(
    small_rows, act, dx, shard, block, ortho, mats, averages, vgrad, vmom, vec, vavg,
    act_out, dx_out, shard_out, block_out, mats_out, averages_out, vgrad_out, vmom_out, vec_out, vavg_out,
):
    act_out[...] = act[...]
    dx_out[...] = dx[...]
    shard_out[:, 0] = shard[...]
    block_out[:, 0] = block[...].astype(F32)
    rows, width = mats_out.shape[2] * pl.num_programs(0), mats_out.shape[3]
    small = lax.axis_index("seq") * rows < small_rows
    factor = jnp.where(small, 0.2 * math.sqrt(max(H, width)), 0.2 * math.sqrt(max(FF, width)))
    fresh = mats[:, 0] - MATRIX_RATE * (ortho[...].astype(F32) * factor)
    mats_out[:, 0] = fresh
    averages_out[:, 0] = AVERAGE_DECAY * averages[:, 0] + (1.0 - AVERAGE_DECAY) * fresh
    vgrad_out[...] = vgrad[...]
    vmom_out[...] = vmom[...]
    vec_out[...] = vec[...]
    vavg_out[...] = vavg[...]


def run_closing(geo, act, dx, shard, block, ortho, mats, averages, vecs):
    layers, _, rows, width = mats.shape
    tokens, block_rows = act.shape[0], block.shape[1]
    grid = max(min(2, rows // 16), 1)

    def flat(count):
        return pl.BlockSpec((count // grid, width), lambda k: (k, 0))

    def deep(count):
        return pl.BlockSpec((layers, count // grid, width), lambda k: (0, k, 0))

    def boxed(count):
        return pl.BlockSpec((layers, 1, count // grid, width), lambda k: (0, 0, k, 0))

    vec = pl.BlockSpec(vecs[0].shape, lambda k: (0, 0))
    vec_shape = jax.ShapeDtypeStruct(vecs[0].shape, F32)
    box = jax.ShapeDtypeStruct(mats.shape, F32)
    return pl.pallas_call(
        functools.partial(closing_kernel, 4 * (H // geo.n_batch)),
        grid=(grid,),
        out_shape=(
            jax.ShapeDtypeStruct(act.shape, BF16),
            jax.ShapeDtypeStruct(dx.shape, F32),
            box,
            jax.ShapeDtypeStruct((layers, 1, block_rows, width), F32),
            box,
            box,
            *[vec_shape] * 4,
        ),
        in_specs=[
            flat(tokens), flat(tokens), deep(rows), deep(block_rows), deep(rows), boxed(rows), boxed(rows), *[vec] * 4
        ],
        out_specs=(
            flat(tokens), flat(tokens), boxed(rows), boxed(block_rows), boxed(rows), boxed(rows), *[vec] * 4
        ),
        compiler_params=pltpu.CompilerParams(vmem_limit_bytes=60 * 2**20),
        name="closing",
    )(act, dx, shard, block, ortho, mats, averages, *vecs)


def per_device(
    geo, stream_in, out_grad, doc_lengths, mats, mat_momenta, mat_averages, vectors, vec_momenta, vec_averages
):
    act, dx, shard, block, ortho, *vecs = run_step(
        geo, stream_in, out_grad, doc_lengths, mats, mat_momenta, vectors, vec_momenta, vec_averages
    )
    act, dx, *rest = run_closing(geo, act, dx, shard, block, ortho, mats, mat_averages, vecs)
    return (act.reshape(stream_in.shape), dx.reshape(stream_in.shape), *rest)


def solution(mesh):
    geo = Geometry(mesh.shape["seq"], mesh.shape["batch"])
    rows = P(None, "batch", "seq", None)
    tokens = P("batch", "seq", None)
    return jax.shard_map(
        functools.partial(per_device, geo),
        mesh=mesh,
        in_specs=(tokens, tokens, P("batch", None), rows, rows, rows, P(), P(), P()),
        out_specs=(tokens, tokens, rows, P(None, "batch", None, None), rows, rows, P(), P(), P(), P()),
        check_vma=False,
    )
```

```python
import functools
import math

import jax
import jax.numpy as jnp
from jax import lax
from jax.experimental import pallas as pl
from jax.experimental.pallas import tpu as pltpu
from jax.sharding import PartitionSpec as P

H = 1024
FF = 2048
NS_STEPS = 2
MESH = pl.DeviceIdType.MESH
F32 = jnp.float32
BF16 = jnp.bfloat16

EPSILON = 1e-05
MOMENTUM_DECAY = 0.5
AVERAGE_DECAY = 0.9
MATRIX_RATE = 0.3
SEGMENT_RATES = (0.3, 0.3, 0.5, 2.0)
QUINTIC = (3.4445, -4.775, 2.0315)
GELU_A = 0.7978845608
GELU_B = 0.044715


class Geometry:
    def __init__(self, n_seq, n_batch):
        self.n_seq, self.n_batch = n_seq, n_batch
        self.nz, self.ny, self.stride_z, self.stride_y = {
            8: (4, 2, 2, 1),
            32: (8, 4, 1, 8),
        }.get(n_seq, (n_seq, 1, 1, n_seq))
        self.nx = n_batch // 2
        self.swaps = self.ny == self.nx
        self.nu, self.nv = self.ny, self.nx

    def seq_of(self, z, y):
        return z * self.stride_z + y * self.stride_y

    def here(self):
        seq, batch = lax.axis_index("seq"), lax.axis_index("batch")
        z = seq // self.stride_z % self.nz
        y = seq // self.stride_y % self.ny
        return seq, batch, z, y, batch // 2, batch % 2

    def to_yx(self, u, v, core):
        if not self.swaps:
            return u, v
        return u + core * (v - u), v + core * (u - v)


def dot_nn(a, b):
    return lax.dot_general(a, b, (((1,), (0,)), ((), ())), preferred_element_type=F32)


def dot_nt(a, b):
    return lax.dot_general(a, b, (((1,), (1,)), ((), ())), preferred_element_type=F32)


def dot_tn(a, b):
    return lax.dot_general(a, b, (((0,), (0,)), ((), ())), preferred_element_type=F32)


def other(mine, step, count):
    return lax.rem(mine + step, count)


def sigmoid(values):
    return 1.0 / (1.0 + jnp.exp(-values))


def widen(column_tile, width):
    return jnp.concatenate([column_tile] * (width // 128), axis=1)


def count(first, last, body):
    lax.fori_loop(first, last, lambda k, _: body(k) or 0, 0)


def remote(src, dst, send, recv, device):
    return pltpu.make_async_remote_copy(
        src_ref=src, dst_ref=dst, send_sem=send, recv_sem=recv, device_id=device, device_id_type=MESH
    )


class Gather:
    def __init__(self, geo, weights, rows, refs):
        self.geo, self.weights, self.rows, self.half_rows = geo, weights, rows, rows // 2
        self.send_z, self.send_u, self.send_v, self.send_s = refs.send_z, refs.send_u, refs.send_v, refs.send_s
        self.recv, self.recv_s = refs.recv, refs.recv_s
        self.seq, self.batch, self.z, self.y, self.x, self.core = geo.here()
        if geo.swaps:
            self.u = self.y + self.core * (self.x - self.y)
            self.v = self.x + self.core * (self.y - self.x)
        else:
            self.u, self.v = self.y, self.x
        self.sibling = (self.seq, self.x * 2 + 1 - self.core)

    def part(self, layer, half, z, u, v):
        y, x = self.geo.to_yx(u, v, self.core)
        start = self.geo.seq_of(z, y) * self.rows + half * self.half_rows
        return self.weights.at[layer, x * 2 + self.core, pl.ds(pl.multiple_of(start, self.half_rows), self.half_rows)]

    def arrival(self, layer, half, z, u, v):
        geo = self.geo
        return self.recv.at[(((layer * 2 + half) * geo.nz + z) * geo.nu + u) * geo.nv + v]

    def device(self, z, u, v):
        y, x = self.geo.to_yx(u, v, self.core)
        return (self.geo.seq_of(z, y), x * 2 + self.core)

    def push(self, layer, half, z, u, device, send):
        part = self.part(layer, half, z, u, self.v)
        remote(part, part, send, self.arrival(layer, half, z, u, self.v), device).start()

    def arrived(self, layer, half, z, u, v):
        part = self.part(layer, half, z, u, v)
        remote(part, part, self.send_s.at[layer], self.arrival(layer, half, z, u, v), self.sibling).wait_recv()

    def along_z(self, layer, half, z, u, go):
        for way, passes, to in (
            (0, jnp.logical_and(z <= self.z, self.z + 1 < self.geo.nz), self.z + 1),
            (1, jnp.logical_and(z >= self.z, self.z >= 1), self.z - 1),
        ):
            sem = self.send_z.at[layer, (half * 2 + way) * self.geo.nz + z, u]

            @pl.when(passes)
            def _():
                go(to, sem)

    def to_z(self, layer, half, z, u):
        self.along_z(
            layer, half, z, u,
            lambda to, sem: self.push(layer, half, z, u, self.device(to, self.u, self.v), sem),
        )

    def to_u(self, layer, half, z):
        for step in range(1, self.geo.nu):
            self.push(
                layer, half, z, self.u, self.device(self.z, other(self.u, step, self.geo.nu), self.v),
                self.send_u.at[layer, half, step - 1],
            )

    def to_v(self, layer, half, z, u):
        for step in range(1, self.geo.nv):
            self.push(
                layer, half, z, u, self.device(self.z, self.u, other(self.v, step, self.geo.nv)),
                self.send_v.at[layer, step - 1],
            )

    def to_sibling(self, layer, half, z, u, v):
        part = self.part(layer, half, z, u, v)
        remote(part, part, self.send_s.at[layer], self.recv_s.at[layer], self.sibling).start()

    def begin(self, layer):
        for half in range(2):
            self.to_z(layer, half, self.z, self.u)
            self.to_u(layer, half, self.z)
            self.to_v(layer, half, self.z, self.u)
            self.to_sibling(layer, half, self.z, self.u, self.v)

        def one(k):
            u = other(self.u, k, self.geo.nu)
            self.arrived(layer, 1, self.z, u, self.v)
            self.to_z(layer, 1, self.z, u)
            self.to_v(layer, 1, self.z, u)
            self.to_sibling(layer, 1, self.z, u, self.v)

        count(1, self.geo.nu, one)

    def at_distance(self, distance, body):
        if distance == 0:
            body(self.z)
            return

        @pl.when(self.z >= distance)
        def _():
            body(self.z - distance)

        @pl.when(self.z + distance < self.geo.nz)
        def _():
            body(self.z + distance)

    def from_z(self, layer, z):
        self.arrived(layer, 0, z, self.u, self.v)
        self.to_z(layer, 0, z, self.u)
        self.to_u(layer, 0, z)
        self.to_v(layer, 0, z, self.u)
        self.to_sibling(layer, 0, z, self.u, self.v)

        def one(k):
            u = other(self.u, k, self.geo.nu)
            self.arrived(layer, 1, z, u, self.v)
            self.to_z(layer, 1, z, u)
            self.to_v(layer, 1, z, u)
            self.to_sibling(layer, 1, z, u, self.v)

        count(0, self.geo.nu, one)

    def from_u(self, layer, z):
        def one(k):
            u = other(self.u, k, self.geo.nu)
            self.arrived(layer, 0, z, u, self.v)
            self.to_v(layer, 0, z, u)
            self.to_sibling(layer, 0, z, u, self.v)

        count(1, self.geo.nu, one)

    def from_v(self, layer, z):
        def one(k):
            half = k % 2
            u = other(self.u, k // 2 // (self.geo.nv - 1), self.geo.nu)
            v = other(self.v, k // 2 % (self.geo.nv - 1) + 1, self.geo.nv)
            self.arrived(layer, half, z, u, v)
            self.to_sibling(layer, half, z, u, v)

        count(0, 2 * self.geo.nu * (self.geo.nv - 1), one)

    def step(self, layer, t):
        nz = self.geo.nz
        if t == 0:
            self.begin(layer)
        if 1 <= t < nz:
            self.at_distance(t, lambda z: self.from_z(layer, z))
        if 1 <= t <= nz:
            self.at_distance(t - 1, lambda z: self.from_u(layer, z))
        if 2 <= t <= nz + 1:
            self.at_distance(t - 2, lambda z: self.from_v(layer, z))

    def steps(self, layers):
        last = self.geo.nz + 1
        order = []
        for layer in range(layers):
            order += [(layer, t) for t in range(0 if layer == 0 else 1, last)]
            if layer + 1 < layers:
                order.append((layer + 1, 0))
            order.append((layer, last))
        return order

    def ready(self, layer):
        part = self.weights.at[layer, pl.ds(0, self.geo.nx)]
        remote(part, part, self.send_s.at[layer], self.recv_s.at[layer], self.sibling).wait_recv()

    def finish(self, layer):
        geo = self.geo

        def drain(part, sem):
            remote(part, part, sem, self.recv_s.at[layer], self.sibling).wait_send()

        one = self.part(layer, 0, self.z, self.u, self.v)
        for z in range(geo.nz):
            self.along_z(layer, 0, z, self.u, lambda to, sem: drain(one, sem))
            for u in range(geo.nu):
                self.along_z(layer, 1, z, u, lambda to, sem: drain(one, sem))
        for step in range(1, geo.nu):
            drain(self.weights.at[layer, 0, pl.ds(0, geo.nz * self.half_rows)], self.send_u.at[layer, 0, step - 1])
            drain(one, self.send_u.at[layer, 1, step - 1])
        for step in range(1, geo.nv):
            drain(self.weights.at[layer, 0, pl.ds(0, geo.nz * geo.nu * self.rows)], self.send_v.at[layer, step - 1])
        drain(self.weights.at[layer, pl.ds(0, geo.nx)], self.send_s.at[layer])


class Scratch:
    def __init__(self):
        self.names, self.shapes = [], []

    def add(self, name, kind, *shape):
        self.names.append(name)
        self.shapes.append(pltpu.SemaphoreType.DMA(shape) if kind is None else pltpu.VMEM(shape, kind))

    def bind(self, refs):
        return dict(zip(self.names, refs, strict=True))


class Sizes:
    def __init__(self, geo, layers, streams, span, width, rows, docs):
        self.layers, self.streams, self.span, self.width = layers, streams, span, width
        self.rows, self.docs = rows, docs
        self.tokens = streams * span
        self.hid, self.ffn = H // geo.n_batch, FF // geo.n_batch
        self.block = 4 * self.hid + 2 * self.ffn
        self.vec = 2 * width + 2 * H


def make_scratch(geo, sz):
    layers, tokens, width, rows, hid, ffn = sz.layers, sz.tokens, sz.width, sz.rows, sz.hid, sz.ffn
    nb, nx, ny, nz, n_seq = geo.n_batch, geo.nx, geo.ny, geo.nz, geo.n_seq
    half, most = width // 2, max(ffn // rows - 1, 1)
    s = Scratch()
    add = s.add
    add("weights", BF16, layers, nb, sz.block, width)
    add("resid", F32, layers + 1, tokens, width)
    for name in ("fgate", "igate", "cand", "states"):
        add(name, F32, layers, nb, tokens, hid)
    add("slope", F32, layers, nb, tokens, ffn)
    add("middle", F32, layers, tokens, width)
    add("gated", BF16, layers, 2 * tokens, width)
    add("normed", BF16, layers, 2 * tokens, width)
    add("states_low", BF16, layers, nx, 2 * tokens, hid)
    add("active", BF16, layers, nx, 2 * tokens, ffn)
    add("ginner", BF16, nx, 2 * tokens, ffn)
    add("gmlp", BF16, 2 * tokens, width)
    add("gy", BF16, 2 * tokens, width)
    add("ggate", BF16, 3, nx, 2 * tokens, hid)
    add("states_out", BF16, nx, tokens, hid)
    add("active_out", BF16, nx, tokens, ffn)
    add("ginner_out", BF16, nx, tokens, ffn)
    add("ggate_out", BF16, 3, nx, tokens, hid)
    add("carry_in", F32, layers, nb, sz.streams, hid)
    add("incoming", F32, nb, sz.streams, hid)
    for name in ("prods", "gstates", "deltas"):
        add(name, F32, nb, tokens, hid)
    add("mask", F32, tokens, 128)
    add("summary", F32, 2 * layers, nb, 2 * sz.streams, hid)
    add("mailbox", F32, 2 * layers, n_seq, nb, 2 * sz.streams, hid)
    add("dgrad", F32, tokens, width)
    add("acc", F32, tokens, width)
    add("wide", F32, tokens, ffn)
    add("gains", F32, layers, 2, width)
    add("biases", F32, layers, nb, 2, hid)
    add("ggains", F32, layers, 2, width)
    add("gbiases", F32, layers, nb, 2, hid)
    add("landing", BF16, nx, sz.block, width)
    add("landing_below", BF16, layers, rows, width)
    add("low_moments", BF16, layers, rows, width)
    add("gram_full", BF16, layers, 2, 3, half // 2, half)
    add("gram_out", BF16, layers, 2, 3, half // 2, half)
    add("gram_s", BF16, layers, 3, half // 2, half)
    add("gram_x", BF16, layers, nx - 1, 3, half // 2, half)
    add("gram_g", BF16, layers, most, 3, half // 2, half)
    add("gram_sum", F32, layers, 2, 3, half // 2, half)
    add("square_own", F32, layers, 8, 128)
    add("square_out", F32, layers, 2, 8, 128)
    add("square_s", F32, layers, 8, 128)
    add("square_x", F32, layers, nx - 1, 8, 128)
    add("square_g", F32, layers, most, 8, 128)
    add("odd", F32, width, width)
    add("vec_out", F32, 3, layers, sz.vec)
    add("vec_s", F32, 1, layers, sz.vec)
    add("vec_x", F32, nx, layers, sz.vec)
    add("vec_q", F32, n_seq, layers, sz.vec)
    for name, shape in (
        ("load", (4,)),
        ("send_z", (layers, 4 * nz, geo.nu)),
        ("send_u", (layers, 2, geo.nu - 1)),
        ("send_v", (layers, geo.nv - 1)),
        ("send_s", (layers,)),
        ("recv", (layers * 2 * nz * geo.nu * geo.nv,)),
        ("recv_s", (layers,)),
        ("mail_send", (2 * layers, n_seq)),
        ("mail_recv", (2 * layers, n_seq)),
        ("gated_send", (layers,)),
        ("gated_recv", (layers,)),
        ("normed_send", (layers,)),
        ("normed_recv", (layers,)),
        ("states_send", (nx,)),
        ("states_recv", (layers, nx)),
        ("active_send", (nx,)),
        ("active_recv", (layers, nx)),
        ("gmlp_send", (1,)),
        ("gmlp_recv", (1,)),
        ("gy_send", (1,)),
        ("gy_recv", (1,)),
        ("ginner_send", (nx,)),
        ("ginner_recv", (nx,)),
        ("ggate_send", (3, nx)),
        ("ggate_recv", (3, nx)),
        ("sum_send_x", (layers, nx - 1, n_seq)),
        ("sum_send_y", (layers, ny - 1)),
        ("sum_send_z", (layers, nz, PIECES)),
        ("sum_recv_x", (layers, nx - 1, n_seq)),
        ("sum_recv_y", (layers, ny - 1, nz)),
        ("sum_recv_z", (layers, nz + 1, PIECES)),
        ("block_send_z", (layers, 2, nz, PIECES)),
        ("block_send_y", (layers, ny - 1)),
        ("block_recv", (layers, n_seq, PIECES)),
        ("block_own", (layers,)),
        ("gram_send_s", (layers, 2)),
        ("gram_send_x", (layers, nx - 1, 2)),
        ("gram_send_g", (layers, most, 2)),
        ("gram_recv_s", (layers, 2)),
        ("gram_recv_x", (layers, nx - 1, 2)),
        ("gram_recv_g", (layers, most, 2)),
        ("gram_send_e", (layers,)),
        ("gram_recv_e", (layers,)),
        ("vec_send_s", (1,)),
        ("vec_send_x", (nx,)),
        ("vec_send_q", (n_seq,)),
        ("vec_recv_s", (1,)),
        ("vec_recv_x", (nx,)),
        ("vec_recv_q", (n_seq,)),
        ("store", (4,)),
    ):
        add(name, None, *shape)
    for name in ("credit_mlp", "credit_gate", "credit_x", "credit_y", "credit_z"):
        s.names.append(name)
        s.shapes.append(pltpu.SemaphoreType.REGULAR)
    return s

WINDOW = 3
PIECES = 2
CROSSED = 1
LAST_AHEAD = 16
NS_PLACES = (1, 2, 4, 6)
DELAYS = (1, 2, 3, 2)
PUMPS = ((1, 1, 1, 1, 1), (2, 1, 1, 1, 1))


def step_kernel(
    geo, sz, names, mats_ref, old_ref, x_ref, out_grad_ref, doc_ref, vec_ref, vmom_ref, vavg_ref,
    act_ref, dx_ref, shard_ref, block_ref, ortho_ref, vgrad_ref, new_vmom_ref, new_vec_ref, new_vavg_ref, *scratch
):
    r = type("Refs", (), names.bind(scratch))
    layers, streams, span, width, rows = sz.layers, sz.streams, sz.span, sz.width, sz.rows
    tokens, hid, ffn = sz.tokens, sz.hid, sz.ffn
    nb, nx, ny, nz, n_seq = geo.n_batch, geo.nx, geo.ny, geo.nz, geo.n_seq
    seq, batch, z, y, x, core = geo.here()
    sibling = (seq, x * 2 + 1 - core)
    tile, half, groups = 64, width // 2, span // 8
    weights = r.weights
    at_out, at_up, at_down = 3 * hid, 4 * hid, 4 * hid + ffn
    own_part, far_part = slice(0, tokens), slice(tokens, 2 * tokens)

    def rows_at(k, size):
        return pl.ds(pl.multiple_of(k * size, size), size)

    def each_tile(body):
        count(0, tokens // tile, lambda k: body(rows_at(k, tile)))

    barrier = pltpu.get_barrier_semaphore()

    def greet(seq_id, batch_id):
        pl.semaphore_signal(barrier, inc=1, device_id=(seq_id, batch_id), device_id_type=MESH)

    for step in range(1, n_seq):
        greet(other(seq, step, n_seq), batch)
    for step in range(1, nx):
        greet(seq, other(x, step, nx) * 2 + core)
    greet(*sibling)
    for layer in range(layers):
        pltpu.make_async_copy(
            mats_ref.at[layer, 0], r.resid.at[layer, pl.ds(0, rows)], r.load.at[layer]
        ).start()
    for layer in range(layers):
        pltpu.make_async_copy(
            mats_ref.at[layer, 0], r.resid.at[layer, pl.ds(0, rows)], r.load.at[layer]
        ).wait()
        weights[layer, batch, rows_at(seq, rows), :] = r.resid[layer, 0:rows, :].astype(BF16)
    pl.semaphore_wait(barrier, n_seq - 1 + nx - 1 + 1)

    gather = Gather(geo, weights, rows, r)
    gather_steps = gather.steps(layers)

    def advance(steps):
        for _ in range(min(steps, len(gather_steps))):
            gather.step(*gather_steps.pop(0))

    def need(layer):
        while any(step[0] == layer for step in gather_steps):
            advance(1)
        gather.ready(layer)

    advance(1)

    def each_piece(body):
        for layer in range(layers):
            for k in range(2):
                body(slice(layer, layer + 1), slice(k * width, (k + 1) * width), k, r.gains, r.ggains, (layer,))
                for b in range(nb):
                    first = 2 * width + k * H + b * hid
                    body(slice(layer, layer + 1), slice(first, first + hid), k, r.biases, r.gbiases, (layer, b))

    def read_piece(row, columns, k, kept, made, at):
        kept[(*at, slice(k, k + 1), slice(None))] = vec_ref[row, columns]

    def write_piece(row, columns, k, kept, made, at):
        r.vec_out[0, row, columns] = made[(*at, slice(k, k + 1), slice(None))]

    each_piece(read_piece)
    for stream in range(streams):
        position = seq * span + lax.broadcasted_iota(jnp.int32, (span, 128), 0)
        begin, keep = jnp.int32(0), jnp.ones((span, 128), F32)
        for doc in range(sz.docs):
            keep = jnp.where(position == begin, 0.0, keep)
            begin = begin + doc_ref[stream, doc]
        r.mask[stream * span : (stream + 1) * span, :] = keep

    def load_input(at):
        r.resid[0, at, :] = x_ref[at, :].astype(F32)

    each_tile(load_input)

    def give(src, dst, send, recv):
        remote(src, dst, send, recv, sibling).start()

    def given(dst, recv):
        remote(dst, dst, r.gmlp_send.at[0], recv, sibling).wait_recv()

    def gone(src, send):
        remote(src, src, send, r.gmlp_recv.at[0], sibling).wait_send()

    def blocks(k):
        f = other(x, k + 1, nx)
        return f, 2 * f + core, 2 * f + 1 - core

    def mail(number, forward):
        first, last = (seq + 1, n_seq) if forward else (0, seq)

        def copy(peer, source):
            return remote(
                r.summary.at[number], r.mailbox.at[number, source], r.mail_send.at[number, peer],
                r.mail_recv.at[number, source], (peer, batch),
            )

        hops = seq if forward else n_seq - 1 - seq

        def fold(k, before):
            source = k if forward else n_seq - 1 - k
            copy(source, source).wait_recv()
            packed = r.mailbox[number, source]
            return packed[:, streams:] + packed[:, 0:streams] * before

        def post():
            count(first, last, lambda peer: copy(peer, seq).start())

        def collect():
            total = lax.fori_loop(0, hops, fold, jnp.zeros((nb, streams, hid), F32))
            count(first, last, lambda peer: copy(peer, seq).wait_send())
            return total

        return post, collect

    row8 = lax.broadcasted_iota(jnp.int32, (8, hid), 0)
    start_scan = tuple((jnp.ones((1, hid), F32), jnp.zeros((1, hid), F32)) for _ in range(streams))

    def in_eights(group):
        def eight(k, carried):
            for step in range(8):
                carried = group(k * 8 + step, carried)
            return carried

        return lax.fori_loop(0, groups // 8, eight, start_scan)

    def put_summary(number, b, last):
        for stream in range(streams):
            r.summary[number, b, stream : stream + 1, :] = last[stream][0]
            r.summary[number, b, streams + stream : streams + stream + 1, :] = last[stream][1]

    def forward(layer, pumps):
        gain_one, gain_two = r.gains[layer, 0:1, :], r.gains[layer, 1:2, :]

        def norm_one(at):
            values = r.resid[layer, at, :]
            scale = lax.rsqrt(jnp.mean(values * values, axis=-1, keepdims=True) + EPSILON)
            r.gated[layer, at, :] = (values * scale * gain_one).astype(BF16)

        each_tile(norm_one)
        near = r.gated.at[layer, own_part]
        give(near, r.gated.at[layer, far_part], r.gated_send.at[layer], r.gated_recv.at[layer])
        need(layer)

        def front(b):
            source = r.gated[layer, own_part, :]
            r.wide[:, 0:hid] = dot_nt(source, weights[layer, b, 0:hid, :]) + r.biases[layer, b, 0:1, :]
            r.wide[:, hid : 2 * hid] = dot_nt(source, weights[layer, b, hid : 2 * hid, :]) + r.biases[layer, b, 1:2, :]
            r.cand[layer, b] = dot_nt(source, weights[layer, b, 2 * hid : at_out, :])

            def group(k, carried):
                new = []
                for stream in range(streams):
                    at = pl.ds(pl.multiple_of(stream * span + k * 8, 8), 8)
                    f, i = sigmoid(r.wide[at, 0:hid]), sigmoid(r.wide[at, hid : 2 * hid])
                    share = 1.0 / (f + i)
                    decay = f * share * widen(r.mask[at, :], hid)
                    term = i * share * r.cand[layer, b, at, :]
                    r.fgate[layer, b, at, :] = f
                    r.igate[layer, b, at, :] = i
                    for step in (1, 2, 4):
                        reach = row8 >= step
                        term = term + decay * jnp.where(reach, pltpu.roll(term, step, 0), 0.0)
                        decay = decay * jnp.where(reach, pltpu.roll(decay, step, 0), 1.0)
                    prod_in, state_in = carried[stream]
                    term = term + decay * state_in
                    decay = decay * prod_in
                    r.states[layer, b, at, :] = term
                    r.prods[b, at, :] = decay
                    new.append((decay[7:8], term[7:8]))
                return tuple(new)

            put_summary(layer, b, in_eights(group))

        count(0, nb // 2, front)
        pumps[0]()
        count(nb // 2, nb, front)
        post, collect = mail(layer, True)
        post()
        pumps[1]()
        r.carry_in[layer] = collect()
        r.acc[...] = jnp.zeros_like(r.acc)

        def rear(k):
            f, b_own, b_far = blocks(k)

            def states_of(b, put):
                for stream in range(streams):
                    at = slice(stream * span, (stream + 1) * span)
                    full = r.states[layer, b, at, :] + r.prods[b, at, :] * r.carry_in[layer, b, stream : stream + 1, :]
                    r.states[layer, b, at, :] = full
                    put(at, full.astype(BF16))

            def put_far(at, low):
                r.states_out[f, at, :] = low

            def put_own(at, low):
                r.states_low[layer, f, at, :] = low

            states_of(b_far, put_far)
            give(
                r.states_out.at[f], r.states_low.at[layer, f, far_part], r.states_send.at[f],
                r.states_recv.at[layer, f],
            )
            states_of(b_own, put_own)
            r.acc[...] += dot_nn(r.states_out[f], weights[layer, b_far, at_out:at_up, :]) + dot_nn(
                r.states_low[layer, f, own_part, :], weights[layer, b_own, at_out:at_up, :]
            )

        count(0, nx, rear)
        pumps[2]()

        def norm_two(at):
            values = r.resid[layer, at, :] + r.acc[at, :]
            r.middle[layer, at, :] = values
            scale = lax.rsqrt(jnp.mean(values * values, axis=-1, keepdims=True) + EPSILON)
            r.normed[layer, at, :] = (values * scale * gain_two).astype(BF16)

        each_tile(norm_two)
        near = r.normed.at[layer, own_part]
        give(near, r.normed.at[layer, far_part], r.normed_send.at[layer], r.normed_recv.at[layer])
        r.acc[...] = r.middle[layer]


        def mlp(k):
            f, b_own, b_far = blocks(k)

            def active_of(b, put):
                r.wide[...] = dot_nt(r.normed[layer, own_part, :], weights[layer, b, at_up:at_down, :])

                def act(at):
                    v = r.wide[at, :]
                    square = v * v
                    t = jnp.tanh(GELU_A * (v + GELU_B * (v * square)))
                    share = 0.5 * (1.0 + t)
                    put(at, (v * share).astype(BF16))
                    r.slope[layer, b, at, :] = share + 0.5 * v * (1.0 - t * t) * (
                        GELU_A * (1.0 + 3.0 * GELU_B * square)
                    )

                each_tile(act)

            def put_far(at, low):
                r.active_out[f, at, :] = low

            def put_own(at, low):
                r.active[layer, f, at, :] = low

            active_of(b_far, put_far)
            give(r.active_out.at[f], r.active.at[layer, f, far_part], r.active_send.at[f], r.active_recv.at[layer, f])
            r.acc[...] += dot_nn(r.active_out[f], weights[layer, b_far, at_down:, :])
            active_of(b_own, put_own)
            r.acc[...] += dot_nn(r.active[layer, f, own_part, :], weights[layer, b_own, at_down:, :])

        count(0, nx - 1, mlp)
        pumps[3]()
        count(nx - 1, nx, mlp)
        pumps[4]()
        r.resid[layer + 1] = r.acc[...]
        gone(r.gated.at[layer, own_part], r.gated_send.at[layer])
        gone(r.normed.at[layer, own_part], r.normed_send.at[layer])
        for f in range(nx):
            gone(r.states_out.at[f], r.states_send.at[f])
            gone(r.active_out.at[f], r.active_send.at[f])

    def crossed(layer):
        return geo.swaps and layer >= CROSSED

    def axes(layer):
        return (gather.u, gather.v) if crossed(layer) else (y, x)

    def at_device(layer, z_at, u_at, v_at):
        y_at, x_at = geo.to_yx(u_at, v_at, core) if crossed(layer) else (u_at, v_at)
        return (geo.seq_of(z_at, y_at), 2 * x_at + core)

    def landing_at(layer, j, at):
        blk, first = j // n_seq, pl.multiple_of(j % n_seq * rows, rows)
        part = pl.ds(pl.multiple_of(first + at[0], at[1]), at[1])
        if layer == layers - 1:
            return r.landing, (blk, part)
        return weights, (layer + 1, 2 * blk + 1 - core, part)

    def landing(layer, j):
        ref, index = landing_at(layer, j, (0, rows))
        return ref.at[index]

    base_y = (nx - 1) * n_seq
    base_z = base_y + (ny - 1) * nz
    below = None

    def credit(sem, peers):
        for device in peers:
            pl.semaphore_signal(sem, inc=1, device_id=device, device_id_type=MESH)

    taken = set()

    def take_credit(name, sem, layer, amount):
        if layer < layers - 1 and (name, layer) not in taken:
            taken.add((name, layer))
            pl.semaphore_wait(sem, amount)

    def slot(layer, z_at, u_at, v_at):
        s, b = at_device(layer, z_at, u_at, v_at)
        return weights.at[layer, b, rows_at(s, rows)]

    z_groups = [[z_at for z_at in reversed(range(nz)) if z_at >= nz // 2], list(range(nz // 2))]
    order = [
        (z_at, du, dv)
        for group in z_groups
        for du in [*range(1, ny), 0]
        for z_at in group
        for dv in range(1, nx)
    ]
    per_layer, window = len(order), WINDOW

    def entry(idx):
        return order[idx]

    def leading(good):
        return next((n for n, one in enumerate(order) if not good(*one)), per_layer)

    def from_mlp(z_at):
        return all(geo.seq_of(z_at, y_at) * rows >= at_up for y_at in range(ny))

    started = (
        leading(lambda z_at, du, dv: du and from_mlp(z_at)),
        leading(lambda z_at, du, dv: from_mlp(z_at)),
        leading(lambda z_at, du, dv: du or from_mlp(z_at)),
        per_layer,
    )

    def copy_x(layer, idx):
        z_at, du, dv = entry(idx)
        u, v = axes(layer)
        u_at, v_at = other(u, du, ny), other(v, dv, nx)
        s = z_at * ny + u_at
        return remote(
            slot(layer, z_at, u_at, v_at), landing(layer, (dv - 1) * n_seq + s),
            r.sum_send_x.at[layer, dv - 1, z_at * ny + du], r.sum_recv_x.at[layer, dv - 1, s],
            at_device(layer, z, u, v_at),
        )

    def from_x(z_at, u_at):
        return [(dv - 1) * n_seq + z_at * ny + u_at for dv in range(1, nx)]

    def arrival_x(layer, idx):
        z_at, du, dv = entry(idx)
        if dv < nx - 1:
            return
        u, v = axes(layer)
        u_at = other(u, du, ny)
        s = z_at * ny + u_at
        for dv in range(1, nx):
            part = landing(layer, (dv - 1) * n_seq + s)
            remote(part, part, r.sum_send_x.at[layer, 0, 0], r.sum_recv_x.at[layer, dv - 1, s], sibling).wait_recv()
        if du:
            add_up(layer, z_at, u_at, from_x(z_at, u_at))
            remote(
                slot(layer, z_at, u_at, v), landing(layer, base_y + (du - 1) * nz + z_at),
                r.sum_send_y.at[layer, du - 1], r.sum_recv_y.at[layer, du - 1, z_at], at_device(layer, z, u_at, v),
            ).start()

    queue = [0, [], 0]

    def place(g):
        return layers - 1 - g // per_layer, g % per_layer

    def plan(g, layer, z_at):
        far = max(z_at, nz - 1 - z_at)
        at = g + DELAYS[0]
        for distance in range(far, 0, -1):
            queue[1].append((at, functools.partial(sum_z, layer, z_at, distance), False))
            at += DELAYS[1]
        queue[1].append((at, functools.partial(own_sum, layer, z_at), False))
        at += DELAYS[2]
        for distance in range(1, far + 1):
            queue[1].append((at, functools.partial(spread_block, layer, z_at, distance), layer == 0 and z_at < nz // 2))
            at += DELAYS[3]

    def start_x(until):
        for g in range(queue[2], min(until, layers * per_layer)):
            to, idx = place(g)
            if idx == 0:
                take_credit("x", r.credit_x, to, nx - 1)
                take_credit("y", r.credit_y, to, ny - 1)
            copy_x(to, idx).start()
            queue[2] = g + 1

    def x_steps(steps, layer=0, limit=per_layer + window):
        for _ in range(steps):
            g = queue[0]
            if g >= (layers - 1 - layer) * per_layer + limit:
                break
            if g >= window:
                copy_x(*place(g - window)).wait_send()
            start_x(g + 1)
            if g >= window:
                to, idx = place(g - window)
                arrival_x(to, idx)
                z_at, du, dv = order[idx]
                if not du and dv == nx - 1:
                    plan(g, to, z_at)
            queue[0] += 1
            run_events(g)

    def run_events(until, held=False):
        due = sorted((e for e in queue[1] if e[0] <= until and (held or not e[2])), key=lambda e: e[0])
        queue[1] = [e for e in queue[1] if not (e[0] <= until and (held or not e[2]))]
        for event in due:
            event[1]()

    def put_grad(layer, b, first, size, value):
        weights[layer, b, first : first + size, :] = value.astype(BF16)

    def backward(layer, pumps):
        gain_one, gain_two = r.gains[layer, 0:1, :], r.gains[layer, 1:2, :]

        def low_grad(at):
            r.gmlp[at, :] = r.dgrad[at, :].astype(BF16)

        each_tile(low_grad)
        take_credit("mlp", r.credit_mlp, layer, 1)
        give(r.gmlp.at[own_part], r.gmlp.at[far_part], r.gmlp_send.at[0], r.gmlp_recv.at[0])
        r.acc[...] = jnp.zeros_like(r.acc)

        def mlp(k):
            f, b_own, b_far = blocks(k)

            def inner_of(b, put):
                r.wide[...] = dot_nt(r.gmlp[own_part, :], weights[layer, b, at_down:, :])

                def act(at):
                    put(at, (r.wide[at, :] * r.slope[layer, b, at, :]).astype(BF16))

                each_tile(act)

            def put_far(at, low):
                r.ginner_out[f, at, :] = low

            def put_own(at, low):
                r.ginner[f, at, :] = low

            inner_of(b_far, put_far)
            give(r.ginner_out.at[f], r.ginner.at[f, far_part], r.ginner_send.at[f], r.ginner_recv.at[f])
            r.acc[...] += dot_nn(r.ginner_out[f], weights[layer, b_far, at_up:at_down, :])
            inner_of(b_own, put_own)
            r.acc[...] += dot_nn(r.ginner[f, own_part, :], weights[layer, b_own, at_up:at_down, :])

            @pl.when(k == 0)
            def _():
                given(r.gmlp.at[far_part], r.gmlp_recv.at[0])
                given(r.normed.at[layer, far_part], r.normed_recv.at[layer])

            given(r.active.at[layer, f, far_part], r.active_recv.at[layer, f])
            put_grad(layer, b_own, at_down, ffn, dot_tn(r.active[layer, f], r.gmlp[...]))
            given(r.ginner.at[f, far_part], r.ginner_recv.at[f])
            put_grad(layer, b_own, at_up, ffn, dot_tn(r.ginner[f], r.normed[layer]))

        count(0, nx - 1, mlp)
        pumps[0]()
        count(nx - 1, nx, mlp)
        gone(r.gmlp.at[own_part], r.gmlp_send.at[0])
        for f in range(nx):
            gone(r.ginner_out.at[f], r.ginner_send.at[f])
        if layer > 0:
            credit(r.credit_mlp, [sibling])
        pumps[1]()

        def norm_two(k, total):
            at = rows_at(k, tile)
            values, grad = r.middle[layer, at, :], r.acc[at, :]
            scale = lax.rsqrt(jnp.mean(values * values, axis=-1, keepdims=True) + EPSILON)
            unit = values * scale
            gunit = grad * gain_two
            full = r.dgrad[at, :] + scale * (gunit - unit * jnp.mean(gunit * unit, axis=-1, keepdims=True))
            r.dgrad[at, :] = full
            r.gy[at, :] = full.astype(BF16)
            return total + jnp.sum(grad * unit, axis=0, keepdims=True)

        row_sum = jnp.zeros((1, width), F32)
        r.ggains[layer, 1:2, :] = lax.fori_loop(0, tokens // tile, norm_two, row_sum)
        take_credit("gate", r.credit_gate, layer, 1)
        give(r.gy.at[own_part], r.gy.at[far_part], r.gy_send.at[0], r.gy_recv.at[0])
        number = layers + layer

        def front(k):
            f, b_own, b_far = blocks(k)

            def scan(b):
                r.gstates[b] = dot_nt(r.gy[own_part, :], weights[layer, b, at_out:at_up, :])

                def group(k, carried):
                    new = []
                    for stream in range(streams):
                        at = pl.ds(pl.multiple_of(stream * span + (groups - 1 - k) * 8, 8), 8)
                        f, i = r.fgate[layer, b, at, :], r.igate[layer, b, at, :]
                        decay = f * (1.0 / (f + i)) * widen(r.mask[at, :], hid)
                        term = decay * r.gstates[b, at, :]
                        for step in (1, 2, 4):
                            reach = row8 < 8 - step
                            term = term + decay * jnp.where(reach, pltpu.roll(term, 8 - step, 0), 0.0)
                            decay = decay * jnp.where(reach, pltpu.roll(decay, 8 - step, 0), 1.0)
                        prod_in, state_in = carried[stream]
                        term = term + decay * state_in
                        decay = decay * prod_in
                        r.deltas[b, at, :] = term
                        r.prods[b, at, :] = decay
                        new.append((decay[0:1], term[0:1]))
                    return tuple(new)

                put_summary(number, b, in_eights(group))

            scan(b_far)
            scan(b_own)

            @pl.when(k == 0)
            def _():
                given(r.gy.at[far_part], r.gy_recv.at[0])

            given(r.states_low.at[layer, f, far_part], r.states_recv.at[layer, f])
            put_grad(layer, b_own, at_out, hid, dot_tn(r.states_low[layer, f], r.gy[...]))

        count(0, nx, front)
        post, collect = mail(number, False)
        post()
        pumps[2]()
        r.incoming[...] = collect()
        r.acc[...] = jnp.zeros_like(r.acc)
        span_row = lax.broadcasted_iota(jnp.int32, (span, hid), 0)
        given(r.gated.at[layer, far_part], r.gated_recv.at[layer])

        def rear(k):
            f, b_own, b_far = blocks(k)

            def gates_of(b, put):
                sum_f, sum_i = jnp.zeros((1, hid), F32), jnp.zeros((1, hid), F32)
                for stream in range(streams):
                    at = slice(stream * span, (stream + 1) * span)
                    late = r.incoming[b, stream : stream + 1, :]
                    linked = r.deltas[b, at, :] + r.prods[b, at, :] * late
                    linked = jnp.where(span_row == span - 1, late, pltpu.roll(linked, span - 1, 0))
                    delta = r.gstates[b, at, :] + linked
                    early = r.carry_in[layer, b, stream : stream + 1, :]
                    before = jnp.where(span_row == 0, early, pltpu.roll(r.states[layer, b, at, :], 1, 0))
                    fg, ig = r.fgate[layer, b, at, :], r.igate[layer, b, at, :]
                    share = 1.0 / (fg + ig)
                    fshare, ishare = fg * share, ig * share
                    gap = delta * (before * widen(r.mask[at, :], hid) - r.cand[layer, b, at, :]) * fshare * ishare
                    gf = (gap * (1.0 - fg)).astype(BF16)
                    gi = (gap * (ig - 1.0)).astype(BF16)
                    put(at, (gf, gi, (delta * ishare).astype(BF16)))
                    sum_f = sum_f + jnp.sum(gf.astype(F32), axis=0, keepdims=True)
                    sum_i = sum_i + jnp.sum(gi.astype(F32), axis=0, keepdims=True)
                r.gbiases[layer, b, 0:1, :] = sum_f
                r.gbiases[layer, b, 1:2, :] = sum_i

            def put_far(at, lows):
                for member in range(3):
                    r.ggate_out[member, f, at, :] = lows[member]

            def put_own(at, lows):
                for member in range(3):
                    r.ggate[member, f, at, :] = lows[member]

            gates_of(b_far, put_far)
            for member in range(3):
                give(
                    r.ggate_out.at[member, f], r.ggate.at[member, f, far_part], r.ggate_send.at[member, f],
                    r.ggate_recv.at[member, f],
                )
            gates_of(b_own, put_own)
            total = r.acc[...]
            for member in range(3):
                at = slice(member * hid, (member + 1) * hid)
                total = total + dot_nn(r.ggate_out[member, f], weights[layer, b_far, at, :])
                total = total + dot_nn(r.ggate[member, f, own_part, :], weights[layer, b_own, at, :])
            r.acc[...] = total
            for member in range(3):
                given(r.ggate.at[member, f, far_part], r.ggate_recv.at[member, f])
                put_grad(layer, b_own, member * hid, hid, dot_tn(r.ggate[member, f], r.gated[layer]))

        count(0, nx - 1, rear)
        pumps[3]()
        count(nx - 1, nx, rear)
        gone(r.gy.at[own_part], r.gy_send.at[0])
        for f in range(nx):
            for member in range(3):
                gone(r.ggate_out.at[member, f], r.ggate_send.at[member, f])
        if layer > 0:
            credit(r.credit_gate, [sibling])
            credit(r.credit_x, [(seq, 2 * other(x, step, nx) + core) for step in range(1, nx)])
            credit(r.credit_y, [(geo.seq_of(z, other(y, step, ny)), batch) for step in range(1, ny)])
            for way, ends in ((1, z + 1 < nz), (-1, z >= 1)):

                @pl.when(ends)
                def _():
                    credit(r.credit_z, [(geo.seq_of(z + way, y), batch)])


        def norm_one(k, total):
            at = rows_at(k, tile)
            values, grad = r.resid[layer, at, :], r.acc[at, :]
            scale = lax.rsqrt(jnp.mean(values * values, axis=-1, keepdims=True) + EPSILON)
            unit = values * scale
            gunit = grad * gain_one
            full = r.dgrad[at, :] + scale * (gunit - unit * jnp.mean(gunit * unit, axis=-1, keepdims=True))
            r.dgrad[at, :] = full
            return total + jnp.sum(grad * unit, axis=0, keepdims=True)

        r.ggains[layer, 0:1, :] = lax.fori_loop(0, tokens // tile, norm_one, row_sum)
        if layer > 0:
            load_old(layer - 1).start()
        pumps[4]()

    def load_old(layer):
        return pltpu.make_async_copy(old_ref.at[layer, 0], r.resid.at[layer + 1, pl.ds(0, rows)], r.load.at[layer])

    part_rows = min(rows // PIECES, tile)
    piece_rows = rows // PIECES

    def total_of(layer, z_at, u_at, sources, first):
        s, b = at_device(layer, z_at, u_at, axes(layer)[1])
        total = weights[layer, b, pl.ds(pl.multiple_of(s * rows + first, part_rows), part_rows), :].astype(F32)
        for j in sources:
            if j is None:
                total = total + r.landing_below[layer, pl.ds(pl.multiple_of(first, part_rows), part_rows), :].astype(F32)
            else:
                ref, index = landing_at(layer, j, (first, part_rows))
                total = total + ref[(*index, slice(None))].astype(F32)
        return total

    def add_up(layer, z_at, u_at, sources, start=0, size=rows):
        s, b = at_device(layer, z_at, u_at, axes(layer)[1])

        def one(k):
            first = start + k * part_rows
            weights[layer, b, pl.ds(pl.multiple_of(s * rows + first, part_rows), part_rows), :] = total_of(
                layer, z_at, u_at, sources, first
            ).astype(BF16)

        count(0, size // part_rows, one)

    def from_y(z_at):
        return [base_y + (dy - 1) * nz + z_at for dy in range(1, ny)]

    def wait_y(layer, z_at):
        for dy in range(1, ny):
            part = landing(layer, base_y + (dy - 1) * nz + z_at)
            remote(
                part, part, r.sum_send_y.at[layer, dy - 1], r.sum_recv_y.at[layer, dy - 1, z_at], sibling
            ).wait_recv()

    def piece(ref, k):
        return ref.at[pl.ds(k * piece_rows, piece_rows)]

    def wait_z(layer, number, k):
        part = piece(r.landing_below.at[layer], k)
        remote(part, part, r.sum_send_z.at[layer, 0, k], r.sum_recv_z.at[layer, number, k], sibling).wait_recv()

    def sum_z(layer, z_at, distance):
        def step(z_here, way):
            if not 0 <= z_here < nz:
                return

            @pl.when(z == z_here)
            def _():
                u, v = axes(layer)
                sources = from_x(z_at, u) + from_y(z_at)
                wait_y(layer, z_at)
                inner = 0 <= z_here + way < nz
                if inner:
                    sources = sources + [base_z + z_at]
                to = z_here - way
                if way < 0 and to == z_at:
                    into, number = r.landing_below.at[layer], nz
                else:
                    into, number = landing(layer, base_z + z_at), z_at
                for k in range(PIECES):
                    if inner:
                        wait_z(layer, z_at, k)
                    add_up(layer, z_at, u, sources, k * piece_rows, piece_rows)
                    remote(
                        piece(slot(layer, z_at, u, v), k), piece(into, k), r.sum_send_z.at[layer, z_at, k],
                        r.sum_recv_z.at[layer, number, k], at_device(layer, to, u, v),
                    ).start()

        if ("z", layer) not in taken:
            both = lax.convert_element_type(z + 1 < nz, jnp.int32) + lax.convert_element_type(z >= 1, jnp.int32)
            take_credit("z", r.credit_z, layer, both)
        step(z_at + distance, 1)
        step(z_at - distance, -1)

    def block_slot(layer, z_at, y_at):
        return block_ref.at[layer, rows_at(geo.seq_of(z_at, y_at), rows)]

    def block_arrival(layer, z_at, y_at, k):
        return r.block_recv.at[layer, geo.seq_of(z_at, y_at), k]

    def along_z(layer, z_at, k, go):
        for way, passes, to in (
            (0, jnp.logical_and(z_at <= z, z + 1 < nz), z + 1),
            (1, jnp.logical_and(z_at >= z, z >= 1), z - 1),
        ):
            sem = r.block_send_z.at[layer, way, z_at, k]

            @pl.when(passes)
            def _():
                go(to, sem)

    def pass_block(layer, z_at, part, k):
        into, arrival = piece(block_slot(layer, z_at, y), k), block_arrival(layer, z_at, y, k)
        along_z(
            layer, z_at, k,
            lambda to, sem: remote(part, into, sem, arrival, (geo.seq_of(to, y), batch)).start(),
        )
        for step in range(1, ny):
            remote(
                part, into, r.block_send_y.at[layer, step - 1], arrival, (geo.seq_of(z, other(y, step, ny)), batch)
            ).start()

    def wait_block(layer, z_at, y_at, k):
        part = piece(block_slot(layer, z_at, y_at), k)
        remote(part, part, r.block_send_y.at[layer, 0], block_arrival(layer, z_at, y_at, k), sibling).wait_recv()

    def spread_block(layer, z_at, distance):
        far_away = jnp.logical_or(z == z_at + distance, z == z_at - distance)

        @pl.when(far_away)
        def _():
            for k in range(PIECES):
                wait_block(layer, z_at, y, k)
                pass_block(layer, z_at, piece(block_slot(layer, z_at, y), k), k)

    def own_sum(layer, z_at):
        @pl.when(z == z_at)
        def _():
            wait_y(layer, z_at)
            u = axes(layer)[0]
            sources = from_x(z_at, u) + from_y(z_at)
            if z_at < nz - 1:
                sources = sources + [base_z + z_at]
            if z_at > 0:
                sources = sources + [below]
            load_old(layer).wait()
            squares = jnp.zeros((1, width), F32)
            for k in range(PIECES):
                if z_at < nz - 1:
                    wait_z(layer, z_at, k)
                if z_at > 0:
                    wait_z(layer, nz, k)

                def one(n, squares):
                    first = k * piece_rows + n * part_rows
                    at = pl.ds(pl.multiple_of(first, part_rows), part_rows)
                    total = total_of(layer, z_at, u, sources, first)
                    r.middle[layer, at, :] = total
                    moment = MOMENTUM_DECAY * r.resid[layer + 1, at, :] + total
                    r.resid[layer + 1, at, :] = moment
                    r.low_moments[layer, at, :] = moment.astype(BF16)
                    return squares + jnp.sum(moment * moment, axis=0, keepdims=True)

                squares = lax.fori_loop(0, piece_rows // part_rows, one, squares)
                pass_block(layer, z_at, piece(r.low_moments.at[layer], k), k)
            r.square_own[layer] = jnp.broadcast_to(jnp.sum(squares, axis=1, keepdims=True), (8, 128))
            pltpu.make_async_copy(r.low_moments.at[layer], own_block(layer), r.block_own.at[layer]).start()
            pltpu.make_async_copy(
                r.middle.at[layer, pl.ds(0, rows)], shard_ref.at[layer], r.store.at[layer]
            ).start()

    def own_block(layer):
        return block_ref.at[layer, rows_at(seq, rows)]

    def finish_block(layer):
        for z_at in range(nz):
            for k in range(PIECES):
                count(1, ny, lambda step: wait_block(layer, z_at, other(y, step, ny), k))
        pltpu.make_async_copy(r.low_moments.at[layer], own_block(layer), r.block_own.at[layer]).wait()
        pltpu.make_async_copy(r.middle.at[layer, pl.ds(0, rows)], shard_ref.at[layer], r.store.at[layer]).wait()

    def vec_start():
        each_piece(write_piece)
        remote(r.vec_out.at[0], r.vec_s.at[0], r.vec_send_s.at[0], r.vec_recv_s.at[0], sibling).start()

    def vec_second():
        remote(r.vec_out.at[0], r.vec_s.at[0], r.vec_send_s.at[0], r.vec_recv_s.at[0], sibling).wait_recv()
        total = r.vec_out[0] + r.vec_s[0]
        r.vec_out[1] = total
        r.vec_x[x] = total
        for step in range(1, nx):
            x_at = other(x, step, nx)
            remote(
                r.vec_out.at[1], r.vec_x.at[x], r.vec_send_x.at[x_at], r.vec_recv_x.at[x], (seq, x_at * 2 + core)
            ).start()

    def vec_third():
        for step in range(1, nx):
            x_at = other(x, step, nx)
            remote(
                r.vec_out.at[1], r.vec_x.at[x_at], r.vec_send_x.at[x_at], r.vec_recv_x.at[x_at], sibling
            ).wait_recv()
        total = r.vec_x[0]
        for k in range(1, nx):
            total = total + r.vec_x[k]
        r.vec_out[2] = total
        r.vec_q[seq] = total

        def one(k):
            to = other(seq, k, n_seq)
            remote(r.vec_out.at[2], r.vec_q.at[seq], r.vec_send_q.at[to], r.vec_recv_q.at[seq], (to, batch)).start()

        count(1, n_seq, one)

    def vec_last():
        def one(k):
            source = other(seq, k, n_seq)
            remote(
                r.vec_out.at[2], r.vec_q.at[source], r.vec_send_q.at[source], r.vec_recv_q.at[source], sibling
            ).wait_recv()

        count(1, n_seq, one)
        total = lax.fori_loop(1, n_seq, lambda k, t: t + r.vec_q[k], r.vec_q[0])
        vgrad_ref[...] = total
        new_vmom_ref[...] = MOMENTUM_DECAY * vmom_ref[...] + total
        first = 0
        for member, length in enumerate((width, width, H, H)):
            at = slice(first, first + length)
            segment = new_vmom_ref[:, at]
            scale = lax.rsqrt(jnp.mean(segment * segment, axis=1, keepdims=True) + 1e-06)
            fresh = vec_ref[:, at] - SEGMENT_RATES[member] * segment * scale
            new_vec_ref[:, at] = fresh
            new_vavg_ref[:, at] = AVERAGE_DECAY * vavg_ref[:, at] + (1.0 - AVERAGE_DECAY) * fresh
            first += length

    hid_devices, ffn_devices = hid // rows, ffn // rows
    in_group = jnp.where(seq < 4 * hid_devices, hid_devices, ffn_devices)
    rank = lax.rem(seq, in_group)
    group_first = seq - rank
    lead = QUINTIC[0]

    def gram_pair(pair, into, squares_into, sends, recvs, device):
        return (
            remote(pair[0], into, sends.at[0], recvs.at[0], device),
            remote(pair[1], squares_into, sends.at[1], recvs.at[1], device),
        )

    def to_core(layer):
        return gram_pair(
            (r.gram_full.at[layer, 1 - core], r.square_own.at[layer]), r.gram_s.at[layer], r.square_s.at[layer],
            r.gram_send_s.at[layer], r.gram_recv_s.at[layer], sibling,
        )

    def to_x(layer):
        out = r.gram_out.at[layer, 0], r.square_out.at[layer, 0]
        return [
            copy
            for step in range(1, nx)
            for copy in gram_pair(
                out, r.gram_x.at[layer, step - 1], r.square_x.at[layer, step - 1],
                r.gram_send_x.at[layer, step - 1], r.gram_recv_x.at[layer, step - 1],
                (seq, other(x, step, nx) * 2 + core),
            )
        ]

    def to_group(layer, here_at, device):
        return gram_pair(
            (r.gram_out.at[layer, 1], r.square_out.at[layer, 1]), r.gram_g.at[layer, here_at],
            r.square_g.at[layer, here_at], r.gram_send_g.at[layer, here_at], r.gram_recv_g.at[layer, here_at], device,
        )

    def hand_over(layer):
        part = r.gram_sum.at[layer, core]
        return remote(part, part, r.gram_send_e.at[layer], r.gram_recv_e.at[layer], sibling)

    def gram_start(layer):
        value = dot_tn(r.low_moments[layer], r.low_moments[layer])
        quarter = half // 2
        for c in range(2):
            at = slice(c * quarter, (c + 1) * quarter)
            low = slice(half + c * quarter, half + (c + 1) * quarter)
            r.gram_full[layer, c, 0] = value[at, 0:half].astype(BF16)
            r.gram_full[layer, c, 1] = value[at, half:].astype(BF16)
            r.gram_full[layer, c, 2] = value[low, half:].astype(BF16)
        for copy in to_core(layer):
            copy.start()

    def gram_chip(layer):
        for copy in to_core(layer):
            copy.wait()
        r.gram_out[layer, 0] = (r.gram_full[layer, core].astype(F32) + r.gram_s[layer].astype(F32)).astype(BF16)
        r.square_out[layer, 0] = r.square_own[layer] + r.square_s[layer]
        for copy in to_x(layer):
            copy.start()

    def gram_line(layer):
        for copy in to_x(layer):
            copy.wait()
        total, square = r.gram_out[layer, 0].astype(F32), r.square_out[layer, 0]
        for k in range(nx - 1):
            total = total + r.gram_x[layer, k].astype(F32)
            square = square + r.square_x[layer, k]
        r.gram_out[layer, 1] = total.astype(BF16)
        r.square_out[layer, 1] = square

        def one(k):
            to = lax.rem(rank + k, in_group)
            here_at = lax.rem(rank - to - 1 + in_group, in_group)
            for copy in to_group(layer, here_at, (group_first + to, batch)):
                copy.start()

        count(1, in_group, one)

    def gram_group(layer):
        def one(k):
            for copy in to_group(layer, k - 1, sibling):
                copy.wait()

        count(1, in_group, one)
        r.gram_sum[layer, core] = r.gram_out[layer, 1].astype(F32)

        def add(k):
            r.gram_sum[layer, core] += r.gram_g[layer, k - 1].astype(F32)
            r.square_out[layer, 1] += r.square_g[layer, k - 1]

        count(1, in_group, add)
        hand_over(layer).start()

    def even():
        return jnp.concatenate([r.acc[...], r.resid[0]], axis=0)

    def polynomial():
        low = even().astype(BF16)
        return (QUINTIC[1] * even() + QUINTIC[2] * dot_nn(low, low)).astype(BF16)

    def precise(low, value):
        high = value.astype(BF16)
        rest = (value - high.astype(F32)).astype(BF16)
        return dot_nn(low, high) + dot_nn(low, rest)

    def gram_use(layer):
        hand_over(layer).wait()
        inverse = 1.0 / (jnp.sqrt(r.square_out[layer, 1]) + 1e-07)
        inverse = inverse[0:1, 0:1]
        scale = inverse * inverse

        def corner(n):
            return jnp.concatenate([r.gram_sum[layer, 0, n], r.gram_sum[layer, 1, n]], axis=0) * scale

        r.acc[:, 0:half] = corner(0)
        r.acc[:, half:] = corner(1)
        r.resid[0, :, 0:half] = r.acc[:, half:].T
        r.resid[0, :, half:] = corner(2)
        first = polynomial()
        begin = (r.resid[layer + 1, 0:rows, :] * inverse).astype(BF16)
        begin = (lead * begin.astype(F32) + dot_nn(begin, first)).astype(BF16)
        r.odd[...] = precise(first, even())
        value = lead * lead * even() + 2.0 * lead * r.odd[...] + precise(first, r.odd[...])
        r.acc[...] = value[0:half]
        r.resid[0] = value[half:]
        ortho_ref[layer] = (lead * begin.astype(F32) + dot_nn(begin, polynomial())).astype(BF16)

    def ahead(steps):
        return lambda: advance(steps)

    def nothing():
        pass

    for layer in range(layers):
        forward(layer, [ahead(1)] * 5)
    for layer in range(layers):
        gather.finish(layer)

    def turn(at):
        act_ref[at, :] = r.resid[layers, at, :].astype(BF16)
        r.dgrad[at, :] = out_grad_ref[at, :].astype(F32)

    each_tile(turn)
    load_old(layers - 1).start()

    def starts(layer):
        limits = (started[0], started[1], started[1], started[2], started[3])
        wanted = PUMPS[layer == layers - 1]
        return [
            functools.partial(x_steps, n * max(per_layer // 8, 1), layer, limit)
            for n, limit in zip(wanted, limits, strict=True)
        ]

    share = max(per_layer // 8, 1)
    for layer in reversed(range(layers)):
        backward(layer, starts(layer))
    start_x(queue[0] + LAST_AHEAD * share)
    out_dx = pltpu.make_async_copy(r.dgrad, dx_ref, r.store.at[layers])
    out_dx.start()
    vec_start()
    x_steps(layers * per_layer + window)
    vec_second()
    end = max(event[0] for event in queue[1] if not event[2])
    upper = list(range(layers - 1, 0, -1))
    for step, body in zip(NS_PLACES, (gram_start, gram_chip, gram_line, gram_group), strict=True):
        run_events(queue[0] - 1 + step)
        for layer in upper:
            body(layer)
    run_events(end)
    held = sorted({event[0] for event in queue[1]})

    def spread(share_done):
        if held:
            run_events(held[min(int(share_done * len(held)), len(held) - 1)], True)

    gram_start(0)
    vec_third()
    gram_chip(0)
    spread(0.3)
    for layer in upper:
        gram_use(layer)
    spread(0.6)
    gram_line(0)
    spread(1.0)
    gram_group(0)
    gram_use(0)
    vec_last()
    for layer in range(layers):
        finish_block(layer)
    out_dx.wait()

    def drain(part, sem):
        remote(part, part, sem, r.vec_recv_s.at[0], sibling).wait_send()

    for layer in range(layers):
        for dy in range(1, ny):
            drain(weights.at[layer, 0, pl.ds(0, nz * rows)], r.sum_send_y.at[layer, dy - 1])
            drain(weights.at[layer, 0, pl.ds(0, nz * rows)], r.block_send_y.at[layer, dy - 1])
        for k in range(PIECES):
            part = piece(r.low_moments.at[layer], k)
            for z_at in range(nz):
                along_z(layer, z_at, k, lambda to, sem: drain(part, sem))

                @pl.when(z != z_at)
                def _():
                    drain(part, r.sum_send_z.at[layer, z_at, k])

    drain(r.vec_out.at[0], r.vec_send_s.at[0])
    for step in range(1, nx):
        drain(r.vec_out.at[1], r.vec_send_x.at[other(x, step, nx)])
    count(1, n_seq, lambda k: drain(r.vec_out.at[2], r.vec_send_q.at[other(seq, k, n_seq)]))


def run_step(geo, stream_in, out_grad, doc_lengths, mats, mat_momenta, vectors, vec_momenta, vec_averages):
    layers, _, rows, width = mats.shape
    streams, span, _ = stream_in.shape
    sz = Sizes(geo, layers, streams, span, width, rows, doc_lengths.shape[1])
    names = make_scratch(geo, sz)
    vmem, anywhere = pl.BlockSpec(memory_space=pltpu.VMEM), pl.BlockSpec(memory_space=pl.ANY)
    smem = pl.BlockSpec(memory_space=pltpu.SMEM)
    vec = jax.ShapeDtypeStruct(vectors.shape, F32)
    return pl.pallas_call(
        functools.partial(step_kernel, geo, sz, names),
        out_shape=(
            jax.ShapeDtypeStruct((sz.tokens, width), BF16),
            jax.ShapeDtypeStruct((sz.tokens, width), F32),
            jax.ShapeDtypeStruct((layers, rows, width), F32),
            jax.ShapeDtypeStruct((layers, sz.block, width), BF16),
            jax.ShapeDtypeStruct((layers, rows, width), BF16),
            vec, vec, vec, vec,
        ),
        in_specs=[anywhere, anywhere, vmem, vmem, smem, vmem, vmem, vmem],
        out_specs=(vmem, anywhere, anywhere, anywhere, vmem, vmem, vmem, vmem, vmem),
        scratch_shapes=names.shapes,
        compiler_params=pltpu.CompilerParams(
            collective_id=0, has_side_effects=True, vmem_limit_bytes=66584576
        ),
        name="step",
    )(
        mats, mat_momenta, stream_in.reshape(sz.tokens, width), out_grad.reshape(sz.tokens, width), doc_lengths,
        vectors, vec_momenta, vec_averages,
    )


def closing_kernel(
    small_rows, act, dx, shard, block, ortho, mats, averages, vgrad, vmom, vec, vavg,
    act_out, dx_out, shard_out, block_out, mats_out, averages_out, vgrad_out, vmom_out, vec_out, vavg_out,
):
    act_out[...] = act[...]
    dx_out[...] = dx[...]
    shard_out[:, 0] = shard[...]
    block_out[:, 0] = block[...].astype(F32)
    rows, width = mats_out.shape[2] * pl.num_programs(0), mats_out.shape[3]
    small = lax.axis_index("seq") * rows < small_rows
    factor = jnp.where(small, 0.2 * math.sqrt(max(H, width)), 0.2 * math.sqrt(max(FF, width)))
    fresh = mats[:, 0] - MATRIX_RATE * (ortho[...].astype(F32) * factor)
    mats_out[:, 0] = fresh
    averages_out[:, 0] = AVERAGE_DECAY * averages[:, 0] + (1.0 - AVERAGE_DECAY) * fresh
    vgrad_out[...] = vgrad[...]
    vmom_out[...] = vmom[...]
    vec_out[...] = vec[...]
    vavg_out[...] = vavg[...]


def run_closing(geo, act, dx, shard, block, ortho, mats, averages, vecs):
    layers, _, rows, width = mats.shape
    tokens, block_rows = act.shape[0], block.shape[1]
    grid = max(min(2, rows // 16), 1)

    def flat(count):
        return pl.BlockSpec((count // grid, width), lambda k: (k, 0))

    def deep(count):
        return pl.BlockSpec((layers, count // grid, width), lambda k: (0, k, 0))

    def boxed(count):
        return pl.BlockSpec((layers, 1, count // grid, width), lambda k: (0, 0, k, 0))

    vec = pl.BlockSpec(vecs[0].shape, lambda k: (0, 0))
    vec_shape = jax.ShapeDtypeStruct(vecs[0].shape, F32)
    box = jax.ShapeDtypeStruct(mats.shape, F32)
    return pl.pallas_call(
        functools.partial(closing_kernel, 4 * (H // geo.n_batch)),
        grid=(grid,),
        out_shape=(
            jax.ShapeDtypeStruct(act.shape, BF16),
            jax.ShapeDtypeStruct(dx.shape, F32),
            box,
            jax.ShapeDtypeStruct((layers, 1, block_rows, width), F32),
            box,
            box,
            *[vec_shape] * 4,
        ),
        in_specs=[
            flat(tokens), flat(tokens), deep(rows), deep(block_rows), deep(rows), boxed(rows), boxed(rows), *[vec] * 4
        ],
        out_specs=(
            flat(tokens), flat(tokens), boxed(rows), boxed(block_rows), boxed(rows), boxed(rows), *[vec] * 4
        ),
        compiler_params=pltpu.CompilerParams(vmem_limit_bytes=60 * 2**20),
        name="closing",
    )(act, dx, shard, block, ortho, mats, averages, *vecs)


def per_device(
    geo, stream_in, out_grad, doc_lengths, mats, mat_momenta, mat_averages, vectors, vec_momenta, vec_averages
):
    act, dx, shard, block, ortho, *vecs = run_step(
        geo, stream_in, out_grad, doc_lengths, mats, mat_momenta, vectors, vec_momenta, vec_averages
    )
    act, dx, *rest = run_closing(geo, act, dx, shard, block, ortho, mats, mat_averages, vecs)
    return (act.reshape(stream_in.shape), dx.reshape(stream_in.shape), *rest)


def solution(mesh):
    geo = Geometry(mesh.shape["seq"], mesh.shape["batch"])
    rows = P(None, "batch", "seq", None)
    tokens = P("batch", "seq", None)
    return jax.shard_map(
        functools.partial(per_device, geo),
        mesh=mesh,
        in_specs=(tokens, tokens, P("batch", None), rows, rows, rows, P(), P(), P()),
        out_specs=(tokens, tokens, rows, P(None, "batch", None, None), rows, rows, P(), P(), P(), P()),
        check_vma=False,
    )
```
